128 devices in a mesh: group: 8 (over x_lo, z), member: 16 (over y, x_hi, core).
Axes of the slice: x: 4 (x_hi: 2, x_lo: 2; x = x_hi * 2 + x_lo), y: 4, z: 4, core: 2. Of those that a mesh axis runs over, the one named last changes fastest.
Arguments:
- entities: float32 [8, 4096, 400], P('group', 'member'), may hold values from -4 to 4
- ent_state: float32 [8, 4096], P('group', 'member'), may hold values from 0.05 to 0.5
- relations: float32 [4096, 400], replicated, may hold values from -6 to 6
- rel_state: float32 [4096], replicated, may hold values from 0.05 to 0.5
- lhs_rows: int32 [8, 65536], P('group', 'member'), may hold values from 0 to 255
- rhs_owner: int32 [8, 65536, 1], P('group', 'member'), may hold values from 0 to 15; in each aligned block of 4096 rows (0 to 4095, 4096 to 8191, ..., all dimensions but the last counted through in order) at most 320 rows name the same one
- rhs_off: int32 [8, 65536], P('group', 'member'), may hold values from 0 to 255
- neg_owner: int32 [8, 64000, 1], P('group', 'member'), may hold values from 0 to 15; in each aligned block of 4000 rows (0 to 3999, 4000 to 7999, ..., all dimensions but the last counted through in order) at most 312 rows name the same one
- neg_off: int32 [8, 64000], P('group', 'member'), may hold values from 0 to 255
- rel_ids: int32 [8, 65536], P('group', 'member'), may hold values from 0 to 4095
- counts: int32 [8, 16], P('group', 'member'), may hold values from 1024 to 4096, as said below
Outputs:
- new_entities: float32 [8, 4096, 400], P('group', 'member')
- new_ent_state: float32 [8, 4096], P('group', 'member')
- new_relations: float32 [4096, 400], replicated
- new_rel_state: float32 [4096], replicated
The draws below stay inside these ranges and needn't reach their ends.
Inputs may be any that keep to these rules, and one draw needn't show every extreme that they name: `rhs_owner`: among the 4096 slots of one device at most 320 name one block, and some block is named by exactly 320. `neg_owner`: among the 4000 negatives of one device at most 312 name one block, and some block is named by exactly 312. `counts`: some device is full in every draw.
All inputs are finite; a program needn't handle non-finite values.
Results may differ from the reference program's by a relative error of at most 0.0001.
Values sent between devices are 32-bit elements; how exact they have to be, the bound alone decides.
A program may use at most 256 MiB of HBM per device.

```python
import math
import jax
import jax.numpy as jnp
import numpy as np
from jax import lax

D = 400
REL = 4096
ENT_DEV = 256
E_DEV = 4096
SPAN = 512
NEG = 500
SPANS = 8
SLAB = 4096
CAP_E = 320
CAP_N = 312
N_GROUP = 8
N_MEMBER = 16


def draw_counts(key, part):
    key = jax.random.fold_in(key, 7)
    first, second = jax.random.split(key)
    values = jax.random.randint(first, (N_GROUP * N_MEMBER,), E_DEV // 4, E_DEV + 1)
    chosen = jax.random.randint(second, (), 0, N_GROUP * N_MEMBER)
    values = values.at[chosen].set(E_DEV)
    return values.reshape(N_GROUP, N_MEMBER).astype(jnp.int32)


def with_ends(drawn, stream_key, smallest, largest):
    longest = drawn.shape.index(max(drawn.shape))
    spots = []
    for shift in (0, 1):
        where = [jax.random.randint(jax.random.fold_in(stream_key, axis), (), 0, length) for axis, length in enumerate(drawn.shape)]
        where[longest] = (where[longest] + shift) % drawn.shape[longest]
        spots.append(tuple(where))
    return drawn.at[spots[0]].set(smallest).at[spots[1]].set(largest)


def levels(rng, extent, cuts, least, high):
    def one(axis_at, shards_of):
        steps = jax.random.uniform(jax.random.fold_in(jax.random.fold_in(rng, 6), axis_at), (shards_of,), jnp.float32, least / len(cuts), high / len(cuts))
        return jnp.repeat(jnp.exp(steps), extent[axis_at] // shards_of).reshape((-1,) + (1,) * (len(extent) - axis_at - 1))

    gain = one(*cuts[0])
    for cut in cuts[1:]:
        gain = gain * one(*cut)
    return gain


def rank_table(amount, lean):
    portions = [(1 << 20) // math.isqrt(grade ** lean) + 1 for grade in range(1, amount + 1)]
    scale = 1 + sum(portions) // (1 << 30)
    return np.cumsum(np.array([max(1, weight // scale) for weight in portions]))


def ranked_ids(stream_key, shape, count, skew):
    grid = rank_table(count, skew)
    ticket = jax.random.randint(jax.random.fold_in(stream_key, 1), shape, 0, int(grid[count - 1]))
    standing = jnp.searchsorted(jnp.asarray(grid, jnp.int32), ticket, side="right")
    return jax.random.permutation(jax.random.fold_in(stream_key, 2), count)[standing].astype(jnp.int32)


def assign_block(rng, own, number, rows, count, top, most, skew):
    ranking = jax.random.permutation(rng, count)
    heavy_load, common = shares(count, rows * top, most, skew, True), shares(count, rows * top, most, skew, False)
    places = jnp.arange(count)

    def named(sizes, rotation):
        used = int((sizes > 0).sum())
        fixed = max(1, used // 4)
        passed = fixed + (places - fixed + rotation * (used - fixed)) % max(1, count - fixed)
        return jnp.zeros((count,), jnp.int32).at[ranking[jnp.where(places < fixed, places, passed)]].set(jnp.asarray(sizes, jnp.int32))

    sizes = jnp.where(number % 4 == 0, named(heavy_load, number // 4), named(common, number - number // 4 - 1))
    mixed = jax.random.permutation(jax.random.fold_in(own, 3), count)
    giver, taker = mixed[0:count // 2 * 2:2], mixed[1:count // 2 * 2:2]
    room = jnp.minimum(sizes[giver] - 1, most - sizes[taker]) // 2
    room = jnp.where((giver == ranking[0]) | (taker == ranking[0]) | (sizes[taker] == 0), 0, jnp.maximum(room, 0))
    passed = jax.random.randint(jax.random.fold_in(own, 4), (count // 2,), 0, 1 << 20) % (room + 1)
    sizes = sizes.at[giver].add(-passed).at[taker].add(passed)
    members = jnp.searchsorted(jnp.cumsum(sizes), jnp.arange(rows * top), side="right").astype(jnp.int32)
    grid = members.reshape(top, rows).T
    grid = grid[jax.random.permutation(jax.random.fold_in(own, 1), rows)]
    rotation = jax.random.randint(jax.random.fold_in(own, 2), (rows, 1), 0, top)
    return jnp.take_along_axis(grid, (jnp.arange(top)[None, :] + rotation) % top, axis=1)


def shares(amount, total, limit, lean, full):
    weights = [(1 << 20) // math.isqrt(standing ** lean) + 1 for standing in range(1, amount + 1)]
    largest = limit if full else min(limit, max(-(-total // amount), total * weights[0] // sum(weights)))
    least = 1 if total - largest >= amount - 1 else 0
    holding, rest = [largest] + [least] * (amount - 1), total - largest - least * (amount - 1)
    while rest > 0:
        movable = [i for i in range(1, amount) if holding[i] < largest] or [i for i in range(1, amount) if holding[i] < limit]
        pool, remaining = sum([weights[i] for i in movable]), rest
        for i in movable:
            addition = min(limit - holding[i], max(1, remaining * weights[i] // pool), rest)
            holding[i] = holding[i] + addition
            rest = rest - addition
    return np.array(holding)


def gaussian(own_key, shape, deviation, bound, cuts=(), kind=jnp.bfloat16):
    array = jax.random.normal(own_key, shape, jnp.float32) * deviation
    if len(cuts) > 0:
        array = levels(own_key, shape, cuts, -0.22, 0.18) * array
    return jnp.clip(array, min=-bound, max=bound).astype(kind)


def setup_inputs(seed: int = 0) -> dict:
    key_list = jax.random.split(jax.random.key(seed), 12)
    entities = gaussian(key_list[0], (N_GROUP, SLAB, D), 0.3, 4.0, ((0, 8), (1, 16)), jnp.float32)
    ent_state = jnp.clip(jnp.exp(math.log(0.5) - 2.3025851 * jax.random.uniform(key_list[1], (N_GROUP, SLAB), jnp.float32) ** levels(key_list[1], (N_GROUP, SLAB), ((0, 8), (1, 16)), -0.2, 0.2)), 0.05, 0.5)
    relations = gaussian(key_list[2], (REL, D), 1.0, 6.0, (), jnp.float32)
    rel_state = jnp.clip(jnp.exp(jax.random.uniform(key_list[3], (REL,), jnp.float32, math.log(0.05), math.log(0.5))), 0.05, 0.5)
    lhs_rows = with_ends(jax.random.randint(key_list[4], (N_GROUP, N_MEMBER * E_DEV), 0, ENT_DEV), jax.random.fold_in(key_list[4], 1), 0, ENT_DEV - 1).astype(jnp.int32)
    rhs_owner_keys = jax.random.split(jax.random.fold_in(key_list[5], 1), N_GROUP * (N_MEMBER * E_DEV) // E_DEV)
    rhs_owner_turns = jax.random.permutation(jax.random.fold_in(key_list[5], 3), N_GROUP * (N_MEMBER * E_DEV) // E_DEV)
    rhs_owner = jax.vmap(lambda own, number: assign_block(jax.random.fold_in(key_list[5], 2), own, number, E_DEV, N_MEMBER, 1, CAP_E, 2))(rhs_owner_keys, rhs_owner_turns).reshape((N_GROUP, N_MEMBER * E_DEV, 1))
    rhs_off = with_ends(jax.random.randint(key_list[6], (N_GROUP, N_MEMBER * E_DEV), 0, ENT_DEV), jax.random.fold_in(key_list[6], 1), 0, ENT_DEV - 1).astype(jnp.int32)
    neg_owner_keys = jax.random.split(jax.random.fold_in(key_list[7], 1), N_GROUP * (N_MEMBER * SPANS * NEG) // (SPANS * NEG))
    neg_owner_turns = jax.random.permutation(jax.random.fold_in(key_list[7], 3), N_GROUP * (N_MEMBER * SPANS * NEG) // (SPANS * NEG))
    neg_owner = jax.vmap(lambda own, number: assign_block(jax.random.fold_in(key_list[7], 2), own, number, SPANS * NEG, N_MEMBER, 1, CAP_N, 1))(neg_owner_keys, neg_owner_turns).reshape((N_GROUP, N_MEMBER * SPANS * NEG, 1))
    neg_off = with_ends(jax.random.randint(key_list[8], (N_GROUP, N_MEMBER * SPANS * NEG), 0, ENT_DEV), jax.random.fold_in(key_list[8], 1), 0, ENT_DEV - 1).astype(jnp.int32)
    rel_ids = with_ends(ranked_ids(key_list[9], (N_GROUP, N_MEMBER * E_DEV), REL, 2), jax.random.fold_in(key_list[9], 3), 0, REL - 1).astype(jnp.int32)
    counts = draw_counts(jax.random.fold_in(key_list[11], 71), 0)
    return {"entities": entities, "ent_state": ent_state, "relations": relations, "rel_state": rel_state, "lhs_rows": lhs_rows, "rhs_owner": rhs_owner, "rhs_off": rhs_off, "neg_owner": neg_owner, "neg_off": neg_off, "rel_ids": rel_ids, "counts": counts}


STEP_SIZE = 0.1

def group_grads(left, right, lhs, rown, roff, nown, noff, rid, cnt, relations):
    total = lhs.shape[0]
    slot = jnp.arange(total, dtype=jnp.int32)
    member = slot // E_DEV
    lidx = (member * ENT_DEV + lhs).astype(jnp.int32)
    ridx = (rown * ENT_DEV + roff).astype(jnp.int32)
    nidx = (nown * ENT_DEV + noff).astype(jnp.int32)
    live = (slot % E_DEV < cnt[member]).astype(jnp.float32)
    left_vec = left[lidx]
    right_vec = right[ridx]
    rel_vec = relations[rid]
    query = left_vec * rel_vec
    pos = lax.optimization_barrier(jnp.sum(query * right_vec, axis=1))
    nchunk = total // SPAN
    query_c = query.reshape(nchunk, SPAN, D)
    neg_vec = right[nidx].reshape(nchunk, NEG, D)
    neg = jnp.einsum('cjd,cnd->cjn', query_c, neg_vec, precision=lax.Precision.HIGHEST)
    dpos = -jax.nn.sigmoid(-pos) * live
    dneg = jax.nn.sigmoid(neg) * live.reshape(nchunk, SPAN, 1) / NEG
    grad_query = dpos[:, None] * right_vec + jnp.einsum('cjn,cnd->cjd', dneg, neg_vec, precision=lax.Precision.HIGHEST).reshape(total, D)
    grad_right = dpos[:, None] * query
    grad_neg = jnp.einsum('cjn,cjd->cnd', dneg, query_c, precision=lax.Precision.HIGHEST).reshape(nchunk * NEG, D)
    left_grad = jnp.zeros((SLAB, D), jnp.float32).at[lidx].add(grad_query * rel_vec)
    right_grad = jnp.zeros((SLAB, D), jnp.float32).at[ridx].add(grad_right).at[nidx].add(grad_neg)
    rel_grad = jnp.zeros((REL, D), jnp.float32).at[rid].add(grad_query * left_vec)
    return (left_grad, right_grad, rel_grad)

def reference(entities, ent_state, relations, rel_state, lhs_rows, rhs_owner, rhs_off, neg_owner, neg_off, rel_ids, counts):
    left_list = []
    right_list = []
    rel_total = jnp.zeros((REL, D), jnp.float32)
    for part in range(N_GROUP):
        other = (part + 1) % N_GROUP
        left_grad, right_grad, rel_grad = group_grads(entities[part], entities[other], lhs_rows[part], rhs_owner[part, :, 0], rhs_off[part], neg_owner[part, :, 0], neg_off[part], rel_ids[part], counts[part], relations)
        left_list.append(left_grad)
        right_list.append(right_grad)
        rel_total = rel_total + rel_grad
    new_rows = []
    new_states = []
    for part in range(N_GROUP):
        grad = left_list[part] + right_list[(part - 1) % N_GROUP]
        state = ent_state[part] + lax.optimization_barrier(jnp.mean(grad * grad, axis=1))
        new_rows.append(entities[part] - STEP_SIZE * grad / jnp.sqrt(state)[:, None])
        new_states.append(state)
    rel_new_state = rel_state + lax.optimization_barrier(jnp.mean(rel_total * rel_total, axis=1))
    rel_new = relations - STEP_SIZE * rel_total / jnp.sqrt(rel_new_state)[:, None]
    return (jnp.stack(new_rows), jnp.stack(new_states), rel_new, rel_new_state)
```

```python
import functools
import jax
import jax.numpy as jnp
from jax import lax
from jax.experimental import pallas as pl
from jax.experimental.pallas import tpu as pltpu
from jax.sharding import PartitionSpec as P

SPAN = 512
NEG = 500
STEP_SIZE = 0.1
LANES = 128
F32 = jnp.float32
BF16 = jnp.bfloat16


def split(x):
    hi = x.astype(BF16)
    return hi, (x - hi.astype(F32)).astype(BF16)


def dot2(a, b, dims):
    return lax.dot_general(a, b, (dims, ((), ())), preferred_element_type=F32)


def dot3(a, b, dims):
    ah, al = a
    bh, bl = b
    return dot2(ah, bh, dims) + (dot2(ah, bl, dims) + dot2(al, bh, dims))


def row(i, chunks):
    return pl.ds(pl.multiple_of(i * chunks, chunks), chunks)


def read_rows(ref, rows, chunks):
    return jnp.concatenate([ref[pl.ds(c, rows, stride=chunks), :] for c in range(chunks)], axis=1)


def write_rows(ref, value, rows, chunks):
    for c in range(chunks):
        ref[pl.ds(c, rows, stride=chunks), :] = value[:, c * LANES : (c + 1) * LANES]


def bucket_kernel(
    spans, chunks, unroll,
    cnt_ref, ridx_ref, nidx_ref, rid_ref, lhs_ref, ent_ref, rel_ref, slab_hbm,
    right_hbm, relg_hbm, left_ref,
    slab, racc, nacc, relacc, rvec, nvec, gr, gn, grel, sem,
):
    s = pl.program_id(0)
    rows = racc.shape[0] // chunks

    @pl.when(s == 0)
    def _():
        load = pltpu.make_async_copy(slab_hbm, slab.at[pl.ds(0, rows * chunks)], sem.at[0])
        load.start()
        slab[pl.ds(rows * chunks, 8), :] = jnp.zeros((8, LANES), F32)
        racc[...] = jnp.zeros_like(racc)
        nacc[...] = jnp.zeros_like(nacc)
        relacc[...] = jnp.zeros_like(relacc)
        left_ref[...] = jnp.zeros_like(left_ref)
        gr[...] = jnp.zeros_like(gr)
        gn[...] = jnp.zeros_like(gn)
        grel[...] = jnp.zeros_like(grel)
        load.wait()

    def scatter(j, base):
        rel = row(rid_ref[base + j], chunks)
        rgt = row(ridx_ref[base + j], chunks)
        neg = row(nidx_ref[base + j], chunks)
        own = row(j, chunks)
        relacc[rel, :] = relacc[rel, :] + grel[own, :]
        racc[rgt, :] = racc[rgt, :] + gr[own, :]
        nacc[neg, :] = nacc[neg, :] + gn[own, :]

    def gather(j, base):
        own = row(j, chunks)
        rvec[own, :] = slab[row(ridx_ref[base + j], chunks), :]
        nvec[own, :] = slab[row(nidx_ref[base + j], chunks), :]

    behind = jnp.maximum(s - 1, 0) * SPAN
    ahead = jnp.minimum(s, spans - 1) * SPAN

    def step(b, carry):
        for u in range(unroll):
            j = b * unroll + u
            gather(j, ahead)
            scatter(j, behind)
        return carry

    lax.fori_loop(0, SPAN // unroll, step, 0)

    @pl.when(s < spans)
    def _():
        hot = (lax.broadcasted_iota(jnp.int32, (ent_ref.shape[0], SPAN), 0) == lhs_ref[0]).astype(F32).astype(BF16)
        eh, el = split(ent_ref[...])
        first = ((0,), (0,))
        last = ((1,), (1,))
        inner = ((1,), (0,))
        left = dot2(hot, eh, first) + dot2(hot, el, first)
        rel = rel_ref[...]
        query = left * rel
        live = (s * SPAN + lax.broadcasted_iota(jnp.int32, (SPAN, 1), 0) < cnt_ref[0]).astype(F32)
        q = split(query)
        n = split(read_rows(nvec, SPAN, chunks))
        neg = dot3(q, n, last)
        dneg = split(jax.nn.sigmoid(neg) * (live / NEG))
        right = read_rows(rvec, SPAN, chunks)
        pos = jnp.sum(query * right, axis=1, keepdims=True)
        dpos = -jax.nn.sigmoid(-pos) * live
        write_rows(gr, dpos * query, SPAN, chunks)
        write_rows(gn, dot3(dneg, q, first), SPAN, chunks)
        grad_query = dpos * right + dot3(dneg, n, inner)
        write_rows(grel, grad_query * left, SPAN, chunks)
        gl = split(grad_query * rel)
        left_ref[...] += dot2(hot, gl[0], inner) + dot2(hot, gl[1], inner)

    @pl.when(s == spans)
    def _():
        out_rel = pltpu.make_async_copy(relacc, relg_hbm, sem.at[0])
        out_rel.start()
        tile = 2048

        def add(i, carry):
            part = pl.ds(pl.multiple_of(i * tile, tile), tile)
            racc[part, :] = racc[part, :] + nacc[part, :]
            return carry

        lax.fori_loop(0, rows * chunks // tile, add, 0)
        out_right = pltpu.make_async_copy(racc, right_hbm, sem.at[1])
        out_right.start()
        out_rel.wait()
        out_right.wait()


def bucket(counts, ridx, nidx, rid, lhs, ent, rel_rows, slab):
    edges, width = rel_rows.shape
    chunks = width // LANES
    spans = edges // SPAN
    rows = slab.shape[0] // chunks
    smem = pl.BlockSpec(memory_space=pltpu.SMEM)
    anym = pl.BlockSpec(memory_space=pl.ANY)
    vm = lambda r: pltpu.VMEM((r * chunks, LANES), F32)
    return pl.pallas_call(
        functools.partial(bucket_kernel, spans, chunks, 8),
        grid=(spans + 1,),
        out_shape=(
            jax.ShapeDtypeStruct((rows * chunks, LANES), F32),
            jax.ShapeDtypeStruct((rows * chunks, LANES), F32),
            jax.ShapeDtypeStruct(ent.shape, F32),
        ),
        in_specs=[
            smem, smem, smem, smem,
            pl.BlockSpec((1, 1, SPAN), lambda s: (jnp.minimum(s, spans - 1), 0, 0)),
            pl.BlockSpec(ent.shape, lambda s: (0, 0)),
            pl.BlockSpec((SPAN, width), lambda s: (jnp.minimum(s, spans - 1), 0)),
            anym,
        ],
        out_specs=(anym, anym, pl.BlockSpec(ent.shape, lambda s: (0, 0))),
        scratch_shapes=[
            vm(rows + 2), vm(rows), vm(rows + 2), vm(rows),
            vm(SPAN), vm(SPAN), vm(SPAN), vm(SPAN), vm(SPAN),
            pltpu.SemaphoreType.DMA((2,)),
        ],
        compiler_params=pltpu.CompilerParams(vmem_limit_bytes=58 * 2**20),
        name="bucket",
    )(counts, ridx, nidx, rid, lhs, ent, rel_rows, slab)


def from_behind(array, axis, by):
    devices = lax.axis_size(axis)
    return lax.ppermute(array, axis, [(i, (i + by) % devices) for i in range(devices)])


def on_device(
    entities, ent_state, relations, rel_state, lhs_rows, rhs_owner, rhs_off, neg_owner, neg_off, rel_ids, counts
):
    shard = entities[0]
    rows, width = shard.shape
    wide = -(-width // LANES) * LANES
    chunks = wide // LANES
    members = lax.axis_size("member")
    padded = jnp.pad(shard, ((0, 0), (0, wide - width)))
    right = from_behind(padded.reshape(rows * chunks, LANES), "group", -1)
    slab = lax.all_gather(right, "member", axis=0, tiled=True)
    edges = lhs_rows.shape[1]
    spans = edges // SPAN
    ridx = rhs_owner[0, :, 0] * rows + rhs_off[0]
    nidx = (neg_owner[0, :, 0] * rows + neg_off[0]).reshape(spans, NEG)
    nidx = jnp.pad(nidx, ((0, 0), (0, SPAN - NEG)), constant_values=rows * members).reshape(edges)
    rid = rel_ids[0]
    rel_rows = jnp.pad(relations, ((0, 0), (0, wide - width)))[rid]
    right_part, rel_part, left_grad = bucket(
        counts[0], ridx, nidx, rid, lhs_rows.reshape(spans, 1, SPAN), padded, rel_rows, slab
    )
    right_grad = lax.psum_scatter(right_part, "member", scatter_dimension=0, tiled=True)
    returned = from_behind(right_grad, "group", 1).reshape(rows, wide)
    grad_total = (left_grad + returned)[:, :width]
    new_state = ent_state[0] + jnp.mean(grad_total * grad_total, axis=1)
    new_shard = shard - STEP_SIZE * grad_total / jnp.sqrt(new_state)[:, None]
    rel_total = lax.psum(rel_part, ("group", "member")).reshape(-1, wide)[:, :width]
    rel_new_state = rel_state + jnp.mean(rel_total * rel_total, axis=1)
    rel_new = relations - STEP_SIZE * rel_total / jnp.sqrt(rel_new_state)[:, None]
    return (new_shard[None], new_state[None], rel_new, rel_new_state)


def solution(mesh):
    in_specs = (
        P("group", "member", None), P("group", "member"), P(), P(),
        P("group", "member"), P("group", "member", None), P("group", "member"),
        P("group", "member", None), P("group", "member"), P("group", "member"), P("group", "member"),
    )
    out_specs = (P("group", "member", None), P("group", "member"), P(), P())
    return jax.shard_map(on_device, mesh=mesh, in_specs=in_specs, out_specs=out_specs, check_vma=False)
```

```python
import functools
import jax
import jax.numpy as jnp
from jax import lax
from jax.experimental import pallas as pl
from jax.experimental.pallas import tpu as pltpu
from jax.sharding import PartitionSpec as P

SPAN = 512
NEG = 500
STEP_SIZE = 0.1
LANES = 128
F32 = jnp.float32
BF16 = jnp.bfloat16
MESH = pl.DeviceIdType.MESH

CHUNKS = 4
TAIL = 16
GROUP = 32
PACK = 104
PARTS = 4
PART = 208
BLOCKS = 16
RING = 4
PART_ORDER = (("y", "xhi"), ("xhi", "y"), ("y", "xhi"), ("xhi", "y"))
PIECE_ROWS = (32, 32, 40)
PIECE_SUM = (("z", "y", "x"), ("x", "z", "y"), ("z", "x", "y"))
PIECE_OUT = (("z", "y", "x"), ("x", "z", "y"), ("y", "z", "x"))
SHARDS = 64


def split(x):
    hi = x.astype(BF16)
    return hi, (x - hi.astype(F32)).astype(BF16)


def dot2(a, b, dims):
    return lax.dot_general(a, b, (dims, ((), ())), preferred_element_type=F32)


def dot3(a, b, dims):
    ah, al = a
    bh, bl = b
    return dot2(ah, bh, dims) + (dot2(ah, bl, dims) + dot2(al, bh, dims))


def row(i):
    return pl.ds(pl.multiple_of(i * CHUNKS, CHUNKS), CHUNKS)


def span_of(start, size, tile=8):
    return pl.ds(start if isinstance(start, int) else pl.multiple_of(start, tile), size)


def read_rows(ref, rows):
    return jnp.concatenate([ref[pl.ds(c, rows, stride=CHUNKS), :] for c in range(CHUNKS)], axis=1)


def write_rows(ref, value, rows):
    for c in range(CHUNKS):
        ref[pl.ds(c, rows, stride=CHUNKS), :] = value[:, c * LANES : (c + 1) * LANES]


def pack_tail(tail):
    packed = tail[0:8]
    for g in range(1, GROUP // 8):
        packed = packed + pltpu.roll(tail[8 * g : 8 * g + 8], TAIL * g, 1)
    return packed


def unpack_tail(packed):
    kept = lax.broadcasted_iota(jnp.int32, (8, LANES), 1) < TAIL
    parts = [jnp.where(kept, packed if g == 0 else pltpu.roll(packed, LANES - TAIL * g, 1), 0.0) for g in range(GROUP // 8)]
    return jnp.concatenate(parts, axis=0)


def digits_of(flat, order):
    sizes = {"y": 4, "xhi": 2, "x": 4, "z": 4}
    out = {}
    for name in reversed(order):
        out[name] = flat % sizes[name]
        flat = flat // sizes[name]
    return out


def index_of(where, order):
    sizes = {"y": 4, "xhi": 2, "x": 4, "z": 4}
    at = 0
    for name in order:
        at = at * sizes[name] + where[name]
    return at


def part_row(member, part):
    where = digits_of(member // 2, ("y", "xhi"))
    at = (member % 2) * 8 + index_of(where, PART_ORDER[part])
    return part * BLOCKS * PART + at * PART


def shard_row(group, piece, orders):
    where = digits_of(group % SHARDS, ("z", "y", "x"))
    return ((group // SHARDS) * SHARDS + index_of(where, orders[piece])) * PIECE_ROWS[piece]


def here():
    g = lax.axis_index("group")
    m = lax.axis_index("member")
    return {"x": (m // 2) % 2 * 2 + g // 4, "xhi": (m // 2) % 2, "y": m // 4, "z": g % 4, "core": m % 2}


def device(at):
    return (at["x"] % 2 * 4 + at["z"], at["y"] * 4 + at["x"] // 2 * 2 + at["core"])


def toward(at, axis, step):
    there = dict(at)
    if axis == "core":
        there["core"] = 1 - at["core"]
    elif axis == "xhi":
        there["x"] = (at["x"] + 2) % 4
    else:
        there[axis] = (at[axis] + step + 4) % 4
    return device(there)


def next_group(step):
    return ((lax.axis_index("group") + step + 8) % 8, lax.axis_index("member"))


def greet(devices):
    barrier = pltpu.get_barrier_semaphore()
    for there in devices:
        pl.semaphore_signal(barrier, inc=1, device_id=there, device_id_type=MESH)
    pl.semaphore_wait(barrier, len(devices))


class Copies:
    def __init__(self, send, recv, local):
        self.send, self.recv, self.local = send, recv, local
        self.started, self.kept, self.homes = 0, [], 0

    def to(self, there, src, dst):
        copy = pltpu.make_async_remote_copy(
            src_ref=src, dst_ref=dst, send_sem=self.send.at[self.started], recv_sem=self.recv.at[self.started],
            device_id=there, device_id_type=MESH,
        )
        copy.start()
        self.started += 1
        self.kept.append(copy)
        return copy

    def home(self, src, dst):
        copy = pltpu.make_async_copy(src, dst, self.local.at[self.homes])
        copy.start()
        self.homes += 1
        return copy

    def finish(self):
        for copy in self.kept:
            copy.wait_send()


def merged(flows):
    flows = list(flows)
    while flows:
        left = []
        for flow in flows:
            try:
                next(flow)
            except StopIteration:
                continue
            left.append(flow)
            yield
        flows = left


def run_beside(flows, beside):
    for _ in merged(flows):
        next(beside, None)
    for _ in beside:
        pass


def halves(size):
    first = -(-size // 16) * 8
    return first, size - first


def add_into(dst, at, src, start, size):
    tile = size
    while tile > 256:
        tile = tile // 2 if tile % 16 == 0 else tile // 13
    if tile == size:
        dst[span_of(at, size), :] = dst[span_of(at, size), :] + src[span_of(start, size), :]
        return

    def step(i, carry):
        d = span_of(at + i * tile, tile)
        dst[d, :] = dst[d, :] + src[span_of(start + i * tile, tile), :]
        return carry

    lax.fori_loop(0, size // tile, step, 0)


def sum_flow(net, at, src, acc, landing, ring, order, done):
    half = acc.shape[0]
    core = at["core"]
    over = net.to(toward(at, "core", 1), src.at[span_of((1 - core) * half, half)], landing)
    own = net.home(src.at[span_of(core * half, half)], acc)
    yield
    own.wait()
    over.wait_recv()
    add_into(acc, 0, landing, 0, half)
    base, size, used = 0, half, 0
    for axis in order:
        a = at[axis]
        if axis == "xhi":
            size = size // 2
            copy = net.to(toward(at, axis, 1), acc.at[span_of(base + (1 - a) * size, size)], ring.at[pl.ds(used, size)])
            yield
            copy.wait_recv()
            add_into(acc, base + a * size, ring, used, size)
            used += size
        else:
            size = size // RING
            h1, h2 = halves(size)
            up, down, far = (base + (a + k) % RING * size for k in (1, 3, 2))
            above, below = toward(at, axis, 1), toward(at, axis, -1)
            ra, rb, rc, rd = used, used + h1, used + size, used + 2 * size
            first = net.to(above, acc.at[span_of(far, h1)], ring.at[pl.ds(ra, h1)])
            second = net.to(below, acc.at[span_of(far + h1, h2)], ring.at[pl.ds(rb, h2)])
            c2 = net.to(above, acc.at[span_of(up + h1, h2)], ring.at[pl.ds(rc + h1, h2)])
            d1 = net.to(below, acc.at[span_of(down, h1)], ring.at[pl.ds(rd, h1)])
            yield
            first.wait_recv()
            add_into(acc, up, ring, ra, h1)
            c1 = net.to(above, acc.at[span_of(up, h1)], ring.at[pl.ds(rc, h1)])
            second.wait_recv()
            add_into(acc, down + h1, ring, rb, h2)
            d2 = net.to(below, acc.at[span_of(down + h1, h2)], ring.at[pl.ds(rd + h1, h2)])
            yield
            own = base + a * size
            c2.wait_recv()
            d1.wait_recv()
            c1.wait_recv()
            d2.wait_recv()
            add_into(acc, own, ring, rc, size)
            add_into(acc, own, ring, rd, size)
            used += 3 * size
        base = base + a * size
    yield from done(base)


def spread_flow(net, at, buf, offset, rows, order, arrived):
    radix = {"xhi": 2, "x": 4, "y": 4, "z": 4}
    total = rows
    for name in order:
        total *= radix[name]
    core = at["core"]
    bases = [offset + core * total]
    strides = []
    size = total
    for name in order:
        size = size // radix[name]
        strides.append(size)
        bases.append(bases[-1] + at[name] * size)
    sibling = toward(at, "core", 1)
    shared = []

    def share(start, size):
        there = span_of(start, size)
        shared.append((net.to(sibling, buf.at[there], buf.at[there]), start + (1 - 2 * core) * total, size))
        arrived(start, size)

    for level in reversed(range(len(order))):
        name, size, region = order[level], strides[level], bases[level]
        a = at[name]
        last = level == 0
        own = span_of(region + a * size, size)
        if name == "xhi":
            copy = net.to(toward(at, name, 1), buf.at[own], buf.at[own])
            if last:
                share(region + a * size, size)
            yield
            copy.wait_recv()
            if last:
                share(region + (1 - a) * size, size)
        else:
            h1, h2 = halves(size)
            up, down, far = (region + (a + k) % RING * size for k in (1, 3, 2))
            above, below = toward(at, name, 1), toward(at, name, -1)
            e = net.to(above, buf.at[own], buf.at[own])
            f = net.to(below, buf.at[own], buf.at[own])
            if last:
                share(region + a * size, size)
            yield
            e.wait_recv()
            lower = span_of(down, h1)
            g = net.to(above, buf.at[lower], buf.at[lower])
            f.wait_recv()
            upper = span_of(up + h1, h2)
            h = net.to(below, buf.at[upper], buf.at[upper])
            if last:
                share(down, size)
                share(up, size)
            yield
            g.wait_recv()
            h.wait_recv()
            if last:
                share(far, size)
    yield
    for copy, start, size in shared:
        copy.wait_recv()
        arrived(start, size)


def fetch_kernel(rid_ref, ent_ref, rel_hbm, slab_hbm, rows_hbm, own, packed, slab, rel, rel_rows, got, send, recv, local):
    at = here()
    m = lax.axis_index("member")
    greet(
        [toward(at, "y", 1), toward(at, "y", -1), toward(at, "xhi", 1), toward(at, "core", 1), next_group(1), next_group(-1)]
    )
    net = Copies(send, recv, local)
    entry = net.home(rel_hbm, rel)
    for j in range(8):
        rows = slice(j * GROUP, (j + 1) * GROUP)
        for c in range(3):
            own[pl.ds(j * PACK + c * GROUP, GROUP), :] = ent_ref[rows, c * LANES : (c + 1) * LANES]
        own[pl.ds(j * PACK + 96, 8), :] = pack_tail(ent_ref[rows, 3 * LANES : 4 * LANES])

    writes = []

    def flow(part):
        start = part * BLOCKS * PART
        mine = span_of(part_row(m, part), PART)
        shift = net.to(next_group(-1), own.at[pl.ds(part * PART, PART)], packed.at[mine])
        yield
        shift.wait_recv()

        def arrived(begin, size):
            def block(i, carry):
                source = begin + i * PART
                flat = (source - start) // PART
                where = digits_of(flat % 8, PART_ORDER[part])
                member = (where["y"] * 2 + where["xhi"]) * 2 + flat // 8
                for half in range(2):
                    base = source + half * PACK
                    out = (member * 256 + part * 64 + half * GROUP) * CHUNKS
                    out = pl.multiple_of(out, 128)
                    for c in range(3):
                        slab[pl.ds(out + c, GROUP, stride=CHUNKS), :] = packed[span_of(base + c * GROUP, GROUP), :]
                    slab[pl.ds(out + 3, GROUP, stride=CHUNKS), :] = unpack_tail(packed[span_of(base + 96, 8), :])
                return carry

            lax.fori_loop(0, size // PART, block, 0)

        yield from spread_flow(net, at, packed, start, PART, PART_ORDER[part], arrived)

    def gather():
        tile = 256
        width, total = rel.shape
        entry.wait()
        for t in range(total // (4 * tile)):
            def convert(i, carry):
                k = t * 4 + i
                part = span_of(k * tile, tile, tile)
                wide = jnp.concatenate([rel[:, part], jnp.zeros((CHUNKS * LANES - width, tile), F32)], axis=0)
                rel_rows[part] = wide.T.reshape(tile, CHUNKS, LANES)
                return carry

            lax.fori_loop(0, 4, convert, 0)
            yield
        edges = got.shape[0] // CHUNKS
        segment, unroll = 512, 16
        for t in range(edges // segment):
            def step(b, carry):
                for u in range(unroll):
                    j = t * segment + b * unroll + u
                    got[row(j), :] = rel_rows[rid_ref[j]]
                return carry

            lax.fori_loop(0, segment // unroll, step, 0)
            part = pl.ds(t * segment * CHUNKS, segment * CHUNKS)
            writes.append(net.home(got.at[part], rows_hbm.at[part]))
            yield

    run_beside([flow(part) for part in range(PARTS)], gather())
    writes.append(net.home(slab, slab_hbm))
    for write in writes:
        write.wait()
    net.finish()


def fetch(rid, ent, relations):
    edges = rid.shape[0]
    width, count = relations.shape
    rows = ent.shape[0] * BLOCKS
    anym = pl.BlockSpec(memory_space=pl.ANY)
    return pl.pallas_call(
        fetch_kernel,
        out_shape=(
            jax.ShapeDtypeStruct((rows * CHUNKS, LANES), F32),
            jax.ShapeDtypeStruct((edges * CHUNKS, LANES), F32),
        ),
        in_specs=[pl.BlockSpec(memory_space=pltpu.SMEM), pl.BlockSpec(memory_space=pltpu.VMEM), anym],
        out_specs=(anym, anym),
        scratch_shapes=[
            pltpu.VMEM((PARTS * PART, LANES), F32),
            pltpu.VMEM((PARTS * BLOCKS * PART, LANES), F32),
            pltpu.VMEM((rows * CHUNKS, LANES), F32),
            pltpu.VMEM((width, count), F32),
            pltpu.VMEM((count, CHUNKS, LANES), F32),
            pltpu.VMEM((edges * CHUNKS, LANES), F32),
            pltpu.SemaphoreType.DMA((96,)),
            pltpu.SemaphoreType.DMA((96,)),
            pltpu.SemaphoreType.DMA((16,)),
        ],
        compiler_params=pltpu.CompilerParams(vmem_limit_bytes=56 * 2**20, collective_id=1, has_side_effects=True),
        name="fetch",
    )(rid, ent, relations)


def bucket_kernel(
    spans, unroll,
    cnt_ref, ridx_ref, nidx_ref, rid_ref, lhs_ref, ent_ref, rel_ref, slab_hbm,
    right_hbm, rel0_hbm, rel1_hbm, rel2_hbm, left_ref,
    slab, racc, nacc, relacc, rvec, nvec, gr, gn, grel, sem,
):
    s = pl.program_id(0)
    total = racc.shape[0]

    @pl.when(s == 0)
    def _():
        load = pltpu.make_async_copy(slab_hbm, slab.at[pl.ds(0, total)], sem.at[0])
        load.start()
        slab[pl.ds(total, 8), :] = jnp.zeros((8, LANES), F32)
        racc[...] = jnp.zeros_like(racc)
        nacc[...] = jnp.zeros_like(nacc)
        relacc[...] = jnp.zeros_like(relacc)
        left_ref[...] = jnp.zeros_like(left_ref)
        gr[...] = jnp.zeros_like(gr)
        gn[...] = jnp.zeros_like(gn)
        grel[...] = jnp.zeros_like(grel)
        load.wait()

    def scatter(j, base):
        rel = row(rid_ref[base + j])
        rgt = row(ridx_ref[base + j])
        neg = row(nidx_ref[base + j])
        own = row(j)
        relacc[rel, :] = relacc[rel, :] + grel[own, :]
        racc[rgt, :] = racc[rgt, :] + gr[own, :]
        nacc[neg, :] = nacc[neg, :] + gn[own, :]

    def gather(j, base):
        own = row(j)
        rvec[own, :] = slab[row(ridx_ref[base + j]), :]
        nvec[own, :] = slab[row(nidx_ref[base + j]), :]

    behind = jnp.maximum(s - 1, 0) * SPAN
    ahead = jnp.minimum(s, spans - 1) * SPAN

    def step(b, carry):
        for u in range(unroll):
            j = b * unroll + u
            gather(j, ahead)
            scatter(j, behind)
        return carry

    lax.fori_loop(0, SPAN // unroll, step, 0)

    @pl.when(s < spans)
    def _():
        hot = (lax.broadcasted_iota(jnp.int32, (ent_ref.shape[0], SPAN), 0) == lhs_ref[0]).astype(F32).astype(BF16)
        eh, el = split(ent_ref[...])
        first = ((0,), (0,))
        last = ((1,), (1,))
        inner = ((1,), (0,))
        left = dot2(hot, eh, first) + dot2(hot, el, first)
        rel = read_rows(rel_ref, SPAN)
        query = left * rel
        live = (s * SPAN + lax.broadcasted_iota(jnp.int32, (SPAN, 1), 0) < cnt_ref[0]).astype(F32)
        q = split(query)
        n = split(read_rows(nvec, SPAN))
        neg = dot3(q, n, last)
        dneg = split(jax.nn.sigmoid(neg) * (live / NEG))
        right = read_rows(rvec, SPAN)
        pos = jnp.sum(query * right, axis=1, keepdims=True)
        dpos = -jax.nn.sigmoid(-pos) * live
        write_rows(gr, dpos * query, SPAN)
        write_rows(gn, dot3(dneg, q, first), SPAN)
        grad_query = dpos * right + dot3(dneg, n, inner)
        write_rows(grel, grad_query * left, SPAN)
        gl = split(grad_query * rel)
        left_ref[...] += dot2(hot, gl[0], inner) + dot2(hot, gl[1], inner)

    @pl.when(s == spans)
    def _():
        def right_member(m, carry):
            for part in range(PARTS):
                for half in range(2):
                    src = pl.multiple_of((m * 256 + part * 64 + half * GROUP) * CHUNKS, 128)
                    out = part_row(m, part) + half * PACK
                    planes = [
                        racc[pl.ds(src + c, GROUP, stride=CHUNKS), :] + nacc[pl.ds(src + c, GROUP, stride=CHUNKS), :]
                        for c in range(CHUNKS)
                    ]
                    for c in range(3):
                        slab[span_of(out + c * GROUP, GROUP), :] = planes[c]
                    slab[span_of(out + 96, 8), :] = pack_tail(planes[3])
            return carry

        lax.fori_loop(0, BLOCKS, right_member, 0)
        out = pltpu.make_async_copy(slab.at[pl.ds(0, right_hbm.shape[0])], right_hbm, sem.at[0])
        out.start()
        begins = (0, 2 * SHARDS * PIECE_ROWS[0], 2 * SHARDS * (PIECE_ROWS[0] + PIECE_ROWS[1]))

        def shards(i, carry):
            for k in range(4):
                group = i * 4 + k
                src = pl.multiple_of(group * GROUP * CHUNKS, 128)
                at = [b + shard_row(group, p, PIECE_SUM) for p, b in enumerate(begins)]
                for c in range(3):
                    nacc[span_of(at[c], GROUP), :] = relacc[pl.ds(src + c, GROUP, stride=CHUNKS), :]
                nacc[span_of(at[2] + GROUP, 8), :] = pack_tail(relacc[pl.ds(src + 3, GROUP, stride=CHUNKS), :])
            return carry

        lax.fori_loop(0, 2 * SHARDS // 4, shards, 0)
        copies = [
            pltpu.make_async_copy(nacc.at[pl.ds(b, ref.shape[0])], ref, sem.at[1 + p])
            for p, (b, ref) in enumerate(zip(begins, (rel0_hbm, rel1_hbm, rel2_hbm)))
        ]
        for copy in copies:
            copy.start()
        for copy in copies:
            copy.wait()
        out.wait()


def bucket(counts, ridx, nidx, rid, lhs, ent, rel_rows, slab):
    edges = rid.shape[0]
    spans = edges // SPAN
    total = slab.shape[0]
    smem = pl.BlockSpec(memory_space=pltpu.SMEM)
    anym = pl.BlockSpec(memory_space=pl.ANY)
    vm = lambda r: pltpu.VMEM((r, LANES), F32)
    span_rows = SPAN * CHUNKS
    return pl.pallas_call(
        functools.partial(bucket_kernel, spans, 8),
        grid=(spans + 1,),
        out_shape=(
            jax.ShapeDtypeStruct((PARTS * BLOCKS * PART, LANES), F32),
            *(jax.ShapeDtypeStruct((2 * SHARDS * r, LANES), F32) for r in PIECE_ROWS),
            jax.ShapeDtypeStruct(ent.shape, F32),
        ),
        in_specs=[
            smem, smem, smem, smem,
            pl.BlockSpec((1, 1, SPAN), lambda s: (jnp.minimum(s, spans - 1), 0, 0)),
            pl.BlockSpec(ent.shape, lambda s: (0, 0)),
            pl.BlockSpec((span_rows, LANES), lambda s: (jnp.minimum(s, spans - 1), 0)),
            anym,
        ],
        out_specs=(anym, anym, anym, anym, pl.BlockSpec(ent.shape, lambda s: (0, 0))),
        scratch_shapes=[
            vm(total + 8), vm(total), vm(total + 8), vm(total),
            vm(span_rows), vm(span_rows), vm(span_rows), vm(span_rows), vm(span_rows),
            pltpu.SemaphoreType.DMA((4,)),
        ],
        compiler_params=pltpu.CompilerParams(vmem_limit_bytes=58 * 2**20),
        name="bucket",
    )(counts, ridx, nidx, rid, lhs, ent, rel_rows, slab)


def ring_rows(half, order):
    size, used = half, 0
    for name in order:
        size = size // (2 if name == "xhi" else RING)
        used += size if name == "xhi" else 3 * size
    return used


def reduce_kernel(
    width,
    state_ref, shard_ref, right_hbm, rel0_hbm, rel1_hbm, rel2_hbm,
    back_hbm, new0_hbm, new1_hbm, new2_hbm,
    *scratch,
):
    racc, rland, rring = scratch[0:4], scratch[4:8], scratch[8:12]
    pacc, pland, pring = scratch[12:15], scratch[15:18], scratch[18:21]
    news = scratch[21:24]
    back, send, recv, local = scratch[24:28]
    at = here()
    greet(
        [toward(at, axis, step) for axis in ("x", "y", "z") for step in (1, -1)]
        + [toward(at, "xhi", 1), toward(at, "core", 1), next_group(1), next_group(-1)]
    )
    net = Copies(send, recv, local)
    region = BLOCKS * PART
    backs = []
    bases = [None] * 3

    def right_flow(part):
        def done(base):
            mine = pl.ds(part * PART, PART)
            copy = net.to(next_group(1), racc[part].at[span_of(base, PART)], back.at[mine])
            yield
            copy.wait_recv()
            backs.append(net.home(back.at[mine], back_hbm.at[mine]))

        return sum_flow(
            net, at, right_hbm.at[pl.ds(part * region, region)], racc[part], rland[part], rring[part],
            PART_ORDER[part], done,
        )

    def piece_flow(piece):
        def done(base):
            bases[piece] = base
            return
            yield

        src = (rel0_hbm, rel1_hbm, rel2_hbm)[piece]
        return sum_flow(net, at, src, pacc[piece], pland[piece], pring[piece], PIECE_SUM[piece], done)

    pieces = [piece_flow(p) for p in range(3)]
    rights = [right_flow(p) for p in range(PARTS)]

    def all_pieces():
        yield from merged(pieces)
        planes = [pacc[p][span_of(bases[p], GROUP), :] for p in range(3)]
        planes.append(unpack_tail(pacc[2][span_of(bases[2] + GROUP, 8), :]))
        squares = planes[0] * planes[0]
        for plane in planes[1:]:
            squares = squares + plane * plane
        state = state_ref[...] + jnp.sum(squares, axis=1, keepdims=True) / width
        root = jnp.sqrt(state)
        fresh = [shard_ref[:, c * LANES : (c + 1) * LANES] - STEP_SIZE * planes[c] / root for c in range(CHUNKS)]
        tail = pack_tail(fresh[3])
        lane = lax.broadcasted_iota(jnp.int32, (8, LANES), 1)
        for g in range(GROUP // 8):
            tail = jnp.where(lane == LANES // 2 + g, state[8 * g : 8 * g + 8], tail)
        outs = (new0_hbm, new1_hbm, new2_hbm)
        flows = []
        for p in range(3):
            mine = (at["core"] * SHARDS + index_of(at, PIECE_OUT[p])) * PIECE_ROWS[p]
            news[p][span_of(mine, GROUP), :] = fresh[p]
            if p == 2:
                news[p][span_of(mine + GROUP, 8), :] = tail

            def arrived(start, size, p=p):
                rows = PIECE_ROWS[p]
                half, k = start // (SHARDS * rows), start // (16 * rows) % RING
                src = news[p].at[span_of(start, size)]
                if p == 0:
                    dst = outs[p].at[half, k]
                    src = src.reshape(4, 4, rows, LANES)
                elif p == 1:
                    dst = outs[p].at[half, :, :, k]
                    src = src.reshape(4, 4, rows, LANES)
                else:
                    dst = outs[p].at[half, :, k]
                    src = src.reshape(4, 4, rows, LANES)
                backs.append(net.home(src, dst))

            flows.append(spread_flow(net, at, news[p], 0, PIECE_ROWS[p], PIECE_OUT[p], arrived))
        yield from merged(flows)

    run_beside(rights, all_pieces())
    for copy in backs:
        copy.wait()
    net.finish()


def reduce(width, state, shard, right, pieces):
    anym = pl.BlockSpec(memory_space=pl.ANY)
    vmem = pl.BlockSpec(memory_space=pltpu.VMEM)
    vm = lambda r: pltpu.VMEM((r, LANES), F32)
    half = BLOCKS // 2 * PART
    return pl.pallas_call(
        functools.partial(reduce_kernel, width),
        out_shape=(
            jax.ShapeDtypeStruct((PARTS * PART, LANES), F32),
            *(jax.ShapeDtypeStruct((2, 4, 4, 4, r, LANES), F32) for r in PIECE_ROWS),
        ),
        in_specs=[vmem, vmem, anym, anym, anym, anym],
        out_specs=(anym,) * 4,
        scratch_shapes=[
            *(vm(half) for _ in range(PARTS)),
            *(vm(half) for _ in range(PARTS)),
            *(vm(ring_rows(half, PART_ORDER[p])) for p in range(PARTS)),
            *(vm(SHARDS * r) for r in PIECE_ROWS),
            *(vm(SHARDS * r) for r in PIECE_ROWS),
            *(vm(ring_rows(SHARDS * r, PIECE_SUM[p])) for p, r in enumerate(PIECE_ROWS)),
            *(vm(2 * SHARDS * r) for r in PIECE_ROWS),
            vm(PARTS * PART),
            pltpu.SemaphoreType.DMA((192,)),
            pltpu.SemaphoreType.DMA((192,)),
            pltpu.SemaphoreType.DMA((64,)),
        ],
        compiler_params=pltpu.CompilerParams(vmem_limit_bytes=56 * 2**20, collective_id=2, has_side_effects=True),
        name="reduce",
    )(state, shard, right, *pieces)


def finish_kernel(width, left_ref, back_ref, ent_ref, state_ref, new0, new1, new2, rel_ref, ent_out, state_out):
    s = pl.program_id(0)
    count = rel_ref.shape[1]
    for k in range(count // LANES):
        out = pl.ds(k * LANES, LANES)
        groups = range(k * 4, k * 4 + 4)
        for c, ref in enumerate((new0, new1, new2)):
            r = PIECE_ROWS[c]
            plane = jnp.concatenate([ref[g * r : g * r + GROUP, :] for g in groups], axis=0)
            rel_ref[c * LANES : (c + 1) * LANES, out] = plane.T
        r = PIECE_ROWS[2]
        tail = jnp.concatenate([unpack_tail(new2[g * r + GROUP : (g + 1) * r, :]) for g in groups], axis=0)
        rel_ref[3 * LANES : width, out] = tail.T[: width - 3 * LANES]

    @pl.when(s == 0)
    def _():
        for j in range(8):
            part = slice(j * GROUP, (j + 1) * GROUP)
            planes = [back_ref[pl.ds(j * PACK + c * GROUP, GROUP), :] for c in range(3)]
            planes.append(unpack_tail(back_ref[pl.ds(j * PACK + 96, 8), :]))
            grad = left_ref[part, :] + jnp.concatenate(planes, axis=1)
            state = state_ref[part, :] + jnp.sum(grad * grad, axis=1, keepdims=True) / width
            state_out[part, :] = state
            fresh = ent_ref[part, :] - STEP_SIZE * grad / jnp.sqrt(state)
            ent_out[part, :] = fresh[:, :width]


def finish(width, left, back, ent, ent_state, news, count):
    steps = 8
    full = lambda a: pl.BlockSpec(a.shape, lambda s: (0, 0))
    rows = ent.shape[0]
    return pl.pallas_call(
        functools.partial(finish_kernel, width),
        grid=(steps,),
        out_shape=(
            jax.ShapeDtypeStruct((width, count), F32),
            jax.ShapeDtypeStruct((rows, width), F32),
            jax.ShapeDtypeStruct((rows, 1), F32),
        ),
        in_specs=[full(a) for a in (left, back, ent, ent_state)]
        + [pl.BlockSpec((2 * SHARDS // steps * r, LANES), lambda s: (s, 0)) for r in PIECE_ROWS],
        out_specs=(
            pl.BlockSpec((width, count // steps), lambda s: (0, s)),
            pl.BlockSpec((rows, width), lambda s: (0, 0)),
            pl.BlockSpec((rows, 1), lambda s: (0, 0)),
        ),
        compiler_params=pltpu.CompilerParams(vmem_limit_bytes=60 * 2**20),
        name="finish",
    )(left, back, ent, ent_state, *news)


def on_device(
    entities, ent_state, relations, rel_state, lhs_rows, rhs_owner, rhs_off, neg_owner, neg_off, rel_ids, counts
):
    shard = entities[0]
    rows, width = shard.shape
    wide = CHUNKS * LANES
    padded = jnp.pad(shard, ((0, 0), (0, wide - width)))
    edges = lhs_rows.shape[1]
    spans = edges // SPAN
    ridx = rhs_owner[0, :, 0] * rows + rhs_off[0]
    nidx = (neg_owner[0, :, 0] * rows + neg_off[0]).reshape(spans, NEG)
    nidx = jnp.pad(nidx, ((0, 0), (0, SPAN - NEG)), constant_values=rows * BLOCKS).reshape(edges)
    rid = rel_ids[0]
    at = here()
    mine = (at["core"] * SHARDS + index_of(at, ("z", "y", "x"))) * GROUP
    rel_shard = jnp.pad(lax.dynamic_slice_in_dim(relations, mine, GROUP, 0), ((0, 0), (0, wide - width)))
    rel_state_shard = lax.dynamic_slice_in_dim(rel_state, mine, GROUP, 0)[:, None]

    slab, rel_rows = fetch(rid, padded, relations.T)
    right, *pieces, left = bucket(counts[0], ridx, nidx, rid, lhs_rows.reshape(spans, 1, SPAN), padded, rel_rows, slab)
    back, *news = reduce(width, rel_state_shard, rel_shard, right, pieces)
    rel_new, new_shard, new_state = finish(
        width, left, back, padded, ent_state[0][:, None], [n.reshape(-1, LANES) for n in news], relations.shape[0]
    )
    states = news[2].reshape(2 * SHARDS, PIECE_ROWS[2], LANES)[:, GROUP:, LANES // 2 : LANES // 2 + 4]
    states = states.transpose(0, 2, 1).reshape(-1)
    return (new_shard[None], new_state.reshape(1, rows), rel_new.T, states)


def solution(mesh):
    in_specs = (
        P("group", "member", None), P("group", "member"), P(), P(),
        P("group", "member"), P("group", "member", None), P("group", "member"),
        P("group", "member", None), P("group", "member"), P("group", "member"), P("group", "member"),
    )
    out_specs = (P("group", "member", None), P("group", "member"), P(), P())
    return jax.shard_map(on_device, mesh=mesh, in_specs=in_specs, out_specs=out_specs, check_vma=False)
```

```python
import functools
import jax
import jax.numpy as jnp
from jax import lax
from jax.experimental import pallas as pl
from jax.experimental.pallas import tpu as pltpu
from jax.sharding import PartitionSpec as P

SPAN = 512
NEG = 500
STEP_SIZE = 0.1
LANES = 128
F32 = jnp.float32
BF16 = jnp.bfloat16
MESH = pl.DeviceIdType.MESH

CHUNKS = 4
TAIL = 16
GROUP = 32
PACK = 104
BLOCKS = 16
RING = 4
Y_FIRST = ("y", "xhi")
X_FIRST = ("xhi", "y")
PART_IN = (X_FIRST, Y_FIRST) * 2
PART_SUM = (X_FIRST, Y_FIRST, Y_FIRST, Y_FIRST) * 2
PIECE_ROWS = (32, 32, 40)
PIECE_SUM = (("z", "y", "x"), ("x", "z", "y"), ("z", "x", "y"))
PIECE_OUT = (("z", "y", "x"), ("x", "z", "y"), ("y", "z", "x"))
SHARDS = 64
SHIFTS = 8
RINGS_IN = 8
RINGS_SUM = 2
LINK_ROWS = 85.0
CORE_ROWS = 1000.0
LATENCY = 1.7


def split(x):
    hi = x.astype(BF16)
    return hi, (x - hi.astype(F32)).astype(BF16)


def dot2(a, b, dims):
    return lax.dot_general(a, b, (dims, ((), ())), preferred_element_type=F32)


def dot3(a, b, dims):
    ah, al = a
    bh, bl = b
    return dot2(ah, bh, dims) + (dot2(ah, bl, dims) + dot2(al, bh, dims))


def row(i):
    return pl.ds(pl.multiple_of(i * CHUNKS, CHUNKS), CHUNKS)


def span_of(start, size, tile=8):
    return pl.ds(start if isinstance(start, int) else pl.multiple_of(start, tile), size)


def read_rows(ref, rows):
    return jnp.concatenate([ref[pl.ds(c, rows, stride=CHUNKS), :] for c in range(CHUNKS)], axis=1)


def write_rows(ref, value, rows):
    for c in range(CHUNKS):
        ref[pl.ds(c, rows, stride=CHUNKS), :] = value[:, c * LANES : (c + 1) * LANES]


def pack_tail(tail):
    packed = tail[0:8]
    for g in range(1, GROUP // 8):
        packed = packed + pltpu.roll(tail[8 * g : 8 * g + 8], TAIL * g, 1)
    return packed


def unpack_tail(packed):
    kept = lax.broadcasted_iota(jnp.int32, (8, LANES), 1) < TAIL
    parts = [jnp.where(kept, packed if g == 0 else pltpu.roll(packed, LANES - TAIL * g, 1), 0.0) for g in range(GROUP // 8)]
    return jnp.concatenate(parts, axis=0)


def digits_of(flat, order):
    sizes = {"y": 4, "xhi": 2, "x": 4, "z": 4}
    out = {}
    for name in reversed(order):
        out[name] = flat % sizes[name]
        flat = flat // sizes[name]
    return out


def index_of(where, order):
    sizes = {"y": 4, "xhi": 2, "x": 4, "z": 4}
    at = 0
    for name in order:
        at = at * sizes[name] + where[name]
    return at


def part_size(orders):
    return 256 // GROUP * PACK // len(orders)


def part_row(member, part, orders):
    where = digits_of(member // 2, ("y", "xhi"))
    at = (member % 2) * 8 + index_of(where, orders[part])
    return (part * BLOCKS + at) * part_size(orders)


def shard_row(group, piece, orders):
    where = digits_of(group % SHARDS, ("z", "y", "x"))
    return ((group // SHARDS) * SHARDS + index_of(where, orders[piece])) * PIECE_ROWS[piece]


def here():
    g = lax.axis_index("group")
    m = lax.axis_index("member")
    return {"x": (m // 2) % 2 * 2 + g // 4, "xhi": (m // 2) % 2, "y": m // 4, "z": g % 4, "core": m % 2}


def device(at):
    return (at["x"] % 2 * 4 + at["z"], at["y"] * 4 + at["x"] // 2 * 2 + at["core"])


def toward(at, axis, step):
    there = dict(at)
    if axis == "core":
        there["core"] = 1 - at["core"]
    elif axis == "xhi":
        there["x"] = (at["x"] + 2) % 4
    else:
        there[axis] = (at[axis] + step + 4) % 4
    return device(there)


def next_group(step):
    return ((lax.axis_index("group") + step + 8) % 8, lax.axis_index("member"))


def greet(devices):
    barrier = pltpu.get_barrier_semaphore()
    for there in devices:
        pl.semaphore_signal(barrier, inc=1, device_id=there, device_id_type=MESH)
    pl.semaphore_wait(barrier, len(devices))


class Copies:
    def __init__(self, send, recv, local):
        self.send, self.recv, self.local = send, recv, local
        self.started, self.kept, self.homes = 0, [], 0
        self.now, self.busy, self.flows, self.added, self.gates = 0.0, {}, [], 0, {}

    def to(self, there, src, dst, links, rows):
        copy = pltpu.make_async_remote_copy(
            src_ref=src, dst_ref=dst, send_sem=self.send.at[self.started], recv_sem=self.recv.at[self.started],
            device_id=there, device_id_type=MESH,
        )
        copy.start()
        self.started += 1
        self.kept.append(copy)
        begin = max([self.now] + [self.busy.get(link, 0.0) for link in links])
        end = begin + rows / (CORE_ROWS if links == ("core",) else LINK_ROWS)
        for link in links:
            self.busy[link] = end
        self.now += 0.05
        return copy, end + LATENCY

    def home(self, src, dst):
        copy = pltpu.make_async_copy(src, dst, self.local.at[self.homes])
        copy.start()
        self.homes += 1
        return copy

    def enter(self, name, limit):
        held, waiting = self.gates.setdefault(name, ([], []))
        if len(held) == limit:
            yield waiting
        held.append(None)

    def leave(self, name):
        held, waiting = self.gates[name]
        held.pop()
        if waiting:
            number, flow = waiting.pop(0)
            self.step(number, flow)

    def step(self, number, flow):
        ready = next(flow, None)
        if ready is None:
            return
        if any(ready is waiting for _, waiting in self.gates.values()):
            ready.append((number, flow))
        else:
            self.flows.append((max(r for _, r in ready), number, flow))

    def add(self, flow):
        self.added += 1
        self.step(self.added, flow)

    def run(self, beside=iter(()), cost=0.7):
        while self.flows:
            entry = min(self.flows)
            while entry[0] > self.now + cost and next(beside, None) is not None:
                self.now += cost
            self.flows.remove(entry)
            self.now = max(self.now, entry[0]) + 0.1
            self.step(entry[1], entry[2])
        for _ in beside:
            pass

    def finish(self):
        for copy in self.kept:
            copy.wait_send()


def wait_all(copies):
    for copy, _ in copies:
        copy.wait_recv()


def halves(size):
    first = -(-size // 16) * 8
    return first, size - first


def add_into(dst, at, src, start, size):
    tile = size
    while tile > 256:
        tile = tile // 2 if tile % 16 == 0 else tile // 13
    if tile == size:
        dst[span_of(at, size), :] = dst[span_of(at, size), :] + src[span_of(start, size), :]
        return

    def step(i, carry):
        d = span_of(at + i * tile, tile)
        dst[d, :] = dst[d, :] + src[span_of(start + i * tile, tile), :]
        return carry

    lax.fori_loop(0, size // tile, step, 0)


def both(axis):
    return (axis + "+", axis + "-")


def sum_flow(net, at, src, acc, landing, ring, order, direct, done):
    half = acc.shape[0]
    core = at["core"]
    over = net.to(toward(at, "core", 1), src.at[span_of((1 - core) * half, half)], landing, ("core",), half)
    own = net.home(src.at[span_of(core * half, half)], acc)
    yield [over]
    own.wait()
    wait_all([over])
    add_into(acc, 0, landing, 0, half)
    base, size, used = 0, half, 0
    for level, axis in enumerate(order):
        a = at[axis]
        if axis == "xhi":
            size = size // 2
            src_at = acc.at[span_of(base + (1 - a) * size, size)]
            copies = [net.to(toward(at, axis, 1), src_at, ring.at[pl.ds(used, size)], both("x"), size)]
            yield copies
            wait_all(copies)
            add_into(acc, base + a * size, ring, used, size)
            used += size
        else:
            size = size // RING
            up, down, far = (base + (a + k) % RING * size for k in (1, 3, 2))
            above, below, opposite = (toward(at, axis, k) for k in (1, -1, 2))
            plus, minus = ((link,) for link in both(axis))
            ra, rc, rd = used, used + size, used + 2 * size
            if level >= direct:
                copies = [
                    net.to(opposite, acc.at[span_of(far, size)], ring.at[pl.ds(ra, size)], both(axis), size),
                    net.to(above, acc.at[span_of(up, size)], ring.at[pl.ds(rc, size)], plus, size),
                    net.to(below, acc.at[span_of(down, size)], ring.at[pl.ds(rd, size)], minus, size),
                ]
                yield copies
                wait_all(copies)
                add_into(acc, base + a * size, ring, ra, size)
            else:
                h1, h2 = halves(size)
                yield from net.enter(axis, RINGS_SUM)
                first = net.to(above, acc.at[span_of(far, h1)], ring.at[pl.ds(ra, h1)], plus, h1)
                second = net.to(below, acc.at[span_of(far + h1, h2)], ring.at[pl.ds(ra + h1, h2)], minus, h2)
                c2 = net.to(above, acc.at[span_of(up + h1, h2)], ring.at[pl.ds(rc + h1, h2)], plus, h2)
                d1 = net.to(below, acc.at[span_of(down, h1)], ring.at[pl.ds(rd, h1)], minus, h1)
                yield [first, second]
                wait_all([first])
                add_into(acc, up, ring, ra, h1)
                c1 = net.to(above, acc.at[span_of(up, h1)], ring.at[pl.ds(rc, h1)], plus, h1)
                wait_all([second])
                add_into(acc, down + h1, ring, ra + h1, h2)
                d2 = net.to(below, acc.at[span_of(down + h1, h2)], ring.at[pl.ds(rd + h1, h2)], minus, h2)
                copies = [c2, d1, c1, d2]
                yield copies
                wait_all(copies)
                net.leave(axis)
            add_into(acc, base + a * size, ring, rc, size)
            add_into(acc, base + a * size, ring, rd, size)
            used += 3 * size
        base = base + a * size
    yield from done(base)


def spread_flow(net, at, buf, offset, rows, order, direct, arrived):
    radix = {"xhi": 2, "x": 4, "y": 4, "z": 4}
    total = rows
    for name in order:
        total *= radix[name]
    core = at["core"]
    bases = [offset + core * total]
    strides = []
    size = total
    for name in order:
        size = size // radix[name]
        strides.append(size)
        bases.append(bases[-1] + at[name] * size)
    sibling = toward(at, "core", 1)
    shared = []

    def share(start, size):
        there = span_of(start, size)
        copy = net.to(sibling, buf.at[there], buf.at[there], ("core",), size)
        shared.append((copy, start + (1 - 2 * core) * total, size))

    def send(there, start, size, links):
        part = span_of(start, size)
        return net.to(there, buf.at[part], buf.at[part], links, size)

    for level in reversed(range(len(order))):
        name, size, region = order[level], strides[level], bases[level]
        a = at[name]
        last = level == 0
        if name == "xhi":
            other = region + (1 - a) * size
            copies = [send(toward(at, name, 1), region + a * size, size, both("x"))]
            if last:
                share(region + a * size, size)
                arrived(region + a * size, size)
            yield copies
            wait_all(copies)
            if last:
                share(other, size)
                arrived(other, size)
        else:
            h1, h2 = halves(size)
            own, up, down, far = (region + (a + k) % RING * size for k in (0, 1, 3, 2))
            above, below, opposite = (toward(at, name, k) for k in (1, -1, 2))
            plus, minus = ((link,) for link in both(name))
            if level < direct:
                yield from net.enter(name, RINGS_IN)
            e = send(above, own, size, plus)
            f = send(below, own, size, minus)
            if last:
                share(own, size)
            if level >= direct:
                g = send(opposite, own, size, both(name))
                yield [e, f, g]
                wait_all([e, f, g])
            else:
                if last:
                    arrived(own, size)
                yield [e, f]
                wait_all([e])
                g = send(above, down, h1, plus)
                wait_all([f])
                h = send(below, up + h1, h2, minus)
                if last:
                    share(down, size)
                    share(up, size)
                    arrived(down, size)
                    arrived(up, size)
                yield [g, h]
                wait_all([g, h])
                net.leave(name)
                if last:
                    share(far, size)
                    arrived(far, size)
    for copy, start, size in shared:
        yield [copy]
        wait_all([copy])
        arrived(start, size)


def fetch_kernel(rid_ref, ent_ref, rel_hbm, slab_hbm, rows_hbm, own, packed, slab, rel, rel_rows, got, send, recv, local):
    at = here()
    m = lax.axis_index("member")
    greet(
        [toward(at, "y", 1), toward(at, "y", -1), toward(at, "xhi", 1), toward(at, "core", 1), next_group(1), next_group(-1)]
    )
    net = Copies(send, recv, local)
    entry = net.home(rel_hbm, rel)
    for j in range(8):
        rows = slice(j * GROUP, (j + 1) * GROUP)
        for c in range(3):
            own[pl.ds(j * PACK + c * GROUP, GROUP), :] = ent_ref[rows, c * LANES : (c + 1) * LANES]
        own[pl.ds(j * PACK + 96, 8), :] = pack_tail(ent_ref[rows, 3 * LANES : 4 * LANES])

    writes = []
    parts = len(PART_IN)
    size = part_size(PART_IN)
    groups = size // PACK

    def flow(part):
        start = part * BLOCKS * size
        mine = span_of(part_row(m, part, PART_IN), size)
        yield from net.enter("shift", SHIFTS)
        shift = net.to(next_group(-1), own.at[pl.ds(part * size, size)], packed.at[mine], ("z-",), size)
        yield [shift]
        wait_all([shift])
        net.leave("shift")

        def arrived(begin, rows):
            def block(i, carry):
                source = begin + i * size
                flat = (source - start) // size
                where = digits_of(flat % 8, PART_IN[part])
                member = (where["y"] * 2 + where["xhi"]) * 2 + flat // 8
                for k in range(groups):
                    base = source + k * PACK
                    out = (member * 256 + (part * groups + k) * GROUP) * CHUNKS
                    out = pl.multiple_of(out, 128)
                    for c in range(3):
                        slab[pl.ds(out + c, GROUP, stride=CHUNKS), :] = packed[span_of(base + c * GROUP, GROUP), :]
                    slab[pl.ds(out + 3, GROUP, stride=CHUNKS), :] = unpack_tail(packed[span_of(base + 96, 8), :])
                return carry

            lax.fori_loop(0, rows // size, block, 0)
            net.now += 0.04 * rows / PACK

        yield from spread_flow(net, at, packed, start, size, PART_IN[part], 9, arrived)
        view = (BLOCKS, parts, groups * GROUP * CHUNKS, LANES)
        writes.append(net.home(slab.reshape(view).at[:, part], slab_hbm.reshape(view).at[:, part]))

    def gather():
        tile = 256
        width, total = rel.shape
        entry.wait()
        for t in range(total // (4 * tile)):
            def convert(i, carry):
                k = t * 4 + i
                part = span_of(k * tile, tile, tile)
                wide = jnp.concatenate([rel[:, part], jnp.zeros((CHUNKS * LANES - width, tile), F32)], axis=0)
                rel_rows[part] = wide.T.reshape(tile, CHUNKS, LANES)
                return carry

            lax.fori_loop(0, 4, convert, 0)
            yield True
        edges = got.shape[0] // CHUNKS
        segment, unroll = 512, 16
        for t in range(edges // segment):
            def step(b, carry):
                for u in range(unroll):
                    j = t * segment + b * unroll + u
                    got[row(j), :] = rel_rows[rid_ref[j]]
                return carry

            lax.fori_loop(0, segment // unroll, step, 0)
            part = pl.ds(t * segment * CHUNKS, segment * CHUNKS)
            writes.append(net.home(got.at[part], rows_hbm.at[part]))
            yield True

    for part in range(parts):
        net.add(flow(part))
    net.run(gather())
    for write in writes:
        write.wait()
    net.finish()


def fetch(rid, ent, relations):
    edges = rid.shape[0]
    width, count = relations.shape
    rows = ent.shape[0] * BLOCKS
    anym = pl.BlockSpec(memory_space=pl.ANY)
    return pl.pallas_call(
        fetch_kernel,
        out_shape=(
            jax.ShapeDtypeStruct((rows * CHUNKS, LANES), F32),
            jax.ShapeDtypeStruct((edges * CHUNKS, LANES), F32),
        ),
        in_specs=[pl.BlockSpec(memory_space=pltpu.SMEM), pl.BlockSpec(memory_space=pltpu.VMEM), anym],
        out_specs=(anym, anym),
        scratch_shapes=[
            pltpu.VMEM((256 // GROUP * PACK, LANES), F32),
            pltpu.VMEM((rows // GROUP * PACK, LANES), F32),
            pltpu.VMEM((rows * CHUNKS, LANES), F32),
            pltpu.VMEM((width, count), F32),
            pltpu.VMEM((count, CHUNKS, LANES), F32),
            pltpu.VMEM((edges * CHUNKS, LANES), F32),
            pltpu.SemaphoreType.DMA((128,)),
            pltpu.SemaphoreType.DMA((128,)),
            pltpu.SemaphoreType.DMA((24,)),
        ],
        compiler_params=pltpu.CompilerParams(vmem_limit_bytes=56 * 2**20, collective_id=1, has_side_effects=True),
        name="fetch",
    )(rid, ent, relations)


def bucket_kernel(
    spans, unroll,
    cnt_ref, ridx_ref, nidx_ref, rid_ref, lhs_ref, ent_ref, rel_ref, slab_hbm,
    right_hbm, rel0_hbm, rel1_hbm, rel2_hbm, left_ref,
    slab, racc, nacc, relacc, rvec, nvec, gr, gn, grel, sem,
):
    s = pl.program_id(0)
    total = racc.shape[0]

    @pl.when(s == 0)
    def _():
        load = pltpu.make_async_copy(slab_hbm, slab.at[pl.ds(0, total)], sem.at[0])
        load.start()
        slab[pl.ds(total, 8), :] = jnp.zeros((8, LANES), F32)
        racc[...] = jnp.zeros_like(racc)
        nacc[...] = jnp.zeros_like(nacc)
        relacc[...] = jnp.zeros_like(relacc)
        left_ref[...] = jnp.zeros_like(left_ref)
        load.wait()

    def scatter(j, base):
        rel = row(rid_ref[base + j])
        rgt = row(ridx_ref[base + j])
        neg = row(nidx_ref[base + j])
        own = row(j)
        relacc[rel, :] = relacc[rel, :] + grel[own, :]
        racc[rgt, :] = racc[rgt, :] + gr[own, :]
        nacc[neg, :] = nacc[neg, :] + gn[own, :]

    def gather(j, base):
        own = row(j)
        rvec[own, :] = slab[row(ridx_ref[base + j]), :]
        nvec[own, :] = slab[row(nidx_ref[base + j]), :]

    behind = (s - 1) * SPAN
    ahead = s * SPAN

    def rows_loop(*works):
        def step(b, carry):
            for u in range(unroll):
                for work, base in works:
                    work(b * unroll + u, base)
            return carry

        lax.fori_loop(0, SPAN // unroll, step, 0)

    @pl.when(s == 0)
    def _():
        rows_loop((gather, ahead))

    @pl.when((s > 0) & (s < spans))
    def _():
        rows_loop((gather, ahead), (scatter, behind))

    @pl.when(s == spans)
    def _():
        rows_loop((scatter, behind))

    @pl.when(s < spans)
    def _():
        hot = (lax.broadcasted_iota(jnp.int32, (ent_ref.shape[0], SPAN), 0) == lhs_ref[0]).astype(F32).astype(BF16)
        eh, el = split(ent_ref[...])
        first = ((0,), (0,))
        last = ((1,), (1,))
        inner = ((1,), (0,))
        left = dot2(hot, eh, first) + dot2(hot, el, first)
        rel = read_rows(rel_ref, SPAN)
        query = left * rel
        live = (s * SPAN + lax.broadcasted_iota(jnp.int32, (SPAN, 1), 0) < cnt_ref[0]).astype(F32)
        q = split(query)
        n = split(read_rows(nvec, SPAN))
        neg = dot3(q, n, last)
        dneg = split(jax.nn.sigmoid(neg) * (live / NEG))
        right = read_rows(rvec, SPAN)
        pos = jnp.sum(query * right, axis=1, keepdims=True)
        dpos = -jax.nn.sigmoid(-pos) * live
        write_rows(gr, dpos * query, SPAN)
        write_rows(gn, dot3(dneg, q, first), SPAN)
        grad_query = dpos * right + dot3(dneg, n, inner)
        write_rows(grel, grad_query * left, SPAN)
        gl = split(grad_query * rel)
        left_ref[...] += dot2(hot, gl[0], inner) + dot2(hot, gl[1], inner)

    @pl.when(s == spans)
    def _():
        def right_member(m, carry):
            for part in range(len(PART_SUM)):
                for k in range(256 // GROUP // len(PART_SUM)):
                    at = part * (256 // GROUP // len(PART_SUM)) + k
                    src = pl.multiple_of((m * 256 + at * GROUP) * CHUNKS, 128)
                    out = part_row(m, part, PART_SUM) + k * PACK
                    planes = [
                        racc[pl.ds(src + c, GROUP, stride=CHUNKS), :] + nacc[pl.ds(src + c, GROUP, stride=CHUNKS), :]
                        for c in range(CHUNKS)
                    ]
                    for c in range(3):
                        slab[span_of(out + c * GROUP, GROUP), :] = planes[c]
                    slab[span_of(out + 96, 8), :] = pack_tail(planes[3])
            return carry

        lax.fori_loop(0, BLOCKS, right_member, 0)
        out = pltpu.make_async_copy(slab.at[pl.ds(0, right_hbm.shape[0])], right_hbm, sem.at[0])
        out.start()
        begins = (0, 2 * SHARDS * PIECE_ROWS[0], 2 * SHARDS * (PIECE_ROWS[0] + PIECE_ROWS[1]))

        def shards(i, carry):
            for k in range(4):
                group = i * 4 + k
                src = pl.multiple_of(group * GROUP * CHUNKS, 128)
                at = [b + shard_row(group, p, PIECE_SUM) for p, b in enumerate(begins)]
                for c in range(3):
                    nacc[span_of(at[c], GROUP), :] = relacc[pl.ds(src + c, GROUP, stride=CHUNKS), :]
                nacc[span_of(at[2] + GROUP, 8), :] = pack_tail(relacc[pl.ds(src + 3, GROUP, stride=CHUNKS), :])
            return carry

        lax.fori_loop(0, 2 * SHARDS // 4, shards, 0)
        copies = [
            pltpu.make_async_copy(nacc.at[pl.ds(b, ref.shape[0])], ref, sem.at[1 + p])
            for p, (b, ref) in enumerate(zip(begins, (rel0_hbm, rel1_hbm, rel2_hbm)))
        ]
        for copy in copies:
            copy.start()
        for copy in copies:
            copy.wait()
        out.wait()


def bucket(counts, ridx, nidx, rid, lhs, ent, rel_rows, slab):
    edges = rid.shape[0]
    spans = edges // SPAN
    total = slab.shape[0]
    smem = pl.BlockSpec(memory_space=pltpu.SMEM)
    anym = pl.BlockSpec(memory_space=pl.ANY)
    vm = lambda r: pltpu.VMEM((r, LANES), F32)
    span_rows = SPAN * CHUNKS
    return pl.pallas_call(
        functools.partial(bucket_kernel, spans, 16),
        grid=(spans + 1,),
        out_shape=(
            jax.ShapeDtypeStruct((BLOCKS * 256 // GROUP * PACK, LANES), F32),
            *(jax.ShapeDtypeStruct((2 * SHARDS * r, LANES), F32) for r in PIECE_ROWS),
            jax.ShapeDtypeStruct(ent.shape, F32),
        ),
        in_specs=[
            smem, smem, smem, smem,
            pl.BlockSpec((1, 1, SPAN), lambda s: (jnp.minimum(s, spans - 1), 0, 0)),
            pl.BlockSpec(ent.shape, lambda s: (0, 0)),
            pl.BlockSpec((span_rows, LANES), lambda s: (jnp.minimum(s, spans - 1), 0)),
            anym,
        ],
        out_specs=(anym, anym, anym, anym, pl.BlockSpec(ent.shape, lambda s: (0, 0))),
        scratch_shapes=[
            vm(total + 8), vm(total), vm(total + 8), vm(total),
            vm(span_rows), vm(span_rows), vm(span_rows), vm(span_rows), vm(span_rows),
            pltpu.SemaphoreType.DMA((4,)),
        ],
        compiler_params=pltpu.CompilerParams(vmem_limit_bytes=58 * 2**20),
        name="bucket",
    )(counts, ridx, nidx, rid, lhs, ent, rel_rows, slab)


def ring_rows(half, order):
    size, used = half, 0
    for name in order:
        size = size // (2 if name == "xhi" else RING)
        used += size if name == "xhi" else 3 * size
    return used


def reduce_kernel(
    width,
    state_ref, shard_ref, right_hbm, rel0_hbm, rel1_hbm, rel2_hbm,
    back_hbm, new0_hbm, new1_hbm, new2_hbm,
    *scratch,
):
    scratch = list(scratch)
    take = lambda n: [scratch.pop(0) for _ in range(n)]
    parts = len(PART_SUM)
    racc, rland, rring = take(parts), take(parts), take(parts)
    pacc, pland, pring, news = take(3), take(3), take(3), take(3)
    back, send, recv, local = scratch
    at = here()
    greet(
        [toward(at, axis, step) for axis in ("x", "y", "z") for step in (1, -1, 2)]
        + [toward(at, "core", 1), next_group(1), next_group(-1)]
    )
    net = Copies(send, recv, local)
    size = part_size(PART_SUM)
    region = BLOCKS * size
    backs = []
    bases = {}

    def right_flow(part):
        def done(base):
            mine = pl.ds(part * size, size)
            src = racc[part].at[span_of(base, size)]
            copies = [net.to(next_group(1), src, back.at[mine], ("z+",), size)]
            yield copies
            wait_all(copies)
            backs.append(net.home(back.at[mine], back_hbm.at[mine]))

        return sum_flow(
            net, at, right_hbm.at[pl.ds(part * region, region)], racc[part], rland[part], rring[part],
            PART_SUM[part], 9, done,
        )

    def piece_flow(piece):
        def done(base):
            bases[piece] = base
            if len(bases) == 3:
                update()
            yield from ()

        src = (rel0_hbm, rel1_hbm, rel2_hbm)[piece]
        return sum_flow(net, at, src, pacc[piece], pland[piece], pring[piece], PIECE_SUM[piece], 1, done)

    def update():
        planes = [pacc[p][span_of(bases[p], GROUP), :] for p in range(3)]
        planes.append(unpack_tail(pacc[2][span_of(bases[2] + GROUP, 8), :]))
        squares = planes[0] * planes[0]
        for plane in planes[1:]:
            squares = squares + plane * plane
        state = state_ref[...] + jnp.sum(squares, axis=1, keepdims=True) / width
        root = jnp.sqrt(state)
        fresh = [shard_ref[:, c * LANES : (c + 1) * LANES] - STEP_SIZE * planes[c] / root for c in range(CHUNKS)]
        tail = pack_tail(fresh[3])
        lane = lax.broadcasted_iota(jnp.int32, (8, LANES), 1)
        for g in range(GROUP // 8):
            tail = jnp.where(lane == LANES // 2 + g, state[8 * g : 8 * g + 8], tail)
        outs = (new0_hbm, new1_hbm, new2_hbm)
        net.now += 0.5
        for p in range(3):
            mine = (at["core"] * SHARDS + index_of(at, PIECE_OUT[p])) * PIECE_ROWS[p]
            news[p][span_of(mine, GROUP), :] = fresh[p]
            if p == 2:
                news[p][span_of(mine + GROUP, 8), :] = tail

            def arrived(start, size, p=p):
                rows = PIECE_ROWS[p]
                half, k = start // (SHARDS * rows), start // (16 * rows) % RING
                src = news[p].at[span_of(start, size)].reshape(4, 4, rows, LANES)
                dst = (outs[p].at[half, k], outs[p].at[half, :, :, k], outs[p].at[half, :, k])[p]
                backs.append(net.home(src, dst))

            net.add(spread_flow(net, at, news[p], 0, PIECE_ROWS[p], PIECE_OUT[p], 1, arrived))

    for k in range(max(3, parts)):
        if k < 3:
            net.add(piece_flow(k))
        if k < parts:
            net.add(right_flow(k))
    net.run()
    for copy in backs:
        copy.wait()
    net.finish()


def reduce(width, state, shard, right, pieces):
    anym = pl.BlockSpec(memory_space=pl.ANY)
    vmem = pl.BlockSpec(memory_space=pltpu.VMEM)
    vm = lambda r: pltpu.VMEM((r, LANES), F32)
    parts = len(PART_SUM)
    half = BLOCKS // 2 * part_size(PART_SUM)
    return pl.pallas_call(
        functools.partial(reduce_kernel, width),
        out_shape=(
            jax.ShapeDtypeStruct((256 // GROUP * PACK, LANES), F32),
            *(jax.ShapeDtypeStruct((2, 4, 4, 4, r, LANES), F32) for r in PIECE_ROWS),
        ),
        in_specs=[vmem, vmem, anym, anym, anym, anym],
        out_specs=(anym,) * 4,
        scratch_shapes=[
            *(vm(half) for _ in range(parts)),
            *(vm(half) for _ in range(parts)),
            *(vm(ring_rows(half, PART_SUM[p])) for p in range(parts)),
            *(vm(SHARDS * r) for r in PIECE_ROWS),
            *(vm(SHARDS * r) for r in PIECE_ROWS),
            *(vm(ring_rows(SHARDS * r, PIECE_SUM[p])) for p, r in enumerate(PIECE_ROWS)),
            *(vm(2 * SHARDS * r) for r in PIECE_ROWS),
            vm(256 // GROUP * PACK),
            pltpu.SemaphoreType.DMA((192,)),
            pltpu.SemaphoreType.DMA((192,)),
            pltpu.SemaphoreType.DMA((64,)),
        ],
        compiler_params=pltpu.CompilerParams(vmem_limit_bytes=56 * 2**20, collective_id=2, has_side_effects=True),
        name="reduce",
    )(state, shard, right, *pieces)


def finish_kernel(
    width, left_ref, back_ref, ent_ref, state_ref, new0, new1, new2, rel_ref, rel_state_ref, ent_out, state_out
):
    s = pl.program_id(0)
    count = rel_ref.shape[1]
    lane = lax.broadcasted_iota(jnp.int32, (8, LANES), 1)
    for k in range(count // LANES):
        out = pl.ds(k * LANES, LANES)
        groups = range(k * 4, k * 4 + 4)
        for c, ref in enumerate((new0, new1, new2)):
            r = PIECE_ROWS[c]
            plane = jnp.concatenate([ref[g * r : g * r + GROUP, :] for g in groups], axis=0)
            rel_ref[c * LANES : (c + 1) * LANES, out] = plane.T
        r = PIECE_ROWS[2]
        tails = []
        for group in groups:
            packed = new2[group * r + GROUP : (group + 1) * r, :]
            for g in range(GROUP // 8):
                state = pltpu.roll(packed, LANES // 2 + TAIL - g, 1)
                values = packed if g == 0 else pltpu.roll(packed, LANES - TAIL * g, 1)
                tails.append(jnp.where(lane < TAIL, values, state))
        tail = jnp.concatenate(tails, axis=0).T
        rel_ref[3 * LANES : width, out] = tail[: width - 3 * LANES]
        rel_state_ref[:, out] = tail[TAIL : TAIL + 1]

    @pl.when(s == 0)
    def _():
        for i in range(2):
            part = slice(i * LANES, (i + 1) * LANES)
            wide = []
            for j in range(4 * i, 4 * i + 4):
                planes = [back_ref[pl.ds(j * PACK + c * GROUP, GROUP), :] for c in range(3)]
                planes.append(unpack_tail(back_ref[pl.ds(j * PACK + 96, 8), :]))
                wide.append(jnp.concatenate(planes, axis=1))
            grad = (left_ref[part, :] + jnp.concatenate(wide, axis=0)).T[:width]
            state = state_ref[:, part] + jnp.sum(grad * grad, axis=0, keepdims=True) / width
            state_out[:, part] = state
            ent_out[:, part] = ent_ref[:, part] - STEP_SIZE * grad / jnp.sqrt(state)


def finish(width, left, back, ent, ent_state, news, count):
    steps = 8
    full = lambda a: pl.BlockSpec(a.shape, lambda s: (0, 0))
    rows = ent.shape[1]
    return pl.pallas_call(
        functools.partial(finish_kernel, width),
        grid=(steps,),
        out_shape=(
            jax.ShapeDtypeStruct((width, count), F32),
            jax.ShapeDtypeStruct((1, count), F32),
            jax.ShapeDtypeStruct((width, rows), F32),
            jax.ShapeDtypeStruct((1, rows), F32),
        ),
        in_specs=[full(a) for a in (left, back, ent, ent_state)]
        + [pl.BlockSpec((2 * SHARDS // steps * r, LANES), lambda s: (s, 0)) for r in PIECE_ROWS],
        out_specs=(
            pl.BlockSpec((width, count // steps), lambda s: (0, s)),
            pl.BlockSpec((1, count // steps), lambda s: (0, s)),
            pl.BlockSpec((width, rows), lambda s: (0, 0)),
            pl.BlockSpec((1, rows), lambda s: (0, 0)),
        ),
        compiler_params=pltpu.CompilerParams(vmem_limit_bytes=60 * 2**20),
        name="finish",
    )(left, back, ent, ent_state, *news)


def on_device(
    entities, ent_state, relations, rel_state, lhs_rows, rhs_owner, rhs_off, neg_owner, neg_off, rel_ids, counts
):
    shard = entities[0]
    rows, width = shard.shape
    wide = CHUNKS * LANES
    padded = jnp.pad(shard, ((0, 0), (0, wide - width)))
    edges = lhs_rows.shape[1]
    spans = edges // SPAN
    ridx = rhs_owner[0, :, 0] * rows + rhs_off[0]
    nidx = (neg_owner[0, :, 0] * rows + neg_off[0]).reshape(spans, NEG)
    nidx = jnp.pad(nidx, ((0, 0), (0, SPAN - NEG)), constant_values=rows * BLOCKS).reshape(edges)
    rid = rel_ids[0]
    at = here()
    mine = (at["core"] * SHARDS + index_of(at, ("z", "y", "x"))) * GROUP
    rel_shard = jnp.pad(lax.dynamic_slice_in_dim(relations, mine, GROUP, 0), ((0, 0), (0, wide - width)))
    rel_state_shard = lax.dynamic_slice_in_dim(rel_state, mine, GROUP, 0)[:, None]

    slab, rel_rows = fetch(rid, padded, relations.T)
    right, *pieces, left = bucket(counts[0], ridx, nidx, rid, lhs_rows.reshape(spans, 1, SPAN), padded, rel_rows, slab)
    back, *news = reduce(width, rel_state_shard, rel_shard, right, pieces)
    rel_new, states, new_shard, new_state = finish(
        width, left, back, shard.T, ent_state, [n.reshape(-1, LANES) for n in news], relations.shape[0]
    )
    return (new_shard.T[None], new_state, rel_new.T, states.reshape(-1))


def solution(mesh):
    in_specs = (
        P("group", "member", None), P("group", "member"), P(), P(),
        P("group", "member"), P("group", "member", None), P("group", "member"),
        P("group", "member", None), P("group", "member"), P("group", "member"), P("group", "member"),
    )
    out_specs = (P("group", "member", None), P("group", "member"), P(), P())
    return jax.shard_map(on_device, mesh=mesh, in_specs=in_specs, out_specs=out_specs, check_vma=False)
```

```python
import functools
import jax
import jax.numpy as jnp
from jax import lax
from jax.experimental import pallas as pl
from jax.experimental.pallas import tpu as pltpu
from jax.sharding import PartitionSpec as P

SPAN = 512
NEG = 500
STEP_SIZE = 0.1
LANES = 128
F32 = jnp.float32
BF16 = jnp.bfloat16
MESH = pl.DeviceIdType.MESH

CHUNKS = 4
TAIL = 16
GROUP = 32
PACK = 104
BLOCKS = 16
RING = 4
Y_FIRST = ("y", "xhi")
X_FIRST = ("xhi", "y")
PART_IN = (X_FIRST, Y_FIRST) * 3 + (Y_FIRST, Y_FIRST)
PART_SUM = (X_FIRST, Y_FIRST, Y_FIRST, Y_FIRST) * 2
PIECE_ROWS = (32, 32, 40)
PIECE_SUM = (("z", "y", "x"), ("x", "z", "y"), ("z", "x", "y"))
PIECE_OUT = (("z", "y", "x"), ("x", "z", "y"), ("y", "z", "x"))
SHARDS = 64
SHIFTS = 8
RINGS_IN = 8
RINGS_SUM = 2
LINK_ROWS = 70.0
CORE_ROWS = 1000.0
LATENCY = 4.0


def split(x):
    hi = x.astype(BF16)
    return hi, (x - hi.astype(F32)).astype(BF16)


def dot2(a, b, dims):
    return lax.dot_general(a, b, (dims, ((), ())), preferred_element_type=F32)


def dot3(a, b, dims):
    (ah, al), (bh, bl) = a, b
    (ka,), (kb,) = dims
    return dot2(jnp.concatenate([ah, ah, al], axis=ka), jnp.concatenate([bh, bl, bh], axis=kb), dims)


def row(i):
    return pl.ds(pl.multiple_of(i * CHUNKS, CHUNKS), CHUNKS)


def span_of(start, size, tile=8):
    return pl.ds(start if isinstance(start, int) else pl.multiple_of(start, tile), size)


def read_rows(ref, rows):
    return jnp.concatenate([ref[pl.ds(c, rows, stride=CHUNKS), :] for c in range(CHUNKS)], axis=1)


def write_rows(ref, value, rows):
    for c in range(CHUNKS):
        ref[pl.ds(c, rows, stride=CHUNKS), :] = value[:, c * LANES : (c + 1) * LANES]


def pack_tail(tail):
    packed = tail[0:8]
    for g in range(1, GROUP // 8):
        packed = packed + pltpu.roll(tail[8 * g : 8 * g + 8], TAIL * g, 1)
    return packed


def unpack_tail(packed):
    kept = lax.broadcasted_iota(jnp.int32, (8, LANES), 1) < TAIL
    parts = [jnp.where(kept, packed if g == 0 else pltpu.roll(packed, LANES - TAIL * g, 1), 0.0) for g in range(GROUP // 8)]
    return jnp.concatenate(parts, axis=0)


def digits_of(flat, order):
    sizes = {"y": 4, "xhi": 2, "x": 4, "z": 4}
    out = {}
    for name in reversed(order):
        out[name] = flat % sizes[name]
        flat = flat // sizes[name]
    return out


def index_of(where, order):
    sizes = {"y": 4, "xhi": 2, "x": 4, "z": 4}
    at = 0
    for name in order:
        at = at * sizes[name] + where[name]
    return at


def part_size(orders):
    return 256 // GROUP * PACK // len(orders)


def part_row(member, part, orders):
    where = digits_of(member // 2, ("y", "xhi"))
    at = (member % 2) * 8 + index_of(where, orders[part])
    return (part * BLOCKS + at) * part_size(orders)


def shard_row(group, piece, orders):
    where = digits_of(group % SHARDS, ("z", "y", "x"))
    return ((group // SHARDS) * SHARDS + index_of(where, orders[piece])) * PIECE_ROWS[piece]


def here():
    g = lax.axis_index("group")
    m = lax.axis_index("member")
    return {"x": (m // 2) % 2 * 2 + g // 4, "xhi": (m // 2) % 2, "y": m // 4, "z": g % 4, "core": m % 2}


def device(at):
    return (at["x"] % 2 * 4 + at["z"], at["y"] * 4 + at["x"] // 2 * 2 + at["core"])


def toward(at, axis, step):
    there = dict(at)
    if axis == "core":
        there["core"] = 1 - at["core"]
    elif axis == "xhi":
        there["x"] = (at["x"] + 2) % 4
    else:
        there[axis] = (at[axis] + step + 4) % 4
    return device(there)


def next_group(step):
    return ((lax.axis_index("group") + step + 8) % 8, lax.axis_index("member"))


def greet(devices):
    barrier = pltpu.get_barrier_semaphore()
    for there in devices:
        pl.semaphore_signal(barrier, inc=1, device_id=there, device_id_type=MESH)
    pl.semaphore_wait(barrier, len(devices))


class Copies:
    def __init__(self, send, recv, local):
        self.send, self.recv, self.local = send, recv, local
        self.started, self.kept, self.homes = 0, [], 0
        self.now, self.busy, self.flows, self.added, self.gates = 0.0, {}, [], 0, {}

    def to(self, there, src, dst, links, rows):
        copy = pltpu.make_async_remote_copy(
            src_ref=src, dst_ref=dst, send_sem=self.send.at[self.started], recv_sem=self.recv.at[self.started],
            device_id=there, device_id_type=MESH,
        )
        copy.start()
        self.started += 1
        self.kept.append(copy)
        begin = max([self.now] + [self.busy.get(link, 0.0) for link in links])
        end = begin + rows / (CORE_ROWS if links == ("core",) else LINK_ROWS)
        for link in links:
            self.busy[link] = end
        self.now += 0.05
        return copy, end + LATENCY

    def home(self, src, dst):
        copy = pltpu.make_async_copy(src, dst, self.local.at[self.homes])
        copy.start()
        self.homes += 1
        return copy

    def enter(self, name, limit):
        held, waiting = self.gates.setdefault(name, ([], []))
        if len(held) == limit:
            yield waiting
        held.append(None)

    def leave(self, name):
        held, waiting = self.gates[name]
        held.pop()
        if waiting:
            number, flow = waiting.pop(0)
            self.step(number, flow)

    def step(self, number, flow):
        ready = next(flow, None)
        if ready is None:
            return
        if any(ready is waiting for _, waiting in self.gates.values()):
            ready.append((number, flow))
        else:
            self.flows.append((max(r for _, r in ready), number, flow))

    def add(self, flow):
        self.added += 1
        self.step(self.added, flow)

    def run(self, beside=iter(()), cost=0.7):
        while self.flows:
            entry = min(self.flows)
            while entry[0] > self.now + cost and next(beside, None) is not None:
                self.now += cost
            self.flows.remove(entry)
            self.now = max(self.now, entry[0]) + 0.1
            self.step(entry[1], entry[2])
        for _ in beside:
            pass

    def finish(self):
        for copy in self.kept:
            copy.wait_send()


def wait_all(copies):
    for copy, _ in copies:
        copy.wait_recv()


def halves(size):
    first = -(-size // 16) * 8
    return first, size - first


def add_into(dst, at, src, start, size):
    tile = size
    while tile > 256:
        tile = tile // 2 if tile % 16 == 0 else tile // 13
    if tile == size:
        dst[span_of(at, size), :] = dst[span_of(at, size), :] + src[span_of(start, size), :]
        return

    def step(i, carry):
        d = span_of(at + i * tile, tile)
        dst[d, :] = dst[d, :] + src[span_of(start + i * tile, tile), :]
        return carry

    lax.fori_loop(0, size // tile, step, 0)


def both(axis):
    return (axis + "+", axis + "-")


def sum_flow(net, at, src, acc, landing, ring, order, direct, done):
    half = acc.shape[0]
    core = at["core"]
    over = net.to(toward(at, "core", 1), src.at[span_of((1 - core) * half, half)], landing, ("core",), half)
    own = net.home(src.at[span_of(core * half, half)], acc)
    yield [over]
    own.wait()
    wait_all([over])
    add_into(acc, 0, landing, 0, half)
    base, size, used = 0, half, 0
    for level, axis in enumerate(order):
        a = at[axis]
        if axis == "xhi":
            size = size // 2
            src_at = acc.at[span_of(base + (1 - a) * size, size)]
            copies = [net.to(toward(at, axis, 1), src_at, ring.at[pl.ds(used, size)], both("x"), size)]
            yield copies
            wait_all(copies)
            add_into(acc, base + a * size, ring, used, size)
            used += size
        else:
            size = size // RING
            up, down, far = (base + (a + k) % RING * size for k in (1, 3, 2))
            above, below, opposite = (toward(at, axis, k) for k in (1, -1, 2))
            plus, minus = ((link,) for link in both(axis))
            ra, rc, rd = used, used + size, used + 2 * size
            if level >= direct:
                copies = [
                    net.to(opposite, acc.at[span_of(far, size)], ring.at[pl.ds(ra, size)], both(axis), size),
                    net.to(above, acc.at[span_of(up, size)], ring.at[pl.ds(rc, size)], plus, size),
                    net.to(below, acc.at[span_of(down, size)], ring.at[pl.ds(rd, size)], minus, size),
                ]
                yield copies
                wait_all(copies)
                add_into(acc, base + a * size, ring, ra, size)
            else:
                h1, h2 = halves(size)
                yield from net.enter(axis, RINGS_SUM)
                first = net.to(above, acc.at[span_of(far, h1)], ring.at[pl.ds(ra, h1)], plus, h1)
                second = net.to(below, acc.at[span_of(far + h1, h2)], ring.at[pl.ds(ra + h1, h2)], minus, h2)
                c2 = net.to(above, acc.at[span_of(up + h1, h2)], ring.at[pl.ds(rc + h1, h2)], plus, h2)
                d1 = net.to(below, acc.at[span_of(down, h1)], ring.at[pl.ds(rd, h1)], minus, h1)
                yield [first, second]
                wait_all([first])
                add_into(acc, up, ring, ra, h1)
                c1 = net.to(above, acc.at[span_of(up, h1)], ring.at[pl.ds(rc, h1)], plus, h1)
                wait_all([second])
                add_into(acc, down + h1, ring, ra + h1, h2)
                d2 = net.to(below, acc.at[span_of(down + h1, h2)], ring.at[pl.ds(rd + h1, h2)], minus, h2)
                copies = [c2, d1, c1, d2]
                yield copies
                wait_all(copies)
                net.leave(axis)
            add_into(acc, base + a * size, ring, rc, size)
            add_into(acc, base + a * size, ring, rd, size)
            used += 3 * size
        base = base + a * size
    yield from done(base)


def spread_flow(net, at, buf, offset, rows, order, direct, arrived):
    radix = {"xhi": 2, "x": 4, "y": 4, "z": 4}
    total = rows
    for name in order:
        total *= radix[name]
    core = at["core"]
    bases = [offset + core * total]
    strides = []
    size = total
    for name in order:
        size = size // radix[name]
        strides.append(size)
        bases.append(bases[-1] + at[name] * size)
    sibling = toward(at, "core", 1)
    shared = []

    def share(start, size):
        there = span_of(start, size)
        copy = net.to(sibling, buf.at[there], buf.at[there], ("core",), size)
        shared.append((copy, start + (1 - 2 * core) * total, size))

    def send(there, start, size, links):
        part = span_of(start, size)
        return net.to(there, buf.at[part], buf.at[part], links, size)

    for level in reversed(range(len(order))):
        name, size, region = order[level], strides[level], bases[level]
        a = at[name]
        last = level == 0
        if name == "xhi":
            other = region + (1 - a) * size
            copies = [send(toward(at, name, 1), region + a * size, size, both("x"))]
            if last:
                share(region + a * size, size)
                arrived(region + a * size, size)
            yield copies
            wait_all(copies)
            if last:
                share(other, size)
                arrived(other, size)
        else:
            h1, h2 = halves(size)
            own, up, down, far = (region + (a + k) % RING * size for k in (0, 1, 3, 2))
            above, below, opposite = (toward(at, name, k) for k in (1, -1, 2))
            plus, minus = ((link,) for link in both(name))
            if level < direct:
                yield from net.enter(name, RINGS_IN)
            e = send(above, own, size, plus)
            f = send(below, own, size, minus)
            if last:
                share(own, size)
            if level >= direct:
                g = send(opposite, own, size, both(name))
                yield [e, f, g]
                wait_all([e, f, g])
            else:
                if last:
                    arrived(own, size)
                yield [e, f]
                wait_all([e])
                g = send(above, down, h1, plus)
                wait_all([f])
                h = send(below, up + h1, h2, minus)
                if last:
                    share(down, size)
                    share(up, size)
                    arrived(down, size)
                    arrived(up, size)
                yield [g, h]
                wait_all([g, h])
                net.leave(name)
                if last:
                    share(far, size)
                    arrived(far, size)
    for copy, start, size in shared:
        yield [copy]
        wait_all([copy])
        arrived(start, size)


def fetch_kernel(rid_ref, ent_ref, rel_hbm, slab_hbm, rows_hbm, own, packed, slab, rel, rel_rows, got, send, recv, local):
    at = here()
    m = lax.axis_index("member")
    greet(
        [toward(at, "y", 1), toward(at, "y", -1), toward(at, "xhi", 1), toward(at, "core", 1), next_group(1), next_group(-1)]
    )
    net = Copies(send, recv, local)
    entry = net.home(rel_hbm, rel)
    for j in range(8):
        rows = slice(j * GROUP, (j + 1) * GROUP)
        for c in range(3):
            own[pl.ds(j * PACK + c * GROUP, GROUP), :] = ent_ref[rows, c * LANES : (c + 1) * LANES]
        own[pl.ds(j * PACK + 96, 8), :] = pack_tail(ent_ref[rows, 3 * LANES : 4 * LANES])

    writes = []
    parts = len(PART_IN)
    size = part_size(PART_IN)
    groups = size // PACK

    def flow(part):
        start = part * BLOCKS * size
        mine = span_of(part_row(m, part, PART_IN), size)
        yield from net.enter("shift", SHIFTS)
        shift = net.to(next_group(-1), own.at[pl.ds(part * size, size)], packed.at[mine], ("z-",), size)
        yield [shift]
        wait_all([shift])
        net.leave("shift")

        def arrived(begin, rows):
            def block(i, carry):
                source = begin + i * size
                flat = (source - start) // size
                where = digits_of(flat % 8, PART_IN[part])
                member = (where["y"] * 2 + where["xhi"]) * 2 + flat // 8
                for k in range(groups):
                    base = source + k * PACK
                    out = (member * 256 + (part * groups + k) * GROUP) * CHUNKS
                    out = pl.multiple_of(out, 128)
                    for c in range(3):
                        slab[pl.ds(out + c, GROUP, stride=CHUNKS), :] = packed[span_of(base + c * GROUP, GROUP), :]
                    slab[pl.ds(out + 3, GROUP, stride=CHUNKS), :] = unpack_tail(packed[span_of(base + 96, 8), :])
                return carry

            lax.fori_loop(0, rows // size, block, 0)
            net.now += 0.04 * rows / PACK

        yield from spread_flow(net, at, packed, start, size, PART_IN[part], 9, arrived)
        view = (BLOCKS, parts, groups * GROUP * CHUNKS, LANES)
        writes.append(net.home(slab.reshape(view).at[:, part], slab_hbm.reshape(view).at[:, part]))

    def gather():
        tile = 256
        width, total = rel.shape
        entry.wait()
        for t in range(total // (4 * tile)):
            def convert(i, carry):
                k = t * 4 + i
                part = span_of(k * tile, tile, tile)
                wide = jnp.concatenate([rel[:, part], jnp.zeros((CHUNKS * LANES - width, tile), F32)], axis=0)
                rel_rows[part] = wide.T.reshape(tile, CHUNKS, LANES)
                return carry

            lax.fori_loop(0, 4, convert, 0)
            yield True
        edges = got.shape[0] // CHUNKS
        segment, unroll = 512, 16
        for t in range(edges // segment):
            def step(b, carry):
                for u in range(unroll):
                    j = t * segment + b * unroll + u
                    got[row(j), :] = rel_rows[rid_ref[j]]
                return carry

            lax.fori_loop(0, segment // unroll, step, 0)
            part = pl.ds(t * segment * CHUNKS, segment * CHUNKS)
            writes.append(net.home(got.at[part], rows_hbm.at[part]))
            yield True

    for part in range(parts):
        net.add(flow(part))
    net.run(gather())
    for write in writes:
        write.wait()
    net.finish()


def fetch(rid, ent, relations):
    edges = rid.shape[0]
    width, count = relations.shape
    rows = ent.shape[0] * BLOCKS
    anym = pl.BlockSpec(memory_space=pl.ANY)
    return pl.pallas_call(
        fetch_kernel,
        out_shape=(
            jax.ShapeDtypeStruct((rows * CHUNKS, LANES), F32),
            jax.ShapeDtypeStruct((edges * CHUNKS, LANES), F32),
        ),
        in_specs=[pl.BlockSpec(memory_space=pltpu.SMEM), pl.BlockSpec(memory_space=pltpu.VMEM), anym],
        out_specs=(anym, anym),
        scratch_shapes=[
            pltpu.VMEM((256 // GROUP * PACK, LANES), F32),
            pltpu.VMEM((rows // GROUP * PACK, LANES), F32),
            pltpu.VMEM((rows * CHUNKS, LANES), F32),
            pltpu.VMEM((width, count), F32),
            pltpu.VMEM((count, CHUNKS, LANES), F32),
            pltpu.VMEM((edges * CHUNKS, LANES), F32),
            pltpu.SemaphoreType.DMA((128,)),
            pltpu.SemaphoreType.DMA((128,)),
            pltpu.SemaphoreType.DMA((24,)),
        ],
        compiler_params=pltpu.CompilerParams(vmem_limit_bytes=56 * 2**20, collective_id=1, has_side_effects=True),
        name="fetch",
    )(rid, ent, relations)


def bucket_kernel(
    spans, unroll,
    cnt_ref, ridx_ref, nidx_ref, rid_ref, lhs_ref, ent_ref, rel_ref, slab_hbm,
    right_hbm, rel0_hbm, rel1_hbm, rel2_hbm, left_ref,
    slab, racc, nacc, relacc, rvec, nvec, gr, gn, grel, sem,
):
    s = pl.program_id(0)
    total = racc.shape[0]

    @pl.when(s == 0)
    def _():
        load = pltpu.make_async_copy(slab_hbm, slab.at[pl.ds(0, total)], sem.at[0])
        load.start()
        slab[pl.ds(total, 8), :] = jnp.zeros((8, LANES), F32)
        racc[...] = jnp.zeros_like(racc)
        nacc[...] = jnp.zeros_like(nacc)
        relacc[...] = jnp.zeros_like(relacc)
        left_ref[...] = jnp.zeros_like(left_ref)
        load.wait()

    def scatter(j, base):
        rel = row(rid_ref[base + j])
        rgt = row(ridx_ref[base + j])
        neg = row(nidx_ref[base + j])
        own = row(j)
        relacc[rel, :] = relacc[rel, :] + grel[own, :]
        racc[rgt, :] = racc[rgt, :] + gr[own, :]
        nacc[neg, :] = nacc[neg, :] + gn[own, :]

    def gather(j, base):
        own = row(j)
        rvec[own, :] = slab[row(ridx_ref[base + j]), :]
        nvec[own, :] = slab[row(nidx_ref[base + j]), :]

    behind = (s - 1) * SPAN
    ahead = s * SPAN

    def rows_loop(*works):
        def step(b, carry):
            for u in range(unroll):
                for work, base in works:
                    work(b * unroll + u, base)
            return carry

        lax.fori_loop(0, SPAN // unroll, step, 0)

    @pl.when(s == 0)
    def _():
        rows_loop((gather, ahead))

    @pl.when((s > 0) & (s < spans))
    def _():
        rows_loop((gather, ahead), (scatter, behind))

    @pl.when(s == spans)
    def _():
        rows_loop((scatter, behind))

    @pl.when(s < spans)
    def _():
        hot = (lax.broadcasted_iota(jnp.int32, (ent_ref.shape[0], SPAN), 0) == lhs_ref[0]).astype(F32).astype(BF16)
        eh, el = split(ent_ref[...])
        first = ((0,), (0,))
        last = ((1,), (1,))
        inner = ((1,), (0,))
        left = dot2(jnp.concatenate([hot, hot], axis=0), jnp.concatenate([eh, el], axis=0), first)
        rel = read_rows(rel_ref, SPAN)
        query = left * rel
        live = (s * SPAN + lax.broadcasted_iota(jnp.int32, (SPAN, 1), 0) < cnt_ref[0]).astype(F32)
        q = split(query)
        n = split(read_rows(nvec, SPAN))
        neg = dot3(q, n, last)
        dneg = split(jax.nn.sigmoid(neg) * (live / NEG))
        right = read_rows(rvec, SPAN)
        pos = jnp.sum(query * right, axis=1, keepdims=True)
        dpos = -jax.nn.sigmoid(-pos) * live
        write_rows(gr, dpos * query, SPAN)
        write_rows(gn, dot3(dneg, q, first), SPAN)
        grad_query = dpos * right + dot3(dneg, n, inner)
        write_rows(grel, grad_query * left, SPAN)
        gl = jnp.concatenate(split(grad_query * rel), axis=0)
        left_ref[...] += dot2(jnp.concatenate([hot, hot], axis=1), gl, inner)

    @pl.when(s == spans)
    def _():
        def right_member(m, carry):
            for part in range(len(PART_SUM)):
                for k in range(256 // GROUP // len(PART_SUM)):
                    at = part * (256 // GROUP // len(PART_SUM)) + k
                    src = pl.multiple_of((m * 256 + at * GROUP) * CHUNKS, 128)
                    out = part_row(m, part, PART_SUM) + k * PACK
                    planes = [
                        racc[pl.ds(src + c, GROUP, stride=CHUNKS), :] + nacc[pl.ds(src + c, GROUP, stride=CHUNKS), :]
                        for c in range(CHUNKS)
                    ]
                    for c in range(3):
                        slab[span_of(out + c * GROUP, GROUP), :] = planes[c]
                    slab[span_of(out + 96, 8), :] = pack_tail(planes[3])
            return carry

        lax.fori_loop(0, BLOCKS, right_member, 0)
        out = pltpu.make_async_copy(slab.at[pl.ds(0, right_hbm.shape[0])], right_hbm, sem.at[0])
        out.start()
        begins = (0, 2 * SHARDS * PIECE_ROWS[0], 2 * SHARDS * (PIECE_ROWS[0] + PIECE_ROWS[1]))

        def shards(i, carry):
            for k in range(4):
                group = i * 4 + k
                src = pl.multiple_of(group * GROUP * CHUNKS, 128)
                at = [b + shard_row(group, p, PIECE_SUM) for p, b in enumerate(begins)]
                for c in range(3):
                    nacc[span_of(at[c], GROUP), :] = relacc[pl.ds(src + c, GROUP, stride=CHUNKS), :]
                nacc[span_of(at[2] + GROUP, 8), :] = pack_tail(relacc[pl.ds(src + 3, GROUP, stride=CHUNKS), :])
            return carry

        lax.fori_loop(0, 2 * SHARDS // 4, shards, 0)
        copies = [
            pltpu.make_async_copy(nacc.at[pl.ds(b, ref.shape[0])], ref, sem.at[1 + p])
            for p, (b, ref) in enumerate(zip(begins, (rel0_hbm, rel1_hbm, rel2_hbm)))
        ]
        for copy in copies:
            copy.start()
        for copy in copies:
            copy.wait()
        out.wait()


def bucket(counts, ridx, nidx, rid, lhs, ent, rel_rows, slab):
    edges = rid.shape[0]
    spans = edges // SPAN
    total = slab.shape[0]
    smem = pl.BlockSpec(memory_space=pltpu.SMEM)
    anym = pl.BlockSpec(memory_space=pl.ANY)
    vm = lambda r: pltpu.VMEM((r, LANES), F32)
    span_rows = SPAN * CHUNKS
    return pl.pallas_call(
        functools.partial(bucket_kernel, spans, 16),
        grid=(spans + 1,),
        out_shape=(
            jax.ShapeDtypeStruct((BLOCKS * 256 // GROUP * PACK, LANES), F32),
            *(jax.ShapeDtypeStruct((2 * SHARDS * r, LANES), F32) for r in PIECE_ROWS),
            jax.ShapeDtypeStruct(ent.shape, F32),
        ),
        in_specs=[
            smem, smem, smem, smem,
            pl.BlockSpec((1, 1, SPAN), lambda s: (jnp.minimum(s, spans - 1), 0, 0)),
            pl.BlockSpec(ent.shape, lambda s: (0, 0)),
            pl.BlockSpec((span_rows, LANES), lambda s: (jnp.minimum(s, spans - 1), 0)),
            anym,
        ],
        out_specs=(anym, anym, anym, anym, pl.BlockSpec(ent.shape, lambda s: (0, 0))),
        scratch_shapes=[
            vm(total + 8), vm(total), vm(total + 8), vm(total),
            vm(span_rows), vm(span_rows), vm(span_rows), vm(span_rows), vm(span_rows),
            pltpu.SemaphoreType.DMA((4,)),
        ],
        compiler_params=pltpu.CompilerParams(vmem_limit_bytes=58 * 2**20),
        name="bucket",
    )(counts, ridx, nidx, rid, lhs, ent, rel_rows, slab)


def ring_rows(half, order):
    size, used = half, 0
    for name in order:
        size = size // (2 if name == "xhi" else RING)
        used += size if name == "xhi" else 3 * size
    return used


def reduce_kernel(
    width,
    states_ref, rel_hbm, right_hbm, rel0_hbm, rel1_hbm, rel2_hbm,
    back_hbm, new0_hbm, new1_hbm, new2_hbm,
    *scratch,
):
    scratch = list(scratch)
    take = lambda n: [scratch.pop(0) for _ in range(n)]
    parts = len(PART_SUM)
    racc, rland, rring = take(parts), take(parts), take(parts)
    pacc, pland, pring, news = take(3), take(3), take(3), take(3)
    back, block, shard, send, recv, local = scratch
    at = here()
    mine = (at["core"] * SHARDS + index_of(at, ("z", "y", "x"))) * GROUP
    inside = pl.ds(pl.multiple_of(mine % LANES, GROUP), GROUP)
    lanes = pl.ds(pl.multiple_of(mine // LANES * LANES, LANES), LANES)
    greet(
        [toward(at, axis, step) for axis in ("x", "y", "z") for step in (1, -1, 2)]
        + [toward(at, "core", 1), next_group(1), next_group(-1)]
    )
    net = Copies(send, recv, local)
    entry = net.home(rel_hbm.at[:, lanes], block)
    size = part_size(PART_SUM)
    region = BLOCKS * size
    backs = []
    bases = {}

    def right_flow(part):
        def done(base):
            mine = pl.ds(part * size, size)
            src = racc[part].at[span_of(base, size)]
            copies = [net.to(next_group(1), src, back.at[mine], ("z+",), size)]
            yield copies
            wait_all(copies)
            backs.append(net.home(back.at[mine], back_hbm.at[mine]))

        return sum_flow(
            net, at, right_hbm.at[pl.ds(part * region, region)], racc[part], rland[part], rring[part],
            PART_SUM[part], 9, done,
        )

    def piece_flow(piece):
        def done(base):
            bases[piece] = base
            if len(bases) == 3:
                update()
            yield from ()

        src = (rel0_hbm, rel1_hbm, rel2_hbm)[piece]
        return sum_flow(net, at, src, pacc[piece], pland[piece], pring[piece], PIECE_SUM[piece], 1, done)

    def update():
        planes = [pacc[p][span_of(bases[p], GROUP), :] for p in range(3)]
        planes.append(unpack_tail(pacc[2][span_of(bases[2] + GROUP, 8), :]))
        squares = planes[0] * planes[0]
        for plane in planes[1:]:
            squares = squares + plane * plane
        entry.wait()
        height = CHUNKS * LANES
        wide = jnp.concatenate([block[...], jnp.zeros((height - width, LANES), F32)], axis=0)
        old = jnp.broadcast_to(states_ref[:, lanes], (LANES, LANES)).T
        shard[:, 0:height] = wide.T
        shard[:, height : height + LANES] = old
        state = shard[inside, height : height + 1] + jnp.sum(squares, axis=1, keepdims=True) / width
        root = jnp.sqrt(state)
        fresh = [shard[inside, c * LANES : (c + 1) * LANES] - STEP_SIZE * planes[c] / root for c in range(CHUNKS)]
        tail = pack_tail(fresh[3])
        lane = lax.broadcasted_iota(jnp.int32, (8, LANES), 1)
        for g in range(GROUP // 8):
            tail = jnp.where(lane == LANES // 2 + g, state[8 * g : 8 * g + 8], tail)
        outs = (new0_hbm, new1_hbm, new2_hbm)
        net.now += 0.5
        for p in range(3):
            place = (at["core"] * SHARDS + index_of(at, PIECE_OUT[p])) * PIECE_ROWS[p]
            news[p][span_of(place, GROUP), :] = fresh[p]
            if p == 2:
                news[p][span_of(place + GROUP, 8), :] = tail

            def arrived(start, size, p=p):
                rows = PIECE_ROWS[p]
                half, k = start // (SHARDS * rows), start // (16 * rows) % RING
                src = news[p].at[span_of(start, size)].reshape(4, 4, rows, LANES)
                dst = (outs[p].at[half, k], outs[p].at[half, :, :, k], outs[p].at[half, :, k])[p]
                backs.append(net.home(src, dst))

            net.add(spread_flow(net, at, news[p], 0, PIECE_ROWS[p], PIECE_OUT[p], 1, arrived))

    for k in range(max(3, parts)):
        if k < 3:
            net.add(piece_flow(k))
        if k < parts:
            net.add(right_flow(k))
    net.run()
    for copy in backs:
        copy.wait()
    net.finish()


def reduce(width, states, relations, right, pieces):
    anym = pl.BlockSpec(memory_space=pl.ANY)
    vmem = pl.BlockSpec(memory_space=pltpu.VMEM)
    vm = lambda r: pltpu.VMEM((r, LANES), F32)
    parts = len(PART_SUM)
    half = BLOCKS // 2 * part_size(PART_SUM)
    return pl.pallas_call(
        functools.partial(reduce_kernel, width),
        out_shape=(
            jax.ShapeDtypeStruct((256 // GROUP * PACK, LANES), F32),
            *(jax.ShapeDtypeStruct((2, 4, 4, 4, r, LANES), F32) for r in PIECE_ROWS),
        ),
        in_specs=[vmem, anym, anym, anym, anym, anym],
        out_specs=(anym,) * 4,
        scratch_shapes=[
            *(vm(half) for _ in range(parts)),
            *(vm(half) for _ in range(parts)),
            *(vm(ring_rows(half, PART_SUM[p])) for p in range(parts)),
            *(vm(SHARDS * r) for r in PIECE_ROWS),
            *(vm(SHARDS * r) for r in PIECE_ROWS),
            *(vm(ring_rows(SHARDS * r, PIECE_SUM[p])) for p, r in enumerate(PIECE_ROWS)),
            *(vm(2 * SHARDS * r) for r in PIECE_ROWS),
            vm(256 // GROUP * PACK),
            pltpu.VMEM((width, LANES), F32),
            pltpu.VMEM((LANES, (CHUNKS + 1) * LANES), F32),
            pltpu.SemaphoreType.DMA((192,)),
            pltpu.SemaphoreType.DMA((192,)),
            pltpu.SemaphoreType.DMA((64,)),
        ],
        compiler_params=pltpu.CompilerParams(vmem_limit_bytes=56 * 2**20, collective_id=2, has_side_effects=True),
        name="reduce",
    )(states, relations, right, *pieces)


def finish_kernel(
    width, left_ref, back_ref, ent_ref, state_ref, new0, new1, new2, rel_ref, rel_state_ref, ent_out, state_out
):
    s = pl.program_id(0)
    count = rel_ref.shape[1]
    lane = lax.broadcasted_iota(jnp.int32, (8, LANES), 1)
    for k in range(count // LANES):
        out = pl.ds(k * LANES, LANES)
        groups = range(k * 4, k * 4 + 4)
        for c, ref in enumerate((new0, new1, new2)):
            r = PIECE_ROWS[c]
            plane = jnp.concatenate([ref[g * r : g * r + GROUP, :] for g in groups], axis=0)
            rel_ref[c * LANES : (c + 1) * LANES, out] = plane.T
        r = PIECE_ROWS[2]
        tails = []
        for group in groups:
            packed = new2[group * r + GROUP : (group + 1) * r, :]
            for g in range(GROUP // 8):
                state = pltpu.roll(packed, LANES // 2 + TAIL - g, 1)
                values = packed if g == 0 else pltpu.roll(packed, LANES - TAIL * g, 1)
                tails.append(jnp.where(lane < TAIL, values, state))
        tail = jnp.concatenate(tails, axis=0).T
        rel_ref[3 * LANES : width, out] = tail[: width - 3 * LANES]
        rel_state_ref[:, out] = tail[TAIL : TAIL + 1]

    @pl.when(s == 0)
    def _():
        for i in range(2):
            part = slice(i * LANES, (i + 1) * LANES)
            wide = []
            for j in range(4 * i, 4 * i + 4):
                planes = [back_ref[pl.ds(j * PACK + c * GROUP, GROUP), :] for c in range(3)]
                planes.append(unpack_tail(back_ref[pl.ds(j * PACK + 96, 8), :]))
                wide.append(jnp.concatenate(planes, axis=1))
            grad = (left_ref[part, :] + jnp.concatenate(wide, axis=0)).T[:width]
            state = state_ref[:, part] + jnp.sum(grad * grad, axis=0, keepdims=True) / width
            state_out[:, part] = state
            ent_out[:, part] = ent_ref[:, part] - STEP_SIZE * grad / jnp.sqrt(state)


def finish(width, left, back, ent, ent_state, news, count):
    steps = 4
    full = lambda a: pl.BlockSpec(a.shape, lambda s: (0, 0))
    rows = ent.shape[1]
    return pl.pallas_call(
        functools.partial(finish_kernel, width),
        grid=(steps,),
        out_shape=(
            jax.ShapeDtypeStruct((width, count), F32),
            jax.ShapeDtypeStruct((1, count), F32),
            jax.ShapeDtypeStruct((width, rows), F32),
            jax.ShapeDtypeStruct((1, rows), F32),
        ),
        in_specs=[full(a) for a in (left, back, ent, ent_state)]
        + [pl.BlockSpec((2 * SHARDS // steps * r, LANES), lambda s: (s, 0)) for r in PIECE_ROWS],
        out_specs=(
            pl.BlockSpec((width, count // steps), lambda s: (0, s)),
            pl.BlockSpec((1, count // steps), lambda s: (0, s)),
            pl.BlockSpec((width, rows), lambda s: (0, 0)),
            pl.BlockSpec((1, rows), lambda s: (0, 0)),
        ),
        compiler_params=pltpu.CompilerParams(vmem_limit_bytes=60 * 2**20),
        name="finish",
    )(left, back, ent, ent_state, *news)


def on_device(
    entities, ent_state, relations, rel_state, lhs_rows, rhs_owner, rhs_off, neg_owner, neg_off, rel_ids, counts
):
    shard = entities[0]
    rows, width = shard.shape
    wide = CHUNKS * LANES
    padded = jnp.pad(shard, ((0, 0), (0, wide - width)))
    edges = lhs_rows.shape[1]
    spans = edges // SPAN
    ridx = rhs_owner[0, :, 0] * rows + rhs_off[0]
    nidx = (neg_owner[0, :, 0] * rows + neg_off[0]).reshape(spans, NEG)
    nidx = jnp.pad(nidx, ((0, 0), (0, SPAN - NEG)), constant_values=rows * BLOCKS).reshape(edges)
    rid = rel_ids[0]
    slab, rel_rows = fetch(rid, padded, relations.T)
    right, *pieces, left = bucket(counts[0], ridx, nidx, rid, lhs_rows.reshape(spans, 1, SPAN), padded, rel_rows, slab)
    back, *news = reduce(width, rel_state[None], relations.T, right, pieces)
    rel_new, states, new_shard, new_state = finish(
        width, left, back, shard.T, ent_state, [n.reshape(-1, LANES) for n in news], relations.shape[0]
    )
    return (new_shard.T[None], new_state, rel_new.T, states.reshape(-1))


def solution(mesh):
    in_specs = (
        P("group", "member", None), P("group", "member"), P(), P(),
        P("group", "member"), P("group", "member", None), P("group", "member"),
        P("group", "member", None), P("group", "member"), P("group", "member"), P("group", "member"),
    )
    out_specs = (P("group", "member", None), P("group", "member"), P(), P())
    return jax.shard_map(on_device, mesh=mesh, in_specs=in_specs, out_specs=out_specs, check_vma=False)
```

```python
import functools
import jax
import jax.numpy as jnp
from jax import lax
from jax.experimental import pallas as pl
from jax.experimental.pallas import tpu as pltpu
from jax.sharding import PartitionSpec as P

SPAN = 512
NEG = 500
STEP_SIZE = 0.1
LANES = 128
F32 = jnp.float32
BF16 = jnp.bfloat16
MESH = pl.DeviceIdType.MESH

CHUNKS = 4
TAIL = 16
GROUP = 32
PACK = 104
BLOCKS = 16
RING = 4
Y_FIRST = ("y", "xhi")
X_FIRST = ("xhi", "y")
PART_IN = (X_FIRST, Y_FIRST) * 3 + (Y_FIRST, Y_FIRST)
PART_SUM = (X_FIRST, Y_FIRST, Y_FIRST, Y_FIRST) * 2
PIECE_ROWS = (32, 32, 40)
PIECE_SUM = (("z", "y", "x"), ("x", "z", "y"), ("z", "x", "y"))
PIECE_OUT = (("z", "y", "x"), ("x", "z", "y"), ("y", "z", "x"))
SHARDS = 64
SHIFTS = 8
RINGS_IN = 8
RINGS_SUM = 2
LINK_ROWS = 70.0
CORE_ROWS = 1000.0
LATENCY = 4.0


def split(x):
    hi = x.astype(BF16)
    return hi, (x - hi.astype(F32)).astype(BF16)


def dot2(a, b, dims):
    return lax.dot_general(a, b, (dims, ((), ())), preferred_element_type=F32)


def dot3(a, b, dims):
    (ah, al), (bh, bl) = a, b
    (ka,), (kb,) = dims
    return dot2(jnp.concatenate([ah, ah, al], axis=ka), jnp.concatenate([bh, bl, bh], axis=kb), dims)


def row(i):
    return pl.ds(pl.multiple_of(i * CHUNKS, CHUNKS), CHUNKS)


def span_of(start, size, tile=8):
    return pl.ds(start if isinstance(start, int) else pl.multiple_of(start, tile), size)


def read_rows(ref, rows):
    return jnp.concatenate([ref[pl.ds(c, rows, stride=CHUNKS), :] for c in range(CHUNKS)], axis=1)


def write_rows(ref, value, rows):
    for c in range(CHUNKS):
        ref[pl.ds(c, rows, stride=CHUNKS), :] = value[:, c * LANES : (c + 1) * LANES]


def pack_tail(tail):
    packed = tail[0:8]
    for g in range(1, GROUP // 8):
        packed = packed + pltpu.roll(tail[8 * g : 8 * g + 8], TAIL * g, 1)
    return packed


def unpack_tail(packed):
    kept = lax.broadcasted_iota(jnp.int32, (8, LANES), 1) < TAIL
    parts = [jnp.where(kept, packed if g == 0 else pltpu.roll(packed, LANES - TAIL * g, 1), 0.0) for g in range(GROUP // 8)]
    return jnp.concatenate(parts, axis=0)


def digits_of(flat, order):
    sizes = {"y": 4, "xhi": 2, "x": 4, "z": 4}
    out = {}
    for name in reversed(order):
        out[name] = flat % sizes[name]
        flat = flat // sizes[name]
    return out


def index_of(where, order):
    sizes = {"y": 4, "xhi": 2, "x": 4, "z": 4}
    at = 0
    for name in order:
        at = at * sizes[name] + where[name]
    return at


def part_size(orders):
    return 256 // GROUP * PACK // len(orders)


def part_row(member, part, orders):
    where = digits_of(member // 2, ("y", "xhi"))
    at = (member % 2) * 8 + index_of(where, orders[part])
    return (part * BLOCKS + at) * part_size(orders)


def shard_row(group, piece, orders):
    where = digits_of(group % SHARDS, ("z", "y", "x"))
    return ((group // SHARDS) * SHARDS + index_of(where, orders[piece])) * PIECE_ROWS[piece]


def here():
    g = lax.axis_index("group")
    m = lax.axis_index("member")
    return {"x": (m // 2) % 2 * 2 + g // 4, "xhi": (m // 2) % 2, "y": m // 4, "z": g % 4, "core": m % 2}


def device(at):
    return (at["x"] % 2 * 4 + at["z"], at["y"] * 4 + at["x"] // 2 * 2 + at["core"])


def toward(at, axis, step):
    there = dict(at)
    if axis == "core":
        there["core"] = 1 - at["core"]
    elif axis == "xhi":
        there["x"] = (at["x"] + 2) % 4
    else:
        there[axis] = (at[axis] + step + 4) % 4
    return device(there)


def next_group(step):
    return ((lax.axis_index("group") + step + 8) % 8, lax.axis_index("member"))


def greet(devices):
    barrier = pltpu.get_barrier_semaphore()
    for there in devices:
        pl.semaphore_signal(barrier, inc=1, device_id=there, device_id_type=MESH)
    pl.semaphore_wait(barrier, len(devices))


class Copies:
    def __init__(self, send, recv, local):
        self.send, self.recv, self.local = send, recv, local
        self.started, self.kept, self.homes = 0, [], 0
        self.now, self.busy, self.flows, self.added, self.gates = 0.0, {}, [], 0, {}

    def to(self, there, src, dst, links, rows):
        copy = pltpu.make_async_remote_copy(
            src_ref=src, dst_ref=dst, send_sem=self.send.at[self.started], recv_sem=self.recv.at[self.started],
            device_id=there, device_id_type=MESH,
        )
        copy.start()
        self.started += 1
        self.kept.append(copy)
        begin = max([self.now] + [self.busy.get(link, 0.0) for link in links])
        end = begin + rows / (CORE_ROWS if links == ("core",) else LINK_ROWS)
        for link in links:
            self.busy[link] = end
        self.now += 0.05
        return copy, end + LATENCY

    def home(self, src, dst):
        copy = pltpu.make_async_copy(src, dst, self.local.at[self.homes])
        copy.start()
        self.homes += 1
        return copy

    def enter(self, name, limit):
        held, waiting = self.gates.setdefault(name, ([], []))
        if len(held) == limit:
            yield waiting
        held.append(None)

    def leave(self, name):
        held, waiting = self.gates[name]
        held.pop()
        if waiting:
            number, flow = waiting.pop(0)
            self.step(number, flow)

    def step(self, number, flow):
        ready = next(flow, None)
        if ready is None:
            return
        if any(ready is waiting for _, waiting in self.gates.values()):
            ready.append((number, flow))
        else:
            self.flows.append((max(r for _, r in ready), number, flow))

    def add(self, flow):
        self.added += 1
        self.step(self.added, flow)

    def run(self, beside=iter(()), cost=0.7):
        while self.flows:
            entry = min(self.flows)
            while entry[0] > self.now + cost and next(beside, None) is not None:
                self.now += cost
            self.flows.remove(entry)
            self.now = max(self.now, entry[0]) + 0.1
            self.step(entry[1], entry[2])
        for _ in beside:
            pass

    def finish(self):
        for copy in self.kept:
            copy.wait_send()


def wait_all(copies):
    for copy, _ in copies:
        copy.wait_recv()


def halves(size):
    first = -(-size // 16) * 8
    return first, size - first


def add_into(dst, at, src, start, size):
    tile = size
    while tile > 256:
        tile = tile // 2 if tile % 16 == 0 else tile // 13
    if tile == size:
        dst[span_of(at, size), :] = dst[span_of(at, size), :] + src[span_of(start, size), :]
        return

    def step(i, carry):
        d = span_of(at + i * tile, tile)
        dst[d, :] = dst[d, :] + src[span_of(start + i * tile, tile), :]
        return carry

    lax.fori_loop(0, size // tile, step, 0)


def both(axis):
    return (axis + "+", axis + "-")


def sum_flow(net, at, src, acc, landing, ring, order, direct, done):
    half = acc.shape[0]
    core = at["core"]
    over = net.to(toward(at, "core", 1), src.at[span_of((1 - core) * half, half)], landing, ("core",), half)
    own = net.home(src.at[span_of(core * half, half)], acc)
    yield [over]
    own.wait()
    wait_all([over])
    add_into(acc, 0, landing, 0, half)
    base, size, used = 0, half, 0
    for level, axis in enumerate(order):
        a = at[axis]
        if axis == "xhi":
            size = size // 2
            src_at = acc.at[span_of(base + (1 - a) * size, size)]
            copies = [net.to(toward(at, axis, 1), src_at, ring.at[pl.ds(used, size)], both("x"), size)]
            yield copies
            wait_all(copies)
            add_into(acc, base + a * size, ring, used, size)
            used += size
        else:
            size = size // RING
            up, down, far = (base + (a + k) % RING * size for k in (1, 3, 2))
            above, below, opposite = (toward(at, axis, k) for k in (1, -1, 2))
            plus, minus = ((link,) for link in both(axis))
            ra, rc, rd = used, used + size, used + 2 * size
            if level >= direct:
                copies = [
                    net.to(opposite, acc.at[span_of(far, size)], ring.at[pl.ds(ra, size)], both(axis), size),
                    net.to(above, acc.at[span_of(up, size)], ring.at[pl.ds(rc, size)], plus, size),
                    net.to(below, acc.at[span_of(down, size)], ring.at[pl.ds(rd, size)], minus, size),
                ]
                yield copies
                wait_all(copies)
                add_into(acc, base + a * size, ring, ra, size)
            else:
                h1, h2 = halves(size)
                yield from net.enter(axis, RINGS_SUM)
                first = net.to(above, acc.at[span_of(far, h1)], ring.at[pl.ds(ra, h1)], plus, h1)
                second = net.to(below, acc.at[span_of(far + h1, h2)], ring.at[pl.ds(ra + h1, h2)], minus, h2)
                c2 = net.to(above, acc.at[span_of(up + h1, h2)], ring.at[pl.ds(rc + h1, h2)], plus, h2)
                d1 = net.to(below, acc.at[span_of(down, h1)], ring.at[pl.ds(rd, h1)], minus, h1)
                yield [first, second]
                wait_all([first])
                add_into(acc, up, ring, ra, h1)
                c1 = net.to(above, acc.at[span_of(up, h1)], ring.at[pl.ds(rc, h1)], plus, h1)
                wait_all([second])
                add_into(acc, down + h1, ring, ra + h1, h2)
                d2 = net.to(below, acc.at[span_of(down + h1, h2)], ring.at[pl.ds(rd + h1, h2)], minus, h2)
                copies = [c2, d1, c1, d2]
                yield copies
                wait_all(copies)
                net.leave(axis)
            add_into(acc, base + a * size, ring, rc, size)
            add_into(acc, base + a * size, ring, rd, size)
            used += 3 * size
        base = base + a * size
    yield from done(base)


def spread_flow(net, at, buf, offset, rows, order, direct, arrived):
    radix = {"xhi": 2, "x": 4, "y": 4, "z": 4}
    total = rows
    for name in order:
        total *= radix[name]
    core = at["core"]
    bases = [offset + core * total]
    strides = []
    size = total
    for name in order:
        size = size // radix[name]
        strides.append(size)
        bases.append(bases[-1] + at[name] * size)
    sibling = toward(at, "core", 1)
    shared = []

    def share(start, size):
        there = span_of(start, size)
        copy = net.to(sibling, buf.at[there], buf.at[there], ("core",), size)
        shared.append((copy, start + (1 - 2 * core) * total, size))

    def send(there, start, size, links):
        part = span_of(start, size)
        return net.to(there, buf.at[part], buf.at[part], links, size)

    for level in reversed(range(len(order))):
        name, size, region = order[level], strides[level], bases[level]
        a = at[name]
        last = level == 0
        if name == "xhi":
            other = region + (1 - a) * size
            copies = [send(toward(at, name, 1), region + a * size, size, both("x"))]
            if last:
                share(region + a * size, size)
                arrived(region + a * size, size)
            yield copies
            wait_all(copies)
            if last:
                share(other, size)
                arrived(other, size)
        else:
            h1, h2 = halves(size)
            own, up, down, far = (region + (a + k) % RING * size for k in (0, 1, 3, 2))
            above, below, opposite = (toward(at, name, k) for k in (1, -1, 2))
            plus, minus = ((link,) for link in both(name))
            if level < direct:
                yield from net.enter(name, RINGS_IN)
            e = send(above, own, size, plus)
            f = send(below, own, size, minus)
            if last:
                share(own, size)
            if level >= direct:
                g = send(opposite, own, size, both(name))
                yield [e, f, g]
                wait_all([e, f, g])
            else:
                if last:
                    arrived(own, size)
                yield [e, f]
                wait_all([e])
                g = send(above, down, h1, plus)
                wait_all([f])
                h = send(below, up + h1, h2, minus)
                if last:
                    share(down, size)
                    share(up, size)
                    arrived(down, size)
                    arrived(up, size)
                yield [g, h]
                wait_all([g, h])
                net.leave(name)
                if last:
                    share(far, size)
                    arrived(far, size)
    for copy, start, size in shared:
        yield [copy]
        wait_all([copy])
        arrived(start, size)


def fetch_kernel(rid_ref, ent_ref, rel_hbm, slab_hbm, rows_hbm, own, packed, slab, rel, rel_rows, got, send, recv, local):
    at = here()
    m = lax.axis_index("member")
    greet(
        [toward(at, "y", 1), toward(at, "y", -1), toward(at, "xhi", 1), toward(at, "core", 1), next_group(1), next_group(-1)]
    )
    net = Copies(send, recv, local)
    entry = net.home(rel_hbm, rel)
    for j in range(8):
        rows = slice(j * GROUP, (j + 1) * GROUP)
        for c in range(3):
            own[pl.ds(j * PACK + c * GROUP, GROUP), :] = ent_ref[rows, c * LANES : (c + 1) * LANES]
        own[pl.ds(j * PACK + 96, 8), :] = pack_tail(ent_ref[rows, 3 * LANES : 4 * LANES])

    writes = []
    parts = len(PART_IN)
    size = part_size(PART_IN)
    groups = size // PACK

    def flow(part):
        start = part * BLOCKS * size
        mine = span_of(part_row(m, part, PART_IN), size)
        yield from net.enter("shift", SHIFTS)
        shift = net.to(next_group(-1), own.at[pl.ds(part * size, size)], packed.at[mine], ("z-",), size)
        yield [shift]
        wait_all([shift])
        net.leave("shift")

        def arrived(begin, rows):
            def block(i, carry):
                source = begin + i * size
                flat = (source - start) // size
                where = digits_of(flat % 8, PART_IN[part])
                member = (where["y"] * 2 + where["xhi"]) * 2 + flat // 8
                for k in range(groups):
                    base = source + k * PACK
                    out = (member * 256 + (part * groups + k) * GROUP) * CHUNKS
                    out = pl.multiple_of(out, 128)
                    for c in range(3):
                        slab[pl.ds(out + c, GROUP, stride=CHUNKS), :] = packed[span_of(base + c * GROUP, GROUP), :]
                    slab[pl.ds(out + 3, GROUP, stride=CHUNKS), :] = unpack_tail(packed[span_of(base + 96, 8), :])
                return carry

            lax.fori_loop(0, rows // size, block, 0)
            net.now += 0.04 * rows / PACK

        yield from spread_flow(net, at, packed, start, size, PART_IN[part], 9, arrived)
        view = (BLOCKS, parts, groups * GROUP * CHUNKS, LANES)
        writes.append(net.home(slab.reshape(view).at[:, part], slab_hbm.reshape(view).at[:, part]))

    def gather():
        tile = 256
        width, total = rel.shape
        entry.wait()
        for t in range(total // (4 * tile)):
            def convert(i, carry):
                k = t * 4 + i
                part = span_of(k * tile, tile, tile)
                wide = jnp.concatenate([rel[:, part], jnp.zeros((CHUNKS * LANES - width, tile), F32)], axis=0)
                rel_rows[part] = wide.T.reshape(tile, CHUNKS, LANES)
                return carry

            lax.fori_loop(0, 4, convert, 0)
            yield True
        edges = got.shape[0] // CHUNKS
        segment, unroll = 512, 16
        for t in range(edges // segment):
            def step(b, carry):
                for u in range(unroll):
                    j = t * segment + b * unroll + u
                    got[row(j), :] = rel_rows[rid_ref[0, j]]
                return carry

            lax.fori_loop(0, segment // unroll, step, 0)
            part = pl.ds(t * segment * CHUNKS, segment * CHUNKS)
            writes.append(net.home(got.at[part], rows_hbm.at[part]))
            yield True

    for part in range(parts):
        net.add(flow(part))
    net.run(gather())
    for write in writes:
        write.wait()
    net.finish()


def fetch(rid, ent, relations):
    edges = rid.shape[1]
    width, count = relations.shape
    rows = ent.shape[0] * BLOCKS
    anym = pl.BlockSpec(memory_space=pl.ANY)
    return pl.pallas_call(
        fetch_kernel,
        out_shape=(
            jax.ShapeDtypeStruct((rows * CHUNKS, LANES), F32),
            jax.ShapeDtypeStruct((edges * CHUNKS, LANES), F32),
        ),
        in_specs=[pl.BlockSpec(memory_space=pltpu.SMEM), pl.BlockSpec(memory_space=pltpu.VMEM), anym],
        out_specs=(anym, anym),
        scratch_shapes=[
            pltpu.VMEM((256 // GROUP * PACK, LANES), F32),
            pltpu.VMEM((rows // GROUP * PACK, LANES), F32),
            pltpu.VMEM((rows * CHUNKS, LANES), F32),
            pltpu.VMEM((width, count), F32),
            pltpu.VMEM((count, CHUNKS, LANES), F32),
            pltpu.VMEM((edges * CHUNKS, LANES), F32),
            pltpu.SemaphoreType.DMA((128,)),
            pltpu.SemaphoreType.DMA((128,)),
            pltpu.SemaphoreType.DMA((24,)),
        ],
        compiler_params=pltpu.CompilerParams(vmem_limit_bytes=56 * 2**20, collective_id=1, has_side_effects=True),
        name="fetch",
    )(rid, ent, relations)


def bucket_kernel(
    spans, unroll,
    cnt_ref, ridx_ref, nidx_ref, rid_ref, lhs_ref, ent_ref, rel_ref, slab_hbm,
    right_hbm, rel0_hbm, rel1_hbm, rel2_hbm, left_ref,
    slab, racc, nacc, relacc, rvec, nvec, gr, gn, grel, sem,
):
    s = pl.program_id(0)
    total = racc.shape[0]

    @pl.when(s == 0)
    def _():
        load = pltpu.make_async_copy(slab_hbm, slab.at[pl.ds(0, total)], sem.at[0])
        load.start()
        nvec[pl.ds(NEG * CHUNKS, (SPAN - NEG) * CHUNKS), :] = jnp.zeros(((SPAN - NEG) * CHUNKS, LANES), F32)
        racc[...] = jnp.zeros_like(racc)
        nacc[...] = jnp.zeros_like(nacc)
        relacc[...] = jnp.zeros_like(relacc)
        left_ref[...] = jnp.zeros_like(left_ref)
        load.wait()

    def scatter(j, negative):
        edge = (s - 1) * SPAN + j
        rel = row(rid_ref[0, edge])
        rgt = row(ridx_ref[0, edge])
        own = row(j)
        relacc[rel, :] = relacc[rel, :] + grel[own, :]
        racc[rgt, :] = racc[rgt, :] + gr[own, :]
        if negative:
            neg = row(nidx_ref[0, (s - 1) * NEG + j])
            nacc[neg, :] = nacc[neg, :] + gn[own, :]

    def gather(j, negative):
        own = row(j)
        rvec[own, :] = slab[row(ridx_ref[0, s * SPAN + j]), :]
        if negative:
            nvec[own, :] = slab[row(nidx_ref[0, s * NEG + j]), :]

    def rows_loop(*works):
        def step(b, carry):
            for u in range(unroll):
                for work in works:
                    work(b * unroll + u, True)
            return carry

        last = NEG // unroll * unroll
        lax.fori_loop(0, last // unroll, step, 0)
        for j in range(last, SPAN):
            for work in works:
                work(j, j < NEG)

    @pl.when(s == 0)
    def _():
        rows_loop(gather)

    @pl.when((s > 0) & (s < spans))
    def _():
        rows_loop(gather, scatter)

    @pl.when(s == spans)
    def _():
        rows_loop(scatter)

    @pl.when(s < spans)
    def _():
        hot = (lax.broadcasted_iota(jnp.int32, (ent_ref.shape[0], SPAN), 0) == lhs_ref[...]).astype(F32).astype(BF16)
        eh, el = split(ent_ref[...])
        first = ((0,), (0,))
        last = ((1,), (1,))
        inner = ((1,), (0,))
        left = dot2(jnp.concatenate([hot, hot], axis=0), jnp.concatenate([eh, el], axis=0), first)
        rel = read_rows(rel_ref, SPAN)
        query = left * rel
        live = (s * SPAN + lax.broadcasted_iota(jnp.int32, (SPAN, 1), 0) < cnt_ref[0]).astype(F32)
        q = split(query)
        n = split(read_rows(nvec, SPAN))
        neg = dot3(q, n, last)
        dneg = split(jax.nn.sigmoid(neg) * (live / NEG))
        right = read_rows(rvec, SPAN)
        pos = jnp.sum(query * right, axis=1, keepdims=True)
        dpos = -jax.nn.sigmoid(-pos) * live
        write_rows(gr, dpos * query, SPAN)
        write_rows(gn, dot3(dneg, q, first), SPAN)
        grad_query = dpos * right + dot3(dneg, n, inner)
        write_rows(grel, grad_query * left, SPAN)
        gl = jnp.concatenate(split(grad_query * rel), axis=0)
        left_ref[...] += dot2(jnp.concatenate([hot, hot], axis=1), gl, inner)

    @pl.when(s == spans)
    def _():
        def right_member(m, carry):
            for part in range(len(PART_SUM)):
                for k in range(256 // GROUP // len(PART_SUM)):
                    at = part * (256 // GROUP // len(PART_SUM)) + k
                    src = pl.multiple_of((m * 256 + at * GROUP) * CHUNKS, 128)
                    out = part_row(m, part, PART_SUM) + k * PACK
                    planes = [
                        racc[pl.ds(src + c, GROUP, stride=CHUNKS), :] + nacc[pl.ds(src + c, GROUP, stride=CHUNKS), :]
                        for c in range(CHUNKS)
                    ]
                    for c in range(3):
                        slab[span_of(out + c * GROUP, GROUP), :] = planes[c]
                    slab[span_of(out + 96, 8), :] = pack_tail(planes[3])
            return carry

        lax.fori_loop(0, BLOCKS, right_member, 0)
        out = pltpu.make_async_copy(slab.at[pl.ds(0, right_hbm.shape[0])], right_hbm, sem.at[0])
        out.start()
        begins = (0, 2 * SHARDS * PIECE_ROWS[0], 2 * SHARDS * (PIECE_ROWS[0] + PIECE_ROWS[1]))

        def shards(i, carry):
            for k in range(4):
                group = i * 4 + k
                src = pl.multiple_of(group * GROUP * CHUNKS, 128)
                at = [b + shard_row(group, p, PIECE_SUM) for p, b in enumerate(begins)]
                for c in range(3):
                    nacc[span_of(at[c], GROUP), :] = relacc[pl.ds(src + c, GROUP, stride=CHUNKS), :]
                nacc[span_of(at[2] + GROUP, 8), :] = pack_tail(relacc[pl.ds(src + 3, GROUP, stride=CHUNKS), :])
            return carry

        copies = []
        for half in range(2):
            lax.fori_loop(half * SHARDS // 4, (half + 1) * SHARDS // 4, shards, 0)
            for p, ref in enumerate((rel0_hbm, rel1_hbm, rel2_hbm)):
                size = SHARDS * PIECE_ROWS[p]
                src = nacc.at[pl.ds(begins[p] + half * size, size)]
                copies.append(pltpu.make_async_copy(src, ref.at[pl.ds(half * size, size)], sem.at[1 + len(copies)]))
                copies[-1].start()
        for copy in copies:
            copy.wait()
        out.wait()


def bucket(counts, ridx, nidx, rid, lhs, ent, rel_rows, slab):
    edges = rid.shape[1]
    spans = edges // SPAN
    total = slab.shape[0]
    smem = pl.BlockSpec(memory_space=pltpu.SMEM)
    anym = pl.BlockSpec(memory_space=pl.ANY)
    vm = lambda r: pltpu.VMEM((r, LANES), F32)
    span_rows = SPAN * CHUNKS
    return pl.pallas_call(
        functools.partial(bucket_kernel, spans, 25),
        grid=(spans + 1,),
        out_shape=(
            jax.ShapeDtypeStruct((BLOCKS * 256 // GROUP * PACK, LANES), F32),
            *(jax.ShapeDtypeStruct((2 * SHARDS * r, LANES), F32) for r in PIECE_ROWS),
            jax.ShapeDtypeStruct(ent.shape, F32),
        ),
        in_specs=[
            smem, smem, smem, smem,
            pl.BlockSpec((1, SPAN), lambda s: (0, jnp.minimum(s, spans - 1))),
            pl.BlockSpec(ent.shape, lambda s: (0, 0)),
            pl.BlockSpec((span_rows, LANES), lambda s: (jnp.minimum(s, spans - 1), 0)),
            anym,
        ],
        out_specs=(anym, anym, anym, anym, pl.BlockSpec(ent.shape, lambda s: (0, 0))),
        scratch_shapes=[
            vm(total), vm(total), vm(total), vm(total),
            vm(span_rows), vm(span_rows), vm(span_rows), vm(span_rows), vm(span_rows),
            pltpu.SemaphoreType.DMA((8,)),
        ],
        compiler_params=pltpu.CompilerParams(vmem_limit_bytes=58 * 2**20),
        name="bucket",
    )(counts, ridx, nidx, rid, lhs, ent, rel_rows, slab)


def ring_rows(half, order):
    size, used = half, 0
    for name in order:
        size = size // (2 if name == "xhi" else RING)
        used += size if name == "xhi" else 3 * size
    return used


def reduce_kernel(
    width,
    states_ref, rel_hbm, right_hbm, rel0_hbm, rel1_hbm, rel2_hbm,
    back_hbm, new0_hbm, new1_hbm, new2_hbm,
    *scratch,
):
    scratch = list(scratch)
    take = lambda n: [scratch.pop(0) for _ in range(n)]
    parts = len(PART_SUM)
    racc, rland, rring = take(parts), take(parts), take(parts)
    pacc, pland, pring, news = take(3), take(3), take(3), take(3)
    back, block, shard, send, recv, local = scratch
    at = here()
    mine = (at["core"] * SHARDS + index_of(at, ("z", "y", "x"))) * GROUP
    inside = pl.ds(pl.multiple_of(mine % LANES, GROUP), GROUP)
    lanes = pl.ds(pl.multiple_of(mine // LANES * LANES, LANES), LANES)
    greet(
        [toward(at, axis, step) for axis in ("x", "y", "z") for step in (1, -1, 2)]
        + [toward(at, "core", 1), next_group(1), next_group(-1)]
    )
    net = Copies(send, recv, local)
    entry = net.home(rel_hbm.at[:, lanes], block)
    size = part_size(PART_SUM)
    region = BLOCKS * size
    backs = []
    bases = {}

    def right_flow(part):
        def done(base):
            mine = pl.ds(part * size, size)
            src = racc[part].at[span_of(base, size)]
            copies = [net.to(next_group(1), src, back.at[mine], ("z+",), size)]
            yield copies
            wait_all(copies)
            backs.append(net.home(back.at[mine], back_hbm.at[mine]))

        return sum_flow(
            net, at, right_hbm.at[pl.ds(part * region, region)], racc[part], rland[part], rring[part],
            PART_SUM[part], 9, done,
        )

    def piece_flow(piece):
        def done(base):
            bases[piece] = base
            if len(bases) == 3:
                update()
            yield from ()

        src = (rel0_hbm, rel1_hbm, rel2_hbm)[piece]
        return sum_flow(net, at, src, pacc[piece], pland[piece], pring[piece], PIECE_SUM[piece], 1, done)

    def update():
        planes = [pacc[p][span_of(bases[p], GROUP), :] for p in range(3)]
        planes.append(unpack_tail(pacc[2][span_of(bases[2] + GROUP, 8), :]))
        squares = planes[0] * planes[0]
        for plane in planes[1:]:
            squares = squares + plane * plane
        entry.wait()
        height = CHUNKS * LANES
        wide = jnp.concatenate([block[...], jnp.zeros((height - width, LANES), F32)], axis=0)
        old = jnp.broadcast_to(states_ref[:, lanes], (LANES, LANES)).T
        shard[:, 0:height] = wide.T
        shard[:, height : height + LANES] = old
        state = shard[inside, height : height + 1] + jnp.sum(squares, axis=1, keepdims=True) / width
        root = jnp.sqrt(state)
        fresh = [shard[inside, c * LANES : (c + 1) * LANES] - STEP_SIZE * planes[c] / root for c in range(CHUNKS)]
        tail = pack_tail(fresh[3])
        lane = lax.broadcasted_iota(jnp.int32, (8, LANES), 1)
        for g in range(GROUP // 8):
            tail = jnp.where(lane == LANES // 2 + g, state[8 * g : 8 * g + 8], tail)
        outs = (new0_hbm, new1_hbm, new2_hbm)
        net.now += 0.5
        for p in range(3):
            place = (at["core"] * SHARDS + index_of(at, PIECE_OUT[p])) * PIECE_ROWS[p]
            news[p][span_of(place, GROUP), :] = fresh[p]
            if p == 2:
                news[p][span_of(place + GROUP, 8), :] = tail

            def arrived(start, size, p=p):
                rows = PIECE_ROWS[p]
                half, k = start // (SHARDS * rows), start // (16 * rows) % RING
                src = news[p].at[span_of(start, size)].reshape(4, 4, rows, LANES)
                dst = (outs[p].at[half, k], outs[p].at[half, :, :, k], outs[p].at[half, :, k])[p]
                backs.append(net.home(src, dst))

            net.add(spread_flow(net, at, news[p], 0, PIECE_ROWS[p], PIECE_OUT[p], 1, arrived))

    for k in range(max(3, parts)):
        if k < 3:
            net.add(piece_flow(k))
        if k < parts:
            net.add(right_flow(k))
    net.run()
    for copy in backs:
        copy.wait()
    net.finish()


def reduce(width, states, relations, right, pieces):
    anym = pl.BlockSpec(memory_space=pl.ANY)
    vmem = pl.BlockSpec(memory_space=pltpu.VMEM)
    vm = lambda r: pltpu.VMEM((r, LANES), F32)
    parts = len(PART_SUM)
    half = BLOCKS // 2 * part_size(PART_SUM)
    return pl.pallas_call(
        functools.partial(reduce_kernel, width),
        out_shape=(
            jax.ShapeDtypeStruct((256 // GROUP * PACK, LANES), F32),
            *(jax.ShapeDtypeStruct((2, 4, 4, 4, r, LANES), F32) for r in PIECE_ROWS),
        ),
        in_specs=[vmem, anym, anym, anym, anym, anym],
        out_specs=(anym,) * 4,
        scratch_shapes=[
            *(vm(half) for _ in range(parts)),
            *(vm(half) for _ in range(parts)),
            *(vm(ring_rows(half, PART_SUM[p])) for p in range(parts)),
            *(vm(SHARDS * r) for r in PIECE_ROWS),
            *(vm(SHARDS * r) for r in PIECE_ROWS),
            *(vm(ring_rows(SHARDS * r, PIECE_SUM[p])) for p, r in enumerate(PIECE_ROWS)),
            *(vm(2 * SHARDS * r) for r in PIECE_ROWS),
            vm(256 // GROUP * PACK),
            pltpu.VMEM((width, LANES), F32),
            pltpu.VMEM((LANES, (CHUNKS + 1) * LANES), F32),
            pltpu.SemaphoreType.DMA((192,)),
            pltpu.SemaphoreType.DMA((192,)),
            pltpu.SemaphoreType.DMA((64,)),
        ],
        compiler_params=pltpu.CompilerParams(vmem_limit_bytes=56 * 2**20, collective_id=2, has_side_effects=True),
        name="reduce",
    )(states, relations, right, *pieces)


def finish_kernel(
    width, left_ref, back_ref, ent_ref, state_ref, new0, new1, new2, rel_ref, rel_state_ref, ent_out, state_out
):
    s = pl.program_id(0)
    count = rel_ref.shape[1]
    lane = lax.broadcasted_iota(jnp.int32, (8, LANES), 1)
    for k in range(count // LANES):
        out = pl.ds(k * LANES, LANES)
        groups = range(k * 4, k * 4 + 4)
        for c, ref in enumerate((new0, new1, new2)):
            r = PIECE_ROWS[c]
            plane = jnp.concatenate([ref[g * r : g * r + GROUP, :] for g in groups], axis=0)
            rel_ref[c * LANES : (c + 1) * LANES, out] = plane.T
        r = PIECE_ROWS[2]
        tails = []
        for group in groups:
            packed = new2[group * r + GROUP : (group + 1) * r, :]
            for g in range(GROUP // 8):
                state = pltpu.roll(packed, LANES // 2 + TAIL - g, 1)
                values = packed if g == 0 else pltpu.roll(packed, LANES - TAIL * g, 1)
                tails.append(jnp.where(lane < TAIL, values, state))
        tail = jnp.concatenate(tails, axis=0).T
        rel_ref[3 * LANES : width, out] = tail[: width - 3 * LANES]
        rel_state_ref[:, out] = tail[TAIL : TAIL + 1]

    @pl.when(s == 0)
    def _():
        for i in range(2):
            part = slice(i * LANES, (i + 1) * LANES)
            wide = []
            for j in range(4 * i, 4 * i + 4):
                planes = [back_ref[pl.ds(j * PACK + c * GROUP, GROUP), :] for c in range(3)]
                planes.append(unpack_tail(back_ref[pl.ds(j * PACK + 96, 8), :]))
                wide.append(jnp.concatenate(planes, axis=1))
            grad = (left_ref[part, :] + jnp.concatenate(wide, axis=0)).T[:width]
            state = state_ref[:, part] + jnp.sum(grad * grad, axis=0, keepdims=True) / width
            state_out[:, part] = state
            ent_out[:, part] = ent_ref[:, part] - STEP_SIZE * grad / jnp.sqrt(state)


def finish(width, left, back, ent, ent_state, news, count):
    steps = 4
    full = lambda a: pl.BlockSpec(a.shape, lambda s: (0, 0))
    rows = ent.shape[1]
    return pl.pallas_call(
        functools.partial(finish_kernel, width),
        grid=(steps,),
        out_shape=(
            jax.ShapeDtypeStruct((width, count), F32),
            jax.ShapeDtypeStruct((1, count), F32),
            jax.ShapeDtypeStruct((width, rows), F32),
            jax.ShapeDtypeStruct((1, rows), F32),
        ),
        in_specs=[full(a) for a in (left, back, ent, ent_state)]
        + [pl.BlockSpec((2 * SHARDS // steps * r, LANES), lambda s: (s, 0)) for r in PIECE_ROWS],
        out_specs=(
            pl.BlockSpec((width, count // steps), lambda s: (0, s)),
            pl.BlockSpec((1, count // steps), lambda s: (0, s)),
            pl.BlockSpec((width, rows), lambda s: (0, 0)),
            pl.BlockSpec((1, rows), lambda s: (0, 0)),
        ),
        compiler_params=pltpu.CompilerParams(vmem_limit_bytes=60 * 2**20),
        name="finish",
    )(left, back, ent, ent_state, *news)


def on_device(
    entities, ent_state, relations, rel_state, lhs_rows, rhs_owner, rhs_off, neg_owner, neg_off, rel_ids, counts
):
    shard = entities[0]
    rows, width = shard.shape
    wide = CHUNKS * LANES
    padded = jnp.pad(shard, ((0, 0), (0, wide - width)))
    ridx = rhs_owner[:, :, 0] * rows + rhs_off
    nidx = neg_owner[:, :, 0] * rows + neg_off
    slab, rel_rows = fetch(rel_ids, padded, relations.T)
    right, *pieces, left = bucket(counts[0], ridx, nidx, rel_ids, lhs_rows, padded, rel_rows, slab)
    back, *news = reduce(width, rel_state[None], relations.T, right, pieces)
    rel_new, states, new_shard, new_state = finish(
        width, left, back, shard.T, ent_state, [n.reshape(-1, LANES) for n in news], relations.shape[0]
    )
    return (new_shard.T[None], new_state, rel_new.T, states.reshape(-1))


def solution(mesh):
    in_specs = (
        P("group", "member", None), P("group", "member"), P(), P(),
        P("group", "member"), P("group", "member", None), P("group", "member"),
        P("group", "member", None), P("group", "member"), P("group", "member"), P("group", "member"),
    )
    out_specs = (P("group", "member", None), P("group", "member"), P(), P())
    return jax.shard_map(on_device, mesh=mesh, in_specs=in_specs, out_specs=out_specs, check_vma=False)
```

```python
import functools
import jax
import jax.numpy as jnp
from jax import lax
from jax.experimental import pallas as pl
from jax.experimental.pallas import tpu as pltpu
from jax.sharding import PartitionSpec as P

SPAN = 512
NEG = 500
STEP_SIZE = 0.1
LANES = 128
F32 = jnp.float32
BF16 = jnp.bfloat16
MESH = pl.DeviceIdType.MESH

CHUNKS = 4
TAIL = 16
GROUP = 32
PACK = 104
BLOCKS = 16
RING = 4
Y_FIRST = ("y", "xhi")
X_FIRST = ("xhi", "y")
PART_IN = (X_FIRST, Y_FIRST) * 3 + (Y_FIRST, Y_FIRST)
PART_SUM = (X_FIRST, Y_FIRST, Y_FIRST, Y_FIRST) * 2
PIECE_ROWS = (32, 32, 40)
PIECE_SUM = (("z", "y", "x"), ("x", "z", "y"), ("z", "x", "y"))
PIECE_OUT = (("z", "y", "x"), ("x", "z", "y"), ("y", "z", "x"))
SHARDS = 64
SHIFTS = 8
RINGS_IN = 8
RINGS_SUM = 2
LINK_ROWS = 70.0
CORE_ROWS = 1000.0
LATENCY = 4.0


def split(x):
    hi = x.astype(BF16)
    return hi, (x - hi.astype(F32)).astype(BF16)


def dot2(a, b, dims):
    return lax.dot_general(a, b, (dims, ((), ())), preferred_element_type=F32)


def dot3(a, b, dims):
    (ah, al), (bh, bl) = a, b
    (ka,), (kb,) = dims
    return dot2(jnp.concatenate([ah, ah, al], axis=ka), jnp.concatenate([bh, bl, bh], axis=kb), dims)


def row(i):
    return pl.ds(pl.multiple_of(i * CHUNKS, CHUNKS), CHUNKS)


def span_of(start, size, tile=8):
    return pl.ds(start if isinstance(start, int) else pl.multiple_of(start, tile), size)


def read_rows(ref, rows):
    return jnp.concatenate([ref[pl.ds(c, rows, stride=CHUNKS), :] for c in range(CHUNKS)], axis=1)


def write_rows(ref, value, rows):
    for c in range(CHUNKS):
        ref[pl.ds(c, rows, stride=CHUNKS), :] = value[:, c * LANES : (c + 1) * LANES]


def pack_tail(tail):
    packed = tail[0:8]
    for g in range(1, GROUP // 8):
        packed = packed + pltpu.roll(tail[8 * g : 8 * g + 8], TAIL * g, 1)
    return packed


def unpack_tail(packed):
    kept = lax.broadcasted_iota(jnp.int32, (8, LANES), 1) < TAIL
    parts = [jnp.where(kept, packed if g == 0 else pltpu.roll(packed, LANES - TAIL * g, 1), 0.0) for g in range(GROUP // 8)]
    return jnp.concatenate(parts, axis=0)


def digits_of(flat, order):
    sizes = {"y": 4, "xhi": 2, "x": 4, "z": 4}
    out = {}
    for name in reversed(order):
        out[name] = flat % sizes[name]
        flat = flat // sizes[name]
    return out


def index_of(where, order):
    sizes = {"y": 4, "xhi": 2, "x": 4, "z": 4}
    at = 0
    for name in order:
        at = at * sizes[name] + where[name]
    return at


def part_size(orders):
    return 256 // GROUP * PACK // len(orders)


def part_row(member, part, orders):
    where = digits_of(member // 2, ("y", "xhi"))
    at = (member % 2) * 8 + index_of(where, orders[part])
    return (part * BLOCKS + at) * part_size(orders)


def shard_row(group, piece, orders):
    where = digits_of(group % SHARDS, ("z", "y", "x"))
    return ((group // SHARDS) * SHARDS + index_of(where, orders[piece])) * PIECE_ROWS[piece]


def here():
    g = lax.axis_index("group")
    m = lax.axis_index("member")
    return {"x": (m // 2) % 2 * 2 + g // 4, "xhi": (m // 2) % 2, "y": m // 4, "z": g % 4, "core": m % 2}


def device(at):
    return (at["x"] % 2 * 4 + at["z"], at["y"] * 4 + at["x"] // 2 * 2 + at["core"])


def toward(at, axis, step):
    there = dict(at)
    if axis == "core":
        there["core"] = 1 - at["core"]
    elif axis == "xhi":
        there["x"] = (at["x"] + 2) % 4
    else:
        there[axis] = (at[axis] + step + 4) % 4
    return device(there)


def next_group(step):
    return ((lax.axis_index("group") + step + 8) % 8, lax.axis_index("member"))


def greet(devices):
    barrier = pltpu.get_barrier_semaphore()
    for there in devices:
        pl.semaphore_signal(barrier, inc=1, device_id=there, device_id_type=MESH)
    pl.semaphore_wait(barrier, len(devices))


class Copies:
    def __init__(self, send, recv, local):
        self.send, self.recv, self.local = send, recv, local
        self.started, self.kept, self.homes = 0, [], 0
        self.now, self.busy, self.flows, self.added, self.gates = 0.0, {}, [], 0, {}

    def to(self, there, src, dst, links, rows):
        copy = pltpu.make_async_remote_copy(
            src_ref=src, dst_ref=dst, send_sem=self.send.at[self.started], recv_sem=self.recv.at[self.started],
            device_id=there, device_id_type=MESH,
        )
        copy.start()
        self.started += 1
        self.kept.append(copy)
        begin = max([self.now] + [self.busy.get(link, 0.0) for link in links])
        end = begin + rows / (CORE_ROWS if links == ("core",) else LINK_ROWS)
        for link in links:
            self.busy[link] = end
        self.now += 0.05
        return copy, end + LATENCY

    def home(self, src, dst):
        copy = pltpu.make_async_copy(src, dst, self.local.at[self.homes])
        copy.start()
        self.homes += 1
        return copy

    def enter(self, name, limit):
        held, waiting = self.gates.setdefault(name, ([], []))
        if len(held) == limit:
            yield waiting
        held.append(None)

    def leave(self, name):
        held, waiting = self.gates[name]
        held.pop()
        if waiting:
            number, flow = waiting.pop(0)
            self.step(number, flow)

    def step(self, number, flow):
        ready = next(flow, None)
        if ready is None:
            return
        if any(ready is waiting for _, waiting in self.gates.values()):
            ready.append((number, flow))
        else:
            self.flows.append((max(r for _, r in ready), number, flow))

    def add(self, flow):
        self.added += 1
        self.step(self.added, flow)

    def run(self, beside=iter(()), cost=0.7):
        while self.flows:
            entry = min(self.flows)
            while entry[0] > self.now + cost and next(beside, None) is not None:
                self.now += cost
            self.flows.remove(entry)
            self.now = max(self.now, entry[0]) + 0.1
            self.step(entry[1], entry[2])
        for _ in beside:
            pass

    def finish(self):
        for copy in self.kept:
            copy.wait_send()


def wait_all(copies):
    for copy, _ in copies:
        copy.wait_recv()


def halves(size):
    first = -(-size // 16) * 8
    return first, size - first


def add_into(dst, at, src, start, size):
    tile = size
    while tile > 256:
        tile = tile // 2 if tile % 16 == 0 else tile // 13
    if tile == size:
        dst[span_of(at, size), :] = dst[span_of(at, size), :] + src[span_of(start, size), :]
        return

    def step(i, carry):
        d = span_of(at + i * tile, tile)
        dst[d, :] = dst[d, :] + src[span_of(start + i * tile, tile), :]
        return carry

    lax.fori_loop(0, size // tile, step, 0)


def both(axis):
    return (axis + "+", axis + "-")


def sum_flow(net, at, src, acc, landing, ring, order, direct, done):
    half = acc.shape[0]
    core = at["core"]
    over = net.to(toward(at, "core", 1), src.at[span_of((1 - core) * half, half)], landing, ("core",), half)
    own = net.home(src.at[span_of(core * half, half)], acc)
    yield [over]
    own.wait()
    wait_all([over])
    add_into(acc, 0, landing, 0, half)
    base, size, used = 0, half, 0
    for level, axis in enumerate(order):
        a = at[axis]
        if axis == "xhi":
            size = size // 2
            src_at = acc.at[span_of(base + (1 - a) * size, size)]
            copies = [net.to(toward(at, axis, 1), src_at, ring.at[pl.ds(used, size)], both("x"), size)]
            yield copies
            wait_all(copies)
            add_into(acc, base + a * size, ring, used, size)
            used += size
        else:
            size = size // RING
            up, down, far = (base + (a + k) % RING * size for k in (1, 3, 2))
            above, below, opposite = (toward(at, axis, k) for k in (1, -1, 2))
            plus, minus = ((link,) for link in both(axis))
            ra, rc, rd = used, used + size, used + 2 * size
            if level >= direct:
                copies = [
                    net.to(opposite, acc.at[span_of(far, size)], ring.at[pl.ds(ra, size)], both(axis), size),
                    net.to(above, acc.at[span_of(up, size)], ring.at[pl.ds(rc, size)], plus, size),
                    net.to(below, acc.at[span_of(down, size)], ring.at[pl.ds(rd, size)], minus, size),
                ]
                yield copies
                wait_all(copies)
                add_into(acc, base + a * size, ring, ra, size)
            else:
                h1, h2 = halves(size)
                yield from net.enter(axis, RINGS_SUM)
                first = net.to(above, acc.at[span_of(far, h1)], ring.at[pl.ds(ra, h1)], plus, h1)
                second = net.to(below, acc.at[span_of(far + h1, h2)], ring.at[pl.ds(ra + h1, h2)], minus, h2)
                c2 = net.to(above, acc.at[span_of(up + h1, h2)], ring.at[pl.ds(rc + h1, h2)], plus, h2)
                d1 = net.to(below, acc.at[span_of(down, h1)], ring.at[pl.ds(rd, h1)], minus, h1)
                yield [first, second]
                wait_all([first])
                add_into(acc, up, ring, ra, h1)
                c1 = net.to(above, acc.at[span_of(up, h1)], ring.at[pl.ds(rc, h1)], plus, h1)
                wait_all([second])
                add_into(acc, down + h1, ring, ra + h1, h2)
                d2 = net.to(below, acc.at[span_of(down + h1, h2)], ring.at[pl.ds(rd + h1, h2)], minus, h2)
                copies = [c2, d1, c1, d2]
                yield copies
                wait_all(copies)
                net.leave(axis)
            add_into(acc, base + a * size, ring, rc, size)
            add_into(acc, base + a * size, ring, rd, size)
            used += 3 * size
        base = base + a * size
    yield from done(base)


def spread_flow(net, at, buf, offset, rows, order, direct, arrived):
    radix = {"xhi": 2, "x": 4, "y": 4, "z": 4}
    total = rows
    for name in order:
        total *= radix[name]
    core = at["core"]
    bases = [offset + core * total]
    strides = []
    size = total
    for name in order:
        size = size // radix[name]
        strides.append(size)
        bases.append(bases[-1] + at[name] * size)
    sibling = toward(at, "core", 1)
    shared = []

    def share(start, size):
        there = span_of(start, size)
        copy = net.to(sibling, buf.at[there], buf.at[there], ("core",), size)
        shared.append((copy, start + (1 - 2 * core) * total, size))

    def send(there, start, size, links):
        part = span_of(start, size)
        return net.to(there, buf.at[part], buf.at[part], links, size)

    for level in reversed(range(len(order))):
        name, size, region = order[level], strides[level], bases[level]
        a = at[name]
        last = level == 0
        if name == "xhi":
            other = region + (1 - a) * size
            copies = [send(toward(at, name, 1), region + a * size, size, both("x"))]
            if last:
                share(region + a * size, size)
                arrived(region + a * size, size)
            yield copies
            wait_all(copies)
            if last:
                share(other, size)
                arrived(other, size)
        else:
            h1, h2 = halves(size)
            own, up, down, far = (region + (a + k) % RING * size for k in (0, 1, 3, 2))
            above, below, opposite = (toward(at, name, k) for k in (1, -1, 2))
            plus, minus = ((link,) for link in both(name))
            if level < direct:
                yield from net.enter(name, RINGS_IN)
            e = send(above, own, size, plus)
            f = send(below, own, size, minus)
            if last:
                share(own, size)
            if level >= direct:
                g = send(opposite, own, size, both(name))
                yield [e, f, g]
                wait_all([e, f, g])
            else:
                if last:
                    arrived(own, size)
                yield [e, f]
                wait_all([e])
                g = send(above, down, h1, plus)
                wait_all([f])
                h = send(below, up + h1, h2, minus)
                if last:
                    share(down, size)
                    share(up, size)
                    arrived(down, size)
                    arrived(up, size)
                yield [g, h]
                wait_all([g, h])
                net.leave(name)
                if last:
                    share(far, size)
                    arrived(far, size)
    for copy, start, size in shared:
        yield [copy]
        wait_all([copy])
        arrived(start, size)


def fetch_kernel(rid_ref, ent_ref, rel_hbm, slab_hbm, rows_hbm, own, packed, slab, rel, rel_rows, got, send, recv, local):
    at = here()
    m = lax.axis_index("member")
    greet(
        [toward(at, "y", 1), toward(at, "y", -1), toward(at, "xhi", 1), toward(at, "core", 1), next_group(1), next_group(-1)]
    )
    net = Copies(send, recv, local)
    entry = net.home(rel_hbm, rel)
    for j in range(8):
        rows = slice(j * GROUP, (j + 1) * GROUP)
        for c in range(3):
            own[pl.ds(j * PACK + c * GROUP, GROUP), :] = ent_ref[rows, c * LANES : (c + 1) * LANES]
        own[pl.ds(j * PACK + 96, 8), :] = pack_tail(ent_ref[rows, 3 * LANES : 4 * LANES])

    writes = []
    parts = len(PART_IN)
    size = part_size(PART_IN)
    groups = size // PACK

    def flow(part):
        start = part * BLOCKS * size
        mine = span_of(part_row(m, part, PART_IN), size)
        yield from net.enter("shift", SHIFTS)
        shift = net.to(next_group(-1), own.at[pl.ds(part * size, size)], packed.at[mine], ("z-",), size)
        yield [shift]
        wait_all([shift])
        net.leave("shift")

        def arrived(begin, rows):
            def block(i, carry):
                source = begin + i * size
                flat = (source - start) // size
                where = digits_of(flat % 8, PART_IN[part])
                member = (where["y"] * 2 + where["xhi"]) * 2 + flat // 8
                for k in range(groups):
                    base = source + k * PACK
                    out = (member * 256 + (part * groups + k) * GROUP) * CHUNKS
                    out = pl.multiple_of(out, 128)
                    for c in range(3):
                        slab[pl.ds(out + c, GROUP, stride=CHUNKS), :] = packed[span_of(base + c * GROUP, GROUP), :]
                    slab[pl.ds(out + 3, GROUP, stride=CHUNKS), :] = unpack_tail(packed[span_of(base + 96, 8), :])
                return carry

            lax.fori_loop(0, rows // size, block, 0)
            net.now += 0.04 * rows / PACK

        yield from spread_flow(net, at, packed, start, size, PART_IN[part], 9, arrived)
        view = (BLOCKS, parts, groups * GROUP * CHUNKS, LANES)
        writes.append(net.home(slab.reshape(view).at[:, part], slab_hbm.reshape(view).at[:, part]))

    def gather():
        tile = 256
        width, total = rel.shape
        entry.wait()
        for t in range(total // (4 * tile)):
            def convert(i, carry):
                k = t * 4 + i
                part = span_of(k * tile, tile, tile)
                wide = jnp.concatenate([rel[:, part], jnp.zeros((CHUNKS * LANES - width, tile), F32)], axis=0)
                rel_rows[part] = wide.T.reshape(tile, CHUNKS, LANES)
                return carry

            lax.fori_loop(0, 4, convert, 0)
            yield True
        edges = got.shape[0] // CHUNKS
        segment, unroll = 512, 16
        for t in range(edges // segment):
            def step(b, carry):
                for u in range(unroll):
                    j = t * segment + b * unroll + u
                    got[row(j), :] = rel_rows[rid_ref[0, j]]
                return carry

            lax.fori_loop(0, segment // unroll, step, 0)
            part = pl.ds(t * segment * CHUNKS, segment * CHUNKS)
            writes.append(net.home(got.at[part], rows_hbm.at[part]))
            yield True

    for part in range(parts):
        net.add(flow(part))
    net.run(gather())
    for write in writes:
        write.wait()
    net.finish()


def fetch(rid, ent, relations):
    edges = rid.shape[1]
    width, count = relations.shape
    rows = ent.shape[0] * BLOCKS
    anym = pl.BlockSpec(memory_space=pl.ANY)
    return pl.pallas_call(
        fetch_kernel,
        out_shape=(
            jax.ShapeDtypeStruct((rows * CHUNKS, LANES), F32),
            jax.ShapeDtypeStruct((edges * CHUNKS, LANES), F32),
        ),
        in_specs=[pl.BlockSpec(memory_space=pltpu.SMEM), pl.BlockSpec(memory_space=pltpu.VMEM), anym],
        out_specs=(anym, anym),
        scratch_shapes=[
            pltpu.VMEM((256 // GROUP * PACK, LANES), F32),
            pltpu.VMEM((rows // GROUP * PACK, LANES), F32),
            pltpu.VMEM((rows * CHUNKS, LANES), F32),
            pltpu.VMEM((width, count), F32),
            pltpu.VMEM((count, CHUNKS, LANES), F32),
            pltpu.VMEM((edges * CHUNKS, LANES), F32),
            pltpu.SemaphoreType.DMA((128,)),
            pltpu.SemaphoreType.DMA((128,)),
            pltpu.SemaphoreType.DMA((24,)),
        ],
        compiler_params=pltpu.CompilerParams(vmem_limit_bytes=56 * 2**20, collective_id=1, has_side_effects=True),
        name="fetch",
    )(rid, ent, relations)


def bucket_kernel(
    spans, unroll,
    cnt_ref, ridx_ref, nidx_ref, rid_ref, lhs_ref, ent_ref, rel_ref, slab_hbm,
    right_hbm, rel0_hbm, rel1_hbm, rel2_hbm, left_ref,
    slab, racc, nacc, relacc, rvec, nvec, gr, gn, grel, sem,
):
    s = pl.program_id(0)
    total = racc.shape[0]

    @pl.when(s == 0)
    def _():
        load = pltpu.make_async_copy(slab_hbm, slab.at[pl.ds(0, total)], sem.at[0])
        load.start()
        nvec[pl.ds(NEG * CHUNKS, (SPAN - NEG) * CHUNKS), :] = jnp.zeros(((SPAN - NEG) * CHUNKS, LANES), F32)
        racc[...] = jnp.zeros_like(racc)
        nacc[...] = jnp.zeros_like(nacc)
        relacc[...] = jnp.zeros_like(relacc)
        left_ref[...] = jnp.zeros_like(left_ref)
        load.wait()

    def scatter(j, negative):
        edge = (s - 1) * SPAN + j
        rel = row(rid_ref[0, edge])
        rgt = row(ridx_ref[0, edge])
        own = row(j)
        relacc[rel, :] = relacc[rel, :] + grel[own, :]
        racc[rgt, :] = racc[rgt, :] + gr[own, :]
        if negative:
            neg = row(nidx_ref[0, (s - 1) * NEG + j])
            nacc[neg, :] = nacc[neg, :] + gn[own, :]

    def gather(j, negative):
        own = row(j)
        rvec[own, :] = slab[row(ridx_ref[0, s * SPAN + j]), :]
        if negative:
            nvec[own, :] = slab[row(nidx_ref[0, s * NEG + j]), :]

    def rows_loop(*works):
        def step(b, carry):
            for u in range(unroll):
                for work in works:
                    work(b * unroll + u, True)
            return carry

        last = NEG // unroll * unroll
        lax.fori_loop(0, last // unroll, step, 0)
        for j in range(last, SPAN):
            for work in works:
                work(j, j < NEG)

    @pl.when(s == 0)
    def _():
        rows_loop(gather)

    @pl.when((s > 0) & (s < spans))
    def _():
        rows_loop(gather, scatter)

    @pl.when(s == spans)
    def _():
        rows_loop(scatter)

    @pl.when(s < spans)
    def _():
        hot = (lax.broadcasted_iota(jnp.int32, (ent_ref.shape[0], SPAN), 0) == lhs_ref[...]).astype(F32).astype(BF16)
        eh, el = split(ent_ref[...])
        first = ((0,), (0,))
        last = ((1,), (1,))
        inner = ((1,), (0,))
        left = dot2(jnp.concatenate([hot, hot], axis=0), jnp.concatenate([eh, el], axis=0), first)
        rel = read_rows(rel_ref, SPAN)
        query = left * rel
        live = (s * SPAN + lax.broadcasted_iota(jnp.int32, (SPAN, 1), 0) < cnt_ref[0]).astype(F32)
        q = split(query)
        n = split(read_rows(nvec, SPAN))
        neg = dot3(q, n, last)
        dneg = split(jax.nn.sigmoid(neg) * (live / NEG))
        right = read_rows(rvec, SPAN)
        pos = jnp.sum(query * right, axis=1, keepdims=True)
        dpos = -jax.nn.sigmoid(-pos) * live
        write_rows(gr, dpos * query, SPAN)
        write_rows(gn, dot3(dneg, q, first), SPAN)
        grad_query = dpos * right + dot3(dneg, n, inner)
        write_rows(grel, grad_query * left, SPAN)
        gl = jnp.concatenate(split(grad_query * rel), axis=0)
        left_ref[...] += dot2(jnp.concatenate([hot, hot], axis=1), gl, inner)

    @pl.when(s == spans)
    def _():
        middle = len(PART_SUM) // 2

        def right_member(m, carry, parts):
            for part in parts:
                for k in range(256 // GROUP // len(PART_SUM)):
                    at = part * (256 // GROUP // len(PART_SUM)) + k
                    src = pl.multiple_of((m * 256 + at * GROUP) * CHUNKS, 128)
                    out = part_row(m, part, PART_SUM) + k * PACK
                    planes = [
                        racc[pl.ds(src + c, GROUP, stride=CHUNKS), :] + nacc[pl.ds(src + c, GROUP, stride=CHUNKS), :]
                        for c in range(CHUNKS)
                    ]
                    for c in range(3):
                        slab[span_of(out + c * GROUP, GROUP), :] = planes[c]
                    slab[span_of(out + 96, 8), :] = pack_tail(planes[3])
            return carry

        outs = []
        for k, parts in enumerate((range(middle), range(middle, 2 * middle))):
            lax.fori_loop(0, BLOCKS, functools.partial(right_member, parts=parts), 0)
            stretch = pl.ds(k * right_hbm.shape[0] // 2, right_hbm.shape[0] // 2)
            outs.append(pltpu.make_async_copy(slab.at[stretch], right_hbm.at[stretch], sem.at[7 * k]))
            outs[-1].start()
        begins = (0, 2 * SHARDS * PIECE_ROWS[0], 2 * SHARDS * (PIECE_ROWS[0] + PIECE_ROWS[1]))

        def shards(i, carry):
            for k in range(4):
                group = i * 4 + k
                src = pl.multiple_of(group * GROUP * CHUNKS, 128)
                at = [b + shard_row(group, p, PIECE_SUM) for p, b in enumerate(begins)]
                for c in range(3):
                    nacc[span_of(at[c], GROUP), :] = relacc[pl.ds(src + c, GROUP, stride=CHUNKS), :]
                nacc[span_of(at[2] + GROUP, 8), :] = pack_tail(relacc[pl.ds(src + 3, GROUP, stride=CHUNKS), :])
            return carry

        copies = []
        for half in range(2):
            lax.fori_loop(half * SHARDS // 4, (half + 1) * SHARDS // 4, shards, 0)
            for p, ref in enumerate((rel0_hbm, rel1_hbm, rel2_hbm)):
                size = SHARDS * PIECE_ROWS[p]
                src = nacc.at[pl.ds(begins[p] + half * size, size)]
                copies.append(pltpu.make_async_copy(src, ref.at[pl.ds(half * size, size)], sem.at[1 + len(copies)]))
                copies[-1].start()
        for copy in copies:
            copy.wait()
        for out in outs:
            out.wait()


def bucket(counts, ridx, nidx, rid, lhs, ent, rel_rows, slab):
    edges = rid.shape[1]
    spans = edges // SPAN
    total = slab.shape[0]
    smem = pl.BlockSpec(memory_space=pltpu.SMEM)
    anym = pl.BlockSpec(memory_space=pl.ANY)
    vm = lambda r: pltpu.VMEM((r, LANES), F32)
    span_rows = SPAN * CHUNKS
    return pl.pallas_call(
        functools.partial(bucket_kernel, spans, 25),
        grid=(spans + 1,),
        out_shape=(
            jax.ShapeDtypeStruct((BLOCKS * 256 // GROUP * PACK, LANES), F32),
            *(jax.ShapeDtypeStruct((2 * SHARDS * r, LANES), F32) for r in PIECE_ROWS),
            jax.ShapeDtypeStruct(ent.shape, F32),
        ),
        in_specs=[
            smem, smem, smem, smem,
            pl.BlockSpec((1, SPAN), lambda s: (0, jnp.minimum(s, spans - 1))),
            pl.BlockSpec(ent.shape, lambda s: (0, 0)),
            pl.BlockSpec((span_rows, LANES), lambda s: (jnp.minimum(s, spans - 1), 0)),
            anym,
        ],
        out_specs=(anym, anym, anym, anym, pl.BlockSpec(ent.shape, lambda s: (0, 0))),
        scratch_shapes=[
            vm(total), vm(total), vm(total), vm(total),
            vm(span_rows), vm(span_rows), vm(span_rows), vm(span_rows), vm(span_rows),
            pltpu.SemaphoreType.DMA((8,)),
        ],
        compiler_params=pltpu.CompilerParams(vmem_limit_bytes=58 * 2**20),
        name="bucket",
    )(counts, ridx, nidx, rid, lhs, ent, rel_rows, slab)


def ring_rows(half, order):
    size, used = half, 0
    for name in order:
        size = size // (2 if name == "xhi" else RING)
        used += size if name == "xhi" else 3 * size
    return used


def reduce_kernel(
    width,
    states_ref, rel_hbm, right_hbm, rel0_hbm, rel1_hbm, rel2_hbm,
    back_hbm, new0_hbm, new1_hbm, new2_hbm,
    *scratch,
):
    scratch = list(scratch)
    take = lambda n: [scratch.pop(0) for _ in range(n)]
    parts = len(PART_SUM)
    racc, rland, rring = take(parts), take(parts), take(parts)
    pacc, pland, pring, news = take(3), take(3), take(3), take(3)
    back, block, shard, send, recv, local = scratch
    at = here()
    mine = (at["core"] * SHARDS + index_of(at, ("z", "y", "x"))) * GROUP
    inside = pl.ds(pl.multiple_of(mine % LANES, GROUP), GROUP)
    lanes = pl.ds(pl.multiple_of(mine // LANES * LANES, LANES), LANES)
    greet(
        [toward(at, axis, step) for axis in ("x", "y", "z") for step in (1, -1, 2)]
        + [toward(at, "core", 1), next_group(1), next_group(-1)]
    )
    net = Copies(send, recv, local)
    entry = net.home(rel_hbm.at[:, lanes], block)
    size = part_size(PART_SUM)
    region = BLOCKS * size
    backs = []
    bases = {}

    def right_flow(part):
        def done(base):
            mine = pl.ds(part * size, size)
            src = racc[part].at[span_of(base, size)]
            copies = [net.to(next_group(1), src, back.at[mine], ("z+",), size)]
            yield copies
            wait_all(copies)
            backs.append(net.home(back.at[mine], back_hbm.at[mine]))

        return sum_flow(
            net, at, right_hbm.at[pl.ds(part * region, region)], racc[part], rland[part], rring[part],
            PART_SUM[part], 9, done,
        )

    def piece_flow(piece):
        def done(base):
            bases[piece] = base
            if len(bases) == 3:
                update()
            yield from ()

        src = (rel0_hbm, rel1_hbm, rel2_hbm)[piece]
        return sum_flow(net, at, src, pacc[piece], pland[piece], pring[piece], PIECE_SUM[piece], 1, done)

    def update():
        planes = [pacc[p][span_of(bases[p], GROUP), :] for p in range(3)]
        planes.append(unpack_tail(pacc[2][span_of(bases[2] + GROUP, 8), :]))
        squares = planes[0] * planes[0]
        for plane in planes[1:]:
            squares = squares + plane * plane
        entry.wait()
        height = CHUNKS * LANES
        wide = jnp.concatenate([block[...], jnp.zeros((height - width, LANES), F32)], axis=0)
        old = jnp.broadcast_to(states_ref[:, lanes], (LANES, LANES)).T
        shard[:, 0:height] = wide.T
        shard[:, height : height + LANES] = old
        state = shard[inside, height : height + 1] + jnp.sum(squares, axis=1, keepdims=True) / width
        root = jnp.sqrt(state)
        fresh = [shard[inside, c * LANES : (c + 1) * LANES] - STEP_SIZE * planes[c] / root for c in range(CHUNKS)]
        tail = pack_tail(fresh[3])
        lane = lax.broadcasted_iota(jnp.int32, (8, LANES), 1)
        for g in range(GROUP // 8):
            tail = jnp.where(lane == LANES // 2 + g, state[8 * g : 8 * g + 8], tail)
        outs = (new0_hbm, new1_hbm, new2_hbm)
        net.now += 0.5
        for p in range(3):
            place = (at["core"] * SHARDS + index_of(at, PIECE_OUT[p])) * PIECE_ROWS[p]
            news[p][span_of(place, GROUP), :] = fresh[p]
            if p == 2:
                news[p][span_of(place + GROUP, 8), :] = tail

            def arrived(start, size, p=p):
                rows = PIECE_ROWS[p]
                half, k = start // (SHARDS * rows), start // (16 * rows) % RING
                src = news[p].at[span_of(start, size)].reshape(4, 4, rows, LANES)
                dst = (outs[p].at[half, k], outs[p].at[half, :, :, k], outs[p].at[half, :, k])[p]
                backs.append(net.home(src, dst))

            net.add(spread_flow(net, at, news[p], 0, PIECE_ROWS[p], PIECE_OUT[p], 1, arrived))

    for k in range(max(3, parts)):
        if k < 3:
            net.add(piece_flow(k))
        if k < parts:
            net.add(right_flow(k))
    net.run()
    for copy in backs:
        copy.wait()
    net.finish()


def reduce(width, states, relations, right, pieces):
    anym = pl.BlockSpec(memory_space=pl.ANY)
    vmem = pl.BlockSpec(memory_space=pltpu.VMEM)
    vm = lambda r: pltpu.VMEM((r, LANES), F32)
    parts = len(PART_SUM)
    half = BLOCKS // 2 * part_size(PART_SUM)
    return pl.pallas_call(
        functools.partial(reduce_kernel, width),
        out_shape=(
            jax.ShapeDtypeStruct((256 // GROUP * PACK, LANES), F32),
            *(jax.ShapeDtypeStruct((2, 4, 4, 4, r, LANES), F32) for r in PIECE_ROWS),
        ),
        in_specs=[vmem, anym, anym, anym, anym, anym],
        out_specs=(anym,) * 4,
        scratch_shapes=[
            *(vm(half) for _ in range(parts)),
            *(vm(half) for _ in range(parts)),
            *(vm(ring_rows(half, PART_SUM[p])) for p in range(parts)),
            *(vm(SHARDS * r) for r in PIECE_ROWS),
            *(vm(SHARDS * r) for r in PIECE_ROWS),
            *(vm(ring_rows(SHARDS * r, PIECE_SUM[p])) for p, r in enumerate(PIECE_ROWS)),
            *(vm(2 * SHARDS * r) for r in PIECE_ROWS),
            vm(256 // GROUP * PACK),
            pltpu.VMEM((width, LANES), F32),
            pltpu.VMEM((LANES, (CHUNKS + 1) * LANES), F32),
            pltpu.SemaphoreType.DMA((192,)),
            pltpu.SemaphoreType.DMA((192,)),
            pltpu.SemaphoreType.DMA((64,)),
        ],
        compiler_params=pltpu.CompilerParams(vmem_limit_bytes=56 * 2**20, collective_id=2, has_side_effects=True),
        name="reduce",
    )(states, relations, right, *pieces)


def finish_kernel(
    width, left_ref, back_ref, ent_ref, state_ref, new0, new1, new2, rel_ref, rel_state_ref, ent_out, state_out
):
    s = pl.program_id(0)
    count = rel_ref.shape[1]
    lane = lax.broadcasted_iota(jnp.int32, (8, LANES), 1)
    for k in range(count // LANES):
        out = pl.ds(k * LANES, LANES)
        groups = range(k * 4, k * 4 + 4)
        for c, ref in enumerate((new0, new1, new2)):
            r = PIECE_ROWS[c]
            plane = jnp.concatenate([ref[g * r : g * r + GROUP, :] for g in groups], axis=0)
            rel_ref[c * LANES : (c + 1) * LANES, out] = plane.T
        r = PIECE_ROWS[2]
        tails = []
        for group in groups:
            packed = new2[group * r + GROUP : (group + 1) * r, :]
            for g in range(GROUP // 8):
                state = pltpu.roll(packed, LANES // 2 + TAIL - g, 1)
                values = packed if g == 0 else pltpu.roll(packed, LANES - TAIL * g, 1)
                tails.append(jnp.where(lane < TAIL, values, state))
        tail = jnp.concatenate(tails, axis=0).T
        rel_ref[3 * LANES : width, out] = tail[: width - 3 * LANES]
        rel_state_ref[:, out] = tail[TAIL : TAIL + 1]

    @pl.when(s == 0)
    def _():
        for i in range(2):
            part = slice(i * LANES, (i + 1) * LANES)
            wide = []
            for j in range(4 * i, 4 * i + 4):
                planes = [back_ref[pl.ds(j * PACK + c * GROUP, GROUP), :] for c in range(3)]
                planes.append(unpack_tail(back_ref[pl.ds(j * PACK + 96, 8), :]))
                wide.append(jnp.concatenate(planes, axis=1))
            grad = (left_ref[part, :] + jnp.concatenate(wide, axis=0)).T[:width]
            state = state_ref[:, part] + jnp.sum(grad * grad, axis=0, keepdims=True) / width
            state_out[:, part] = state
            ent_out[:, part] = ent_ref[:, part] - STEP_SIZE * grad / jnp.sqrt(state)


def finish(width, left, back, ent, ent_state, news, count):
    steps = 4
    full = lambda a: pl.BlockSpec(a.shape, lambda s: (0, 0))
    rows = ent.shape[1]
    return pl.pallas_call(
        functools.partial(finish_kernel, width),
        grid=(steps,),
        out_shape=(
            jax.ShapeDtypeStruct((width, count), F32),
            jax.ShapeDtypeStruct((1, count), F32),
            jax.ShapeDtypeStruct((width, rows), F32),
            jax.ShapeDtypeStruct((1, rows), F32),
        ),
        in_specs=[full(a) for a in (left, back, ent, ent_state)]
        + [pl.BlockSpec((2 * SHARDS // steps * r, LANES), lambda s: (s, 0)) for r in PIECE_ROWS],
        out_specs=(
            pl.BlockSpec((width, count // steps), lambda s: (0, s)),
            pl.BlockSpec((1, count // steps), lambda s: (0, s)),
            pl.BlockSpec((width, rows), lambda s: (0, 0)),
            pl.BlockSpec((1, rows), lambda s: (0, 0)),
        ),
        compiler_params=pltpu.CompilerParams(vmem_limit_bytes=60 * 2**20),
        name="finish",
    )(left, back, ent, ent_state, *news)


def on_device(
    entities, ent_state, relations, rel_state, lhs_rows, rhs_owner, rhs_off, neg_owner, neg_off, rel_ids, counts
):
    shard = entities[0]
    rows, width = shard.shape
    wide = CHUNKS * LANES
    padded = jnp.pad(shard, ((0, 0), (0, wide - width)))
    ridx = rhs_owner[:, :, 0] * rows + rhs_off
    nidx = neg_owner[:, :, 0] * rows + neg_off
    slab, rel_rows = fetch(rel_ids, padded, relations.T)
    right, *pieces, left = bucket(counts[0], ridx, nidx, rel_ids, lhs_rows, padded, rel_rows, slab)
    back, *news = reduce(width, rel_state[None], relations.T, right, pieces)
    rel_new, states, new_shard, new_state = finish(
        width, left, back, shard.T, ent_state, [n.reshape(-1, LANES) for n in news], relations.shape[0]
    )
    return (new_shard.T[None], new_state, rel_new.T, states.reshape(-1))


def solution(mesh):
    in_specs = (
        P("group", "member", None), P("group", "member"), P(), P(),
        P("group", "member"), P("group", "member", None), P("group", "member"),
        P("group", "member", None), P("group", "member"), P("group", "member"), P("group", "member"),
    )
    out_specs = (P("group", "member", None), P("group", "member"), P(), P())
    return jax.shard_map(on_device, mesh=mesh, in_specs=in_specs, out_specs=out_specs, check_vma=False)
```

```python
import functools
import jax
import jax.numpy as jnp
from jax import lax
from jax.experimental import pallas as pl
from jax.experimental.pallas import tpu as pltpu
from jax.sharding import PartitionSpec as P

SPAN = 512
NEG = 500
STEP_SIZE = 0.1
LANES = 128
F32 = jnp.float32
BF16 = jnp.bfloat16
MESH = pl.DeviceIdType.MESH

CHUNKS = 4
TAIL = 16
GROUP = 32
PACK = 104
BLOCKS = 16
RING = 4
Y_FIRST = ("y", "xhi")
X_FIRST = ("xhi", "y")
PART_IN = (X_FIRST, Y_FIRST) * 3 + (Y_FIRST, Y_FIRST)
PART_SUM = (X_FIRST, Y_FIRST, Y_FIRST, Y_FIRST) * 2
PIECE_ROWS = (32, 32, 40)
PIECE_SUM = (("z", "y", "x"), ("x", "z", "y"), ("z", "x", "y"))
PIECE_OUT = (("z", "y", "x"), ("x", "z", "y"), ("y", "z", "x"))
SHARDS = 64
SHIFTS = 8
RINGS_IN = 8
RINGS_SUM = 2
LINK_ROWS = 70.0
CORE_ROWS = 1000.0
LATENCY = 4.0


def split(x):
    hi = x.astype(BF16)
    return hi, (x - hi.astype(F32)).astype(BF16)


def dot2(a, b, dims):
    return lax.dot_general(a, b, (dims, ((), ())), preferred_element_type=F32)


def dot3(a, b, dims):
    (ah, al), (bh, bl) = a, b
    (ka,), (kb,) = dims
    return dot2(jnp.concatenate([ah, ah, al], axis=ka), jnp.concatenate([bh, bl, bh], axis=kb), dims)


def row(i):
    return pl.ds(pl.multiple_of(i * CHUNKS, CHUNKS), CHUNKS)


def span_of(start, size, tile=8):
    return pl.ds(start if isinstance(start, int) else pl.multiple_of(start, tile), size)


def read_rows(ref, rows):
    return jnp.concatenate([ref[pl.ds(c, rows, stride=CHUNKS), :] for c in range(CHUNKS)], axis=1)


def write_rows(ref, value, rows):
    for c in range(CHUNKS):
        ref[pl.ds(c, rows, stride=CHUNKS), :] = value[:, c * LANES : (c + 1) * LANES]


def pack_tail(tail):
    packed = tail[0:8]
    for g in range(1, GROUP // 8):
        packed = packed + pltpu.roll(tail[8 * g : 8 * g + 8], TAIL * g, 1)
    return packed


def unpack_tail(packed):
    kept = lax.broadcasted_iota(jnp.int32, (8, LANES), 1) < TAIL
    parts = [jnp.where(kept, packed if g == 0 else pltpu.roll(packed, LANES - TAIL * g, 1), 0.0) for g in range(GROUP // 8)]
    return jnp.concatenate(parts, axis=0)


def digits_of(flat, order):
    sizes = {"y": 4, "xhi": 2, "x": 4, "z": 4}
    out = {}
    for name in reversed(order):
        out[name] = flat % sizes[name]
        flat = flat // sizes[name]
    return out


def index_of(where, order):
    sizes = {"y": 4, "xhi": 2, "x": 4, "z": 4}
    at = 0
    for name in order:
        at = at * sizes[name] + where[name]
    return at


def part_size(orders):
    return 256 // GROUP * PACK // len(orders)


def part_row(member, part, orders):
    where = digits_of(member // 2, ("y", "xhi"))
    at = (member % 2) * 8 + index_of(where, orders[part])
    return (part * BLOCKS + at) * part_size(orders)


def shard_row(group, piece, orders):
    where = digits_of(group % SHARDS, ("z", "y", "x"))
    return ((group // SHARDS) * SHARDS + index_of(where, orders[piece])) * PIECE_ROWS[piece]


def here():
    g = lax.axis_index("group")
    m = lax.axis_index("member")
    return {"x": (m // 2) % 2 * 2 + g // 4, "xhi": (m // 2) % 2, "y": m // 4, "z": g % 4, "core": m % 2}


def device(at):
    return (at["x"] % 2 * 4 + at["z"], at["y"] * 4 + at["x"] // 2 * 2 + at["core"])


def toward(at, axis, step):
    there = dict(at)
    if axis == "core":
        there["core"] = 1 - at["core"]
    elif axis == "xhi":
        there["x"] = (at["x"] + 2) % 4
    else:
        there[axis] = (at[axis] + step + 4) % 4
    return device(there)


def next_group(step):
    return ((lax.axis_index("group") + step + 8) % 8, lax.axis_index("member"))


def greet(devices):
    barrier = pltpu.get_barrier_semaphore()
    for there in devices:
        pl.semaphore_signal(barrier, inc=1, device_id=there, device_id_type=MESH)
    pl.semaphore_wait(barrier, len(devices))


class Copies:
    def __init__(self, send, recv, local):
        self.send, self.recv, self.local = send, recv, local
        self.started, self.kept, self.homes = 0, [], 0
        self.now, self.busy, self.flows, self.added, self.gates = 0.0, {}, [], 0, {}

    def to(self, there, src, dst, links, rows):
        copy = pltpu.make_async_remote_copy(
            src_ref=src, dst_ref=dst, send_sem=self.send.at[self.started], recv_sem=self.recv.at[self.started],
            device_id=there, device_id_type=MESH,
        )
        copy.start()
        self.started += 1
        self.kept.append(copy)
        begin = max([self.now] + [self.busy.get(link, 0.0) for link in links])
        end = begin + rows / (CORE_ROWS if links == ("core",) else LINK_ROWS)
        for link in links:
            self.busy[link] = end
        self.now += 0.05
        return copy, end + LATENCY

    def home(self, src, dst):
        copy = pltpu.make_async_copy(src, dst, self.local.at[self.homes])
        copy.start()
        self.homes += 1
        return copy

    def enter(self, name, limit):
        held, waiting = self.gates.setdefault(name, ([], []))
        if len(held) == limit:
            yield waiting
        held.append(None)

    def leave(self, name):
        held, waiting = self.gates[name]
        held.pop()
        if waiting:
            number, flow = waiting.pop(0)
            self.step(number, flow)

    def step(self, number, flow):
        ready = next(flow, None)
        if ready is None:
            return
        if any(ready is waiting for _, waiting in self.gates.values()):
            ready.append((number, flow))
        else:
            self.flows.append((max(r for _, r in ready), number, flow))

    def add(self, flow):
        self.added += 1
        self.step(self.added, flow)

    def run(self, beside=iter(()), cost=0.7):
        while self.flows:
            entry = min(self.flows)
            while entry[0] > self.now + cost and next(beside, None) is not None:
                self.now += cost
            self.flows.remove(entry)
            self.now = max(self.now, entry[0]) + 0.1
            self.step(entry[1], entry[2])
        for _ in beside:
            pass

    def finish(self):
        for copy in self.kept:
            copy.wait_send()


def wait_all(copies):
    for copy, _ in copies:
        copy.wait_recv()


def halves(size):
    first = -(-size // 16) * 8
    return first, size - first


def add_into(dst, at, src, start, size):
    tile = size
    while tile > 256:
        tile = tile // 2 if tile % 16 == 0 else tile // 13
    if tile == size:
        dst[span_of(at, size), :] = dst[span_of(at, size), :] + src[span_of(start, size), :]
        return

    def step(i, carry):
        d = span_of(at + i * tile, tile)
        dst[d, :] = dst[d, :] + src[span_of(start + i * tile, tile), :]
        return carry

    lax.fori_loop(0, size // tile, step, 0)


def both(axis):
    return (axis + "+", axis + "-")


def sum_flow(net, at, src, acc, landing, ring, order, direct, done):
    half = acc.shape[0]
    core = at["core"]
    over = net.to(toward(at, "core", 1), src.at[span_of((1 - core) * half, half)], landing, ("core",), half)
    own = net.home(src.at[span_of(core * half, half)], acc)
    yield [over]
    own.wait()
    wait_all([over])
    add_into(acc, 0, landing, 0, half)
    base, size, used = 0, half, 0
    for level, axis in enumerate(order):
        a = at[axis]
        if axis == "xhi":
            size = size // 2
            src_at = acc.at[span_of(base + (1 - a) * size, size)]
            copies = [net.to(toward(at, axis, 1), src_at, ring.at[pl.ds(used, size)], both("x"), size)]
            yield copies
            wait_all(copies)
            add_into(acc, base + a * size, ring, used, size)
            used += size
        else:
            size = size // RING
            up, down, far = (base + (a + k) % RING * size for k in (1, 3, 2))
            above, below, opposite = (toward(at, axis, k) for k in (1, -1, 2))
            plus, minus = ((link,) for link in both(axis))
            ra, rc, rd = used, used + size, used + 2 * size
            if level >= direct:
                copies = [
                    net.to(opposite, acc.at[span_of(far, size)], ring.at[pl.ds(ra, size)], both(axis), size),
                    net.to(above, acc.at[span_of(up, size)], ring.at[pl.ds(rc, size)], plus, size),
                    net.to(below, acc.at[span_of(down, size)], ring.at[pl.ds(rd, size)], minus, size),
                ]
                yield copies
                wait_all(copies)
                add_into(acc, base + a * size, ring, ra, size)
            else:
                h1, h2 = halves(size)
                yield from net.enter(axis, RINGS_SUM)
                first = net.to(above, acc.at[span_of(far, h1)], ring.at[pl.ds(ra, h1)], plus, h1)
                second = net.to(below, acc.at[span_of(far + h1, h2)], ring.at[pl.ds(ra + h1, h2)], minus, h2)
                c2 = net.to(above, acc.at[span_of(up + h1, h2)], ring.at[pl.ds(rc + h1, h2)], plus, h2)
                d1 = net.to(below, acc.at[span_of(down, h1)], ring.at[pl.ds(rd, h1)], minus, h1)
                yield [first, second]
                wait_all([first])
                add_into(acc, up, ring, ra, h1)
                c1 = net.to(above, acc.at[span_of(up, h1)], ring.at[pl.ds(rc, h1)], plus, h1)
                wait_all([second])
                add_into(acc, down + h1, ring, ra + h1, h2)
                d2 = net.to(below, acc.at[span_of(down + h1, h2)], ring.at[pl.ds(rd + h1, h2)], minus, h2)
                copies = [c2, d1, c1, d2]
                yield copies
                wait_all(copies)
                net.leave(axis)
            add_into(acc, base + a * size, ring, rc, size)
            add_into(acc, base + a * size, ring, rd, size)
            used += 3 * size
        base = base + a * size
    yield from done(base)


def spread_flow(net, at, buf, offset, rows, order, direct, arrived):
    radix = {"xhi": 2, "x": 4, "y": 4, "z": 4}
    total = rows
    for name in order:
        total *= radix[name]
    core = at["core"]
    bases = [offset + core * total]
    strides = []
    size = total
    for name in order:
        size = size // radix[name]
        strides.append(size)
        bases.append(bases[-1] + at[name] * size)
    sibling = toward(at, "core", 1)
    shared = []

    def share(start, size):
        there = span_of(start, size)
        copy = net.to(sibling, buf.at[there], buf.at[there], ("core",), size)
        shared.append((copy, start + (1 - 2 * core) * total, size))

    def send(there, start, size, links):
        part = span_of(start, size)
        return net.to(there, buf.at[part], buf.at[part], links, size)

    for level in reversed(range(len(order))):
        name, size, region = order[level], strides[level], bases[level]
        a = at[name]
        last = level == 0
        if name == "xhi":
            other = region + (1 - a) * size
            copies = [send(toward(at, name, 1), region + a * size, size, both("x"))]
            if last:
                share(region + a * size, size)
                arrived(region + a * size, size)
            yield copies
            wait_all(copies)
            if last:
                share(other, size)
                arrived(other, size)
        else:
            h1, h2 = halves(size)
            own, up, down, far = (region + (a + k) % RING * size for k in (0, 1, 3, 2))
            above, below, opposite = (toward(at, name, k) for k in (1, -1, 2))
            plus, minus = ((link,) for link in both(name))
            if level < direct:
                yield from net.enter(name, RINGS_IN)
            e = send(above, own, size, plus)
            f = send(below, own, size, minus)
            if last:
                share(own, size)
            if level >= direct:
                g = send(opposite, own, size, both(name))
                yield [e, f, g]
                wait_all([e, f, g])
            else:
                if last:
                    arrived(own, size)
                yield [e, f]
                wait_all([e])
                g = send(above, down, h1, plus)
                wait_all([f])
                h = send(below, up + h1, h2, minus)
                if last:
                    share(down, size)
                    share(up, size)
                    arrived(down, size)
                    arrived(up, size)
                yield [g, h]
                wait_all([g, h])
                net.leave(name)
                if last:
                    share(far, size)
                    arrived(far, size)
    for copy, start, size in shared:
        yield [copy]
        wait_all([copy])
        arrived(start, size)


def fetch_kernel(rid_ref, ent_ref, rel_hbm, slab_hbm, rows_hbm, own, packed, slab, rel, rel_rows, got, send, recv, local):
    at = here()
    m = lax.axis_index("member")
    greet(
        [toward(at, "y", 1), toward(at, "y", -1), toward(at, "xhi", 1), toward(at, "core", 1), next_group(1), next_group(-1)]
    )
    net = Copies(send, recv, local)
    entry = net.home(rel_hbm, rel)
    for j in range(8):
        rows = slice(j * GROUP, (j + 1) * GROUP)
        for c in range(3):
            own[pl.ds(j * PACK + c * GROUP, GROUP), :] = ent_ref[rows, c * LANES : (c + 1) * LANES]
        own[pl.ds(j * PACK + 96, 8), :] = pack_tail(ent_ref[rows, 3 * LANES : 4 * LANES])

    writes = []
    parts = len(PART_IN)
    size = part_size(PART_IN)
    groups = size // PACK

    def flow(part):
        start = part * BLOCKS * size
        mine = span_of(part_row(m, part, PART_IN), size)
        yield from net.enter("shift", SHIFTS)
        shift = net.to(next_group(-1), own.at[pl.ds(part * size, size)], packed.at[mine], ("z-",), size)
        yield [shift]
        wait_all([shift])
        net.leave("shift")

        def arrived(begin, rows):
            def block(i, carry):
                source = begin + i * size
                flat = (source - start) // size
                where = digits_of(flat % 8, PART_IN[part])
                member = (where["y"] * 2 + where["xhi"]) * 2 + flat // 8
                for k in range(groups):
                    base = source + k * PACK
                    out = (member * 256 + (part * groups + k) * GROUP) * CHUNKS
                    out = pl.multiple_of(out, 128)
                    for c in range(3):
                        slab[pl.ds(out + c, GROUP, stride=CHUNKS), :] = packed[span_of(base + c * GROUP, GROUP), :]
                    slab[pl.ds(out + 3, GROUP, stride=CHUNKS), :] = unpack_tail(packed[span_of(base + 96, 8), :])
                return carry

            lax.fori_loop(0, rows // size, block, 0)
            net.now += 0.04 * rows / PACK

        yield from spread_flow(net, at, packed, start, size, PART_IN[part], 9, arrived)
        view = (BLOCKS, parts, groups * GROUP * CHUNKS, LANES)
        writes.append(net.home(slab.reshape(view).at[:, part], slab_hbm.reshape(view).at[:, part]))

    def gather():
        tile = 256
        width, total = rel.shape
        entry.wait()
        for t in range(total // (4 * tile)):
            def convert(i, carry):
                k = t * 4 + i
                part = span_of(k * tile, tile, tile)
                wide = jnp.concatenate([rel[:, part], jnp.zeros((CHUNKS * LANES - width, tile), F32)], axis=0)
                rel_rows[part] = wide.T.reshape(tile, CHUNKS, LANES)
                return carry

            lax.fori_loop(0, 4, convert, 0)
            yield True
        edges = got.shape[0] // CHUNKS
        segment, unroll = 512, 16
        for t in range(edges // segment):
            def step(b, carry):
                for u in range(unroll):
                    j = t * segment + b * unroll + u
                    got[row(j), :] = rel_rows[rid_ref[0, j]]
                return carry

            lax.fori_loop(0, segment // unroll, step, 0)
            part = pl.ds(t * segment * CHUNKS, segment * CHUNKS)
            writes.append(net.home(got.at[part], rows_hbm.at[part]))
            yield True

    for part in range(parts):
        net.add(flow(part))
    net.run(gather())
    for write in writes:
        write.wait()
    net.finish()


def fetch(rid, ent, relations):
    edges = rid.shape[1]
    width, count = relations.shape
    rows = ent.shape[0] * BLOCKS
    anym = pl.BlockSpec(memory_space=pl.ANY)
    return pl.pallas_call(
        fetch_kernel,
        out_shape=(
            jax.ShapeDtypeStruct((rows * CHUNKS, LANES), F32),
            jax.ShapeDtypeStruct((edges * CHUNKS, LANES), F32),
        ),
        in_specs=[pl.BlockSpec(memory_space=pltpu.SMEM), pl.BlockSpec(memory_space=pltpu.VMEM), anym],
        out_specs=(anym, anym),
        scratch_shapes=[
            pltpu.VMEM((256 // GROUP * PACK, LANES), F32),
            pltpu.VMEM((rows // GROUP * PACK, LANES), F32),
            pltpu.VMEM((rows * CHUNKS, LANES), F32),
            pltpu.VMEM((width, count), F32),
            pltpu.VMEM((count, CHUNKS, LANES), F32),
            pltpu.VMEM((edges * CHUNKS, LANES), F32),
            pltpu.SemaphoreType.DMA((128,)),
            pltpu.SemaphoreType.DMA((128,)),
            pltpu.SemaphoreType.DMA((24,)),
        ],
        compiler_params=pltpu.CompilerParams(vmem_limit_bytes=56 * 2**20, collective_id=1, has_side_effects=True),
        name="fetch",
    )(rid, ent, relations)


def bucket_kernel(
    spans, unroll,
    cnt_ref, ridx_ref, nidx_ref, rid_ref, lhs_ref, ent_ref, rel_ref, slab_hbm,
    right_hbm, rel0_hbm, rel1_hbm, rel2_hbm, left_ref,
    slab, racc, nacc, relacc, rvec, nvec, gr, gn, grel, sem,
):
    s = pl.program_id(0)
    total = racc.shape[0]

    @pl.when(s == 0)
    def _():
        load = pltpu.make_async_copy(slab_hbm, slab.at[pl.ds(0, total)], sem.at[0])
        load.start()
        nvec[pl.ds(NEG * CHUNKS, (SPAN - NEG) * CHUNKS), :] = jnp.zeros(((SPAN - NEG) * CHUNKS, LANES), F32)
        racc[...] = jnp.zeros_like(racc)
        nacc[...] = jnp.zeros_like(nacc)
        relacc[...] = jnp.zeros_like(relacc)
        left_ref[...] = jnp.zeros_like(left_ref)
        load.wait()

    def scatter(j, negative):
        edge = (s - 1) * SPAN + j
        rel = row(rid_ref[0, edge])
        rgt = row(ridx_ref[0, edge])
        own = row(j)
        relacc[rel, :] = relacc[rel, :] + grel[own, :]
        racc[rgt, :] = racc[rgt, :] + gr[own, :]
        if negative:
            neg = row(nidx_ref[0, (s - 1) * NEG + j])
            nacc[neg, :] = nacc[neg, :] + gn[own, :]

    def gather(j, negative):
        own = row(j)
        rvec[own, :] = slab[row(ridx_ref[0, s * SPAN + j]), :]
        if negative:
            nvec[own, :] = slab[row(nidx_ref[0, s * NEG + j]), :]

    def rows_loop(*works):
        def step(b, carry):
            for u in range(unroll):
                for work in works:
                    work(b * unroll + u, True)
            return carry

        last = NEG // unroll * unroll
        lax.fori_loop(0, last // unroll, step, 0)
        for j in range(last, SPAN):
            for work in works:
                work(j, j < NEG)

    @pl.when(s == 0)
    def _():
        rows_loop(gather)

    @pl.when((s > 0) & (s < spans))
    def _():
        rows_loop(gather, scatter)

    @pl.when(s == spans)
    def _():
        rows_loop(scatter)

    @pl.when(s < spans)
    def _():
        hot = (lax.broadcasted_iota(jnp.int32, (ent_ref.shape[0], SPAN), 0) == lhs_ref[...]).astype(F32).astype(BF16)
        eh, el = split(ent_ref[...])
        first = ((0,), (0,))
        last = ((1,), (1,))
        inner = ((1,), (0,))
        left = dot2(jnp.concatenate([hot, hot], axis=0), jnp.concatenate([eh, el], axis=0), first)
        rel = read_rows(rel_ref, SPAN)
        query = left * rel
        live = (s * SPAN + lax.broadcasted_iota(jnp.int32, (SPAN, 1), 0) < cnt_ref[0]).astype(F32)
        q = split(query)
        n = split(read_rows(nvec, SPAN))
        neg = dot3(q, n, last)
        dneg = split(jax.nn.sigmoid(neg) * (live / NEG))
        right = read_rows(rvec, SPAN)
        pos = jnp.sum(query * right, axis=1, keepdims=True)
        dpos = -jax.nn.sigmoid(-pos) * live
        write_rows(gr, dpos * query, SPAN)
        write_rows(gn, dot3(dneg, q, first), SPAN)
        grad_query = dpos * right + dot3(dneg, n, inner)
        write_rows(grel, grad_query * left, SPAN)
        gl = jnp.concatenate(split(grad_query * rel), axis=0)
        left_ref[...] += dot2(jnp.concatenate([hot, hot], axis=1), gl, inner)

    @pl.when(s == spans)
    def _():
        def right_member(m, carry):
            for part in range(len(PART_SUM)):
                for k in range(256 // GROUP // len(PART_SUM)):
                    at = part * (256 // GROUP // len(PART_SUM)) + k
                    src = pl.multiple_of((m * 256 + at * GROUP) * CHUNKS, 128)
                    out = part_row(m, part, PART_SUM) + k * PACK
                    planes = [
                        racc[pl.ds(src + c, GROUP, stride=CHUNKS), :] + nacc[pl.ds(src + c, GROUP, stride=CHUNKS), :]
                        for c in range(CHUNKS)
                    ]
                    for c in range(3):
                        slab[span_of(out + c * GROUP, GROUP), :] = planes[c]
                    slab[span_of(out + 96, 8), :] = pack_tail(planes[3])
            return carry

        lax.fori_loop(0, BLOCKS, right_member, 0)
        out = pltpu.make_async_copy(slab.at[pl.ds(0, right_hbm.shape[0])], right_hbm, sem.at[0])
        out.start()
        begins = (0, 2 * SHARDS * PIECE_ROWS[0], 2 * SHARDS * (PIECE_ROWS[0] + PIECE_ROWS[1]))

        def shards(i, carry):
            for k in range(4):
                group = i * 4 + k
                src = pl.multiple_of(group * GROUP * CHUNKS, 128)
                at = [b + shard_row(group, p, PIECE_SUM) for p, b in enumerate(begins)]
                for c in range(3):
                    nacc[span_of(at[c], GROUP), :] = relacc[pl.ds(src + c, GROUP, stride=CHUNKS), :]
                nacc[span_of(at[2] + GROUP, 8), :] = pack_tail(relacc[pl.ds(src + 3, GROUP, stride=CHUNKS), :])
            return carry

        copies = []
        for half in range(2):
            lax.fori_loop(half * SHARDS // 4, (half + 1) * SHARDS // 4, shards, 0)
            for p, ref in enumerate((rel0_hbm, rel1_hbm, rel2_hbm)):
                size = SHARDS * PIECE_ROWS[p]
                src = nacc.at[pl.ds(begins[p] + half * size, size)]
                copies.append(pltpu.make_async_copy(src, ref.at[pl.ds(half * size, size)], sem.at[1 + len(copies)]))
                copies[-1].start()
        for copy in copies:
            copy.wait()
        out.wait()


def bucket(counts, ridx, nidx, rid, lhs, ent, rel_rows, slab):
    edges = rid.shape[1]
    spans = edges // SPAN
    total = slab.shape[0]
    smem = pl.BlockSpec(memory_space=pltpu.SMEM)
    anym = pl.BlockSpec(memory_space=pl.ANY)
    vm = lambda r: pltpu.VMEM((r, LANES), F32)
    span_rows = SPAN * CHUNKS
    return pl.pallas_call(
        functools.partial(bucket_kernel, spans, 50),
        grid=(spans + 1,),
        out_shape=(
            jax.ShapeDtypeStruct((BLOCKS * 256 // GROUP * PACK, LANES), F32),
            *(jax.ShapeDtypeStruct((2 * SHARDS * r, LANES), F32) for r in PIECE_ROWS),
            jax.ShapeDtypeStruct(ent.shape, F32),
        ),
        in_specs=[
            smem, smem, smem, smem,
            pl.BlockSpec((1, SPAN), lambda s: (0, jnp.minimum(s, spans - 1))),
            pl.BlockSpec(ent.shape, lambda s: (0, 0)),
            pl.BlockSpec((span_rows, LANES), lambda s: (jnp.minimum(s, spans - 1), 0)),
            anym,
        ],
        out_specs=(anym, anym, anym, anym, pl.BlockSpec(ent.shape, lambda s: (0, 0))),
        scratch_shapes=[
            vm(total), vm(total), vm(total), vm(total),
            vm(span_rows), vm(span_rows), vm(span_rows), vm(span_rows), vm(span_rows),
            pltpu.SemaphoreType.DMA((8,)),
        ],
        compiler_params=pltpu.CompilerParams(vmem_limit_bytes=58 * 2**20),
        name="bucket",
    )(counts, ridx, nidx, rid, lhs, ent, rel_rows, slab)


def ring_rows(half, order):
    size, used = half, 0
    for name in order:
        size = size // (2 if name == "xhi" else RING)
        used += size if name == "xhi" else 3 * size
    return used


def reduce_kernel(
    width,
    states_ref, rel_hbm, right_hbm, rel0_hbm, rel1_hbm, rel2_hbm,
    back_hbm, new0_hbm, new1_hbm, new2_hbm,
    *scratch,
):
    scratch = list(scratch)
    take = lambda n: [scratch.pop(0) for _ in range(n)]
    parts = len(PART_SUM)
    racc, rland, rring = take(parts), take(parts), take(parts)
    pacc, pland, pring, news = take(3), take(3), take(3), take(3)
    back, block, shard, send, recv, local = scratch
    at = here()
    mine = (at["core"] * SHARDS + index_of(at, ("z", "y", "x"))) * GROUP
    inside = pl.ds(pl.multiple_of(mine % LANES, GROUP), GROUP)
    lanes = pl.ds(pl.multiple_of(mine // LANES * LANES, LANES), LANES)
    greet(
        [toward(at, axis, step) for axis in ("x", "y", "z") for step in (1, -1, 2)]
        + [toward(at, "core", 1), next_group(1), next_group(-1)]
    )
    net = Copies(send, recv, local)
    entry = net.home(rel_hbm.at[:, lanes], block)
    size = part_size(PART_SUM)
    region = BLOCKS * size
    backs = []
    bases = {}

    def right_flow(part):
        def done(base):
            mine = pl.ds(part * size, size)
            src = racc[part].at[span_of(base, size)]
            copies = [net.to(next_group(1), src, back.at[mine], ("z+",), size)]
            yield copies
            wait_all(copies)
            backs.append(net.home(back.at[mine], back_hbm.at[mine]))

        return sum_flow(
            net, at, right_hbm.at[pl.ds(part * region, region)], racc[part], rland[part], rring[part],
            PART_SUM[part], 9, done,
        )

    def piece_flow(piece):
        def done(base):
            bases[piece] = base
            if len(bases) == 3:
                update()
            yield from ()

        src = (rel0_hbm, rel1_hbm, rel2_hbm)[piece]
        return sum_flow(net, at, src, pacc[piece], pland[piece], pring[piece], PIECE_SUM[piece], 1, done)

    def update():
        planes = [pacc[p][span_of(bases[p], GROUP), :] for p in range(3)]
        planes.append(unpack_tail(pacc[2][span_of(bases[2] + GROUP, 8), :]))
        squares = planes[0] * planes[0]
        for plane in planes[1:]:
            squares = squares + plane * plane
        entry.wait()
        height = CHUNKS * LANES
        wide = jnp.concatenate([block[...], jnp.zeros((height - width, LANES), F32)], axis=0)
        old = jnp.broadcast_to(states_ref[:, lanes], (LANES, LANES)).T
        shard[:, 0:height] = wide.T
        shard[:, height : height + LANES] = old
        state = shard[inside, height : height + 1] + jnp.sum(squares, axis=1, keepdims=True) / width
        root = jnp.sqrt(state)
        fresh = [shard[inside, c * LANES : (c + 1) * LANES] - STEP_SIZE * planes[c] / root for c in range(CHUNKS)]
        tail = pack_tail(fresh[3])
        lane = lax.broadcasted_iota(jnp.int32, (8, LANES), 1)
        for g in range(GROUP // 8):
            tail = jnp.where(lane == LANES // 2 + g, state[8 * g : 8 * g + 8], tail)
        outs = (new0_hbm, new1_hbm, new2_hbm)
        net.now += 0.5
        for p in range(3):
            place = (at["core"] * SHARDS + index_of(at, PIECE_OUT[p])) * PIECE_ROWS[p]
            news[p][span_of(place, GROUP), :] = fresh[p]
            if p == 2:
                news[p][span_of(place + GROUP, 8), :] = tail

            def arrived(start, size, p=p):
                rows = PIECE_ROWS[p]
                half, k = start // (SHARDS * rows), start // (16 * rows) % RING
                src = news[p].at[span_of(start, size)].reshape(4, 4, rows, LANES)
                dst = (outs[p].at[half, k], outs[p].at[half, :, :, k], outs[p].at[half, :, k])[p]
                backs.append(net.home(src, dst))

            net.add(spread_flow(net, at, news[p], 0, PIECE_ROWS[p], PIECE_OUT[p], 1, arrived))

    for k in range(max(3, parts)):
        if k < 3:
            net.add(piece_flow(k))
        if k < parts:
            net.add(right_flow(k))
    net.run()
    for copy in backs:
        copy.wait()
    net.finish()


def reduce(width, states, relations, right, pieces):
    anym = pl.BlockSpec(memory_space=pl.ANY)
    vmem = pl.BlockSpec(memory_space=pltpu.VMEM)
    vm = lambda r: pltpu.VMEM((r, LANES), F32)
    parts = len(PART_SUM)
    half = BLOCKS // 2 * part_size(PART_SUM)
    return pl.pallas_call(
        functools.partial(reduce_kernel, width),
        out_shape=(
            jax.ShapeDtypeStruct((256 // GROUP * PACK, LANES), F32),
            *(jax.ShapeDtypeStruct((2, 4, 4, 4, r, LANES), F32) for r in PIECE_ROWS),
        ),
        in_specs=[vmem, anym, anym, anym, anym, anym],
        out_specs=(anym,) * 4,
        scratch_shapes=[
            *(vm(half) for _ in range(parts)),
            *(vm(half) for _ in range(parts)),
            *(vm(ring_rows(half, PART_SUM[p])) for p in range(parts)),
            *(vm(SHARDS * r) for r in PIECE_ROWS),
            *(vm(SHARDS * r) for r in PIECE_ROWS),
            *(vm(ring_rows(SHARDS * r, PIECE_SUM[p])) for p, r in enumerate(PIECE_ROWS)),
            *(vm(2 * SHARDS * r) for r in PIECE_ROWS),
            vm(256 // GROUP * PACK),
            pltpu.VMEM((width, LANES), F32),
            pltpu.VMEM((LANES, (CHUNKS + 1) * LANES), F32),
            pltpu.SemaphoreType.DMA((192,)),
            pltpu.SemaphoreType.DMA((192,)),
            pltpu.SemaphoreType.DMA((64,)),
        ],
        compiler_params=pltpu.CompilerParams(vmem_limit_bytes=56 * 2**20, collective_id=2, has_side_effects=True),
        name="reduce",
    )(states, relations, right, *pieces)


def finish_kernel(
    width, left_ref, back_ref, ent_ref, state_ref, new0, new1, new2, rel_ref, rel_state_ref, ent_out, state_out
):
    s = pl.program_id(0)
    count = rel_ref.shape[1]
    lane = lax.broadcasted_iota(jnp.int32, (8, LANES), 1)
    for k in range(count // LANES):
        out = pl.ds(k * LANES, LANES)
        groups = range(k * 4, k * 4 + 4)
        for c, ref in enumerate((new0, new1, new2)):
            r = PIECE_ROWS[c]
            plane = jnp.concatenate([ref[g * r : g * r + GROUP, :] for g in groups], axis=0)
            rel_ref[c * LANES : (c + 1) * LANES, out] = plane.T
        r = PIECE_ROWS[2]
        tails = []
        for group in groups:
            packed = new2[group * r + GROUP : (group + 1) * r, :]
            for g in range(GROUP // 8):
                state = pltpu.roll(packed, LANES // 2 + TAIL - g, 1)
                values = packed if g == 0 else pltpu.roll(packed, LANES - TAIL * g, 1)
                tails.append(jnp.where(lane < TAIL, values, state))
        tail = jnp.concatenate(tails, axis=0).T
        rel_ref[3 * LANES : width, out] = tail[: width - 3 * LANES]
        rel_state_ref[:, out] = tail[TAIL : TAIL + 1]

    @pl.when(s == 0)
    def _():
        for i in range(2):
            part = slice(i * LANES, (i + 1) * LANES)
            wide = []
            for j in range(4 * i, 4 * i + 4):
                planes = [back_ref[pl.ds(j * PACK + c * GROUP, GROUP), :] for c in range(3)]
                planes.append(unpack_tail(back_ref[pl.ds(j * PACK + 96, 8), :]))
                wide.append(jnp.concatenate(planes, axis=1))
            grad = (left_ref[part, :] + jnp.concatenate(wide, axis=0)).T[:width]
            state = state_ref[:, part] + jnp.sum(grad * grad, axis=0, keepdims=True) / width
            state_out[:, part] = state
            ent_out[:, part] = ent_ref[:, part] - STEP_SIZE * grad / jnp.sqrt(state)


def finish(width, left, back, ent, ent_state, news, count):
    steps = 4
    full = lambda a: pl.BlockSpec(a.shape, lambda s: (0, 0))
    rows = ent.shape[1]
    return pl.pallas_call(
        functools.partial(finish_kernel, width),
        grid=(steps,),
        out_shape=(
            jax.ShapeDtypeStruct((width, count), F32),
            jax.ShapeDtypeStruct((1, count), F32),
            jax.ShapeDtypeStruct((width, rows), F32),
            jax.ShapeDtypeStruct((1, rows), F32),
        ),
        in_specs=[full(a) for a in (left, back, ent, ent_state)]
        + [pl.BlockSpec((2 * SHARDS // steps * r, LANES), lambda s: (s, 0)) for r in PIECE_ROWS],
        out_specs=(
            pl.BlockSpec((width, count // steps), lambda s: (0, s)),
            pl.BlockSpec((1, count // steps), lambda s: (0, s)),
            pl.BlockSpec((width, rows), lambda s: (0, 0)),
            pl.BlockSpec((1, rows), lambda s: (0, 0)),
        ),
        compiler_params=pltpu.CompilerParams(vmem_limit_bytes=60 * 2**20),
        name="finish",
    )(left, back, ent, ent_state, *news)


def on_device(
    entities, ent_state, relations, rel_state, lhs_rows, rhs_owner, rhs_off, neg_owner, neg_off, rel_ids, counts
):
    shard = entities[0]
    rows, width = shard.shape
    wide = CHUNKS * LANES
    padded = jnp.pad(shard, ((0, 0), (0, wide - width)))
    ridx = rhs_owner[:, :, 0] * rows + rhs_off
    nidx = neg_owner[:, :, 0] * rows + neg_off
    slab, rel_rows = fetch(rel_ids, padded, relations.T)
    right, *pieces, left = bucket(counts[0], ridx, nidx, rel_ids, lhs_rows, padded, rel_rows, slab)
    back, *news = reduce(width, rel_state[None], relations.T, right, pieces)
    rel_new, states, new_shard, new_state = finish(
        width, left, back, shard.T, ent_state, [n.reshape(-1, LANES) for n in news], relations.shape[0]
    )
    return (new_shard.T[None], new_state, rel_new.T, states.reshape(-1))


def solution(mesh):
    in_specs = (
        P("group", "member", None), P("group", "member"), P(), P(),
        P("group", "member"), P("group", "member", None), P("group", "member"),
        P("group", "member", None), P("group", "member"), P("group", "member"), P("group", "member"),
    )
    out_specs = (P("group", "member", None), P("group", "member"), P(), P())
    return jax.shard_map(on_device, mesh=mesh, in_specs=in_specs, out_specs=out_specs, check_vma=False)
```
